32 devices in a mesh: dp: 8 (over z, x), mp: 4 (over y, core).
Axes of the slice: x: 2, y: 2, z: 4, core: 2. Of those that a mesh axis runs over, the one named last changes fastest.
Arguments:
- row_ids: int32 [8192, 16], P('dp', 'mp'), may hold values from 0 to 131071, as said below
- counts: int32 [8], replicated, may hold values from 256 to 1024, as said below
- labels: int32 [8192, 5], P(('dp', 'mp')), may hold values from 0 to 1
- label_mask: int32 [8192, 5], P(('dp', 'mp')), may hold values 0 or 1
- embeddings: float32 [16, 131072, 64], P(None, ('dp', 'mp')), may hold values from -6 to 6
- embed_first: float32 [16, 131072, 64], P(None, ('dp', 'mp')), may hold values from -8.940697e-08 to 8.940697e-08
- embed_second: float32 [16, 131072, 64], P(None, ('dp', 'mp')), may hold values from 3.7252903e-17 to 1.4901161e-16
- expert_in: float32 [1024, 8, 512], P('dp', None, 'mp'), may hold values from -0.1875 to 0.1875
- in_first: float32 [1024, 8, 512], P('dp', None, 'mp'), may hold values from -9.536743e-06 to 9.536743e-06
- in_second: float32 [1024, 8, 512], P('dp', None, 'mp'), may hold values from 4.7683716e-13 to 1.9073486e-12
- expert_out: float32 [512, 8, 512], P('dp', None, 'mp'), may hold values from -0.25 to 0.25
- out_first: float32 [512, 8, 512], P('dp', None, 'mp'), may hold values from -9.536743e-06 to 9.536743e-06
- out_second: float32 [512, 8, 512], P('dp', None, 'mp'), may hold values from 4.7683716e-13 to 1.9073486e-12
- gating: float32 [1024, 40], replicated, may hold values from -0.09375 to 0.09375
- gating_first: float32 [1024, 40], replicated, may hold values from -3.0517578e-05 to 3.0517578e-05
- gating_second: float32 [1024, 40], replicated, may hold values from 4.2915346e-12 to 1.7166138e-11
- towers: float32 [512, 1280], replicated, may hold values from -1 to 1
- towers_first: float32 [512, 1280], replicated, may hold values from -3.0517578e-05 to 3.0517578e-05
- towers_second: float32 [512, 1280], replicated, may hold values from 4.2915346e-12 to 1.7166138e-11
- heads: float32 [5, 256], replicated, may hold values from -0.75 to 0.75
- heads_first: float32 [5, 256], replicated, may hold values from -3.0517578e-05 to 3.0517578e-05
- heads_second: float32 [5, 256], replicated, may hold values from 4.2915346e-12 to 1.7166138e-11
- biases: float32 [9517], replicated, may hold values from -1 to 1
- biases_first: float32 [9517], replicated, may hold values from -0.00010681152 to 0.00010681152
- biases_second: float32 [9517], replicated, may hold values from 4.7683715e-11 to 1.9073486e-10
Outputs:
- embed_next: float32 [16, 131072, 64], P(None, ('dp', 'mp'))
- embed_moment: float32 [16, 131072, 64], P(None, ('dp', 'mp'))
- embed_square: float32 [16, 131072, 64], P(None, ('dp', 'mp'))
- in_next: float32 [1024, 8, 512], P('dp', None, 'mp')
- in_moment: float32 [1024, 8, 512], P('dp', None, 'mp')
- in_square: float32 [1024, 8, 512], P('dp', None, 'mp')
- in_copy: bfloat16 [1024, 8, 512], P('dp', None, 'mp')
- out_next: float32 [512, 8, 512], P('dp', None, 'mp')
- out_moment: float32 [512, 8, 512], P('dp', None, 'mp')
- out_square: float32 [512, 8, 512], P('dp', None, 'mp')
- out_copy: bfloat16 [512, 8, 512], P('dp', None, 'mp')
- gating_next: float32 [1024, 40], replicated
- gating_moment: float32 [1024, 40], replicated
- gating_square: float32 [1024, 40], replicated
- towers_next: float32 [512, 1280], replicated
- towers_moment: float32 [512, 1280], replicated
- towers_square: float32 [512, 1280], replicated
- heads_next: float32 [5, 256], replicated
- heads_moment: float32 [5, 256], replicated
- heads_square: float32 [5, 256], replicated
- biases_next: float32 [9517], replicated
- biases_moment: float32 [9517], replicated
- biases_square: float32 [9517], replicated
- grad_norm: float32 [1], replicated
- loss: float32 [2], replicated
- stats: float32 [14], replicated
The draws below stay inside these ranges and needn't reach their ends.
Inputs may be any that keep to these rules, and one draw needn't show every extreme that they name: `row_ids`: row r of a table lies on the device of index r // 4096 over dp+mp. Of the 4096 ids in the block of one index of dp (its 1024 samples) and one index of mp (its 4 tables), at most 256 fall on the rows of any one device, and some device receives exactly 256 from every such block. `counts`: the last index of dp uses all 1024 slots.
All inputs are finite; a program needn't handle non-finite values. No bound on the sum of `label_mask` on one device may be relied on, other than what follows from the above.
Results may differ from the reference program's by a relative error of at most 0.0076.
Values may be sent and summed in bfloat16 or wider, within the bound.
A program may use at most 256 MiB of HBM per device.

```python
import math
import jax
import jax.numpy as jnp
from jax import lax

TABLES = 16
D_EMB = 64
ROWS_DEV = 4096
EXPERTS = 8
HID = 512
OUT = 512
TASKS = 5
TH = 256
STEP = 3
S_DEV = 1024
IN = 1024
ROWS = 131072
SAMPLES = 8192
BIAS_LEN = 9517
N_DP = 8
N_MP = 4
DEVICES = 32


def draw_row_ids(key, part):
    tables_here = TABLES // N_MP
    requests = S_DEV * tables_here
    middle = requests // DEVICES
    blocks = N_DP * N_MP
    keys = jax.random.split(key, 5)
    spread = jax.random.randint(keys[0], (blocks, DEVICES // 2), 0, middle + 1)
    chosen = jax.random.randint(keys[1], (blocks,), 0, DEVICES // 2)
    spread = jnp.where(jnp.arange(DEVICES // 2)[None, :] == chosen[:, None], middle, spread)
    shares = jnp.stack([middle + spread, middle - spread], axis=2).reshape(blocks, DEVICES)
    ends = jnp.cumsum(shares, axis=1)
    ranks = jax.vmap(lambda k: jax.random.permutation(k, requests))(jax.random.split(keys[2], blocks))
    bucket = jax.vmap(lambda e, r: jnp.searchsorted(e, r, side='right'))(ends, ranks)
    rotate = jax.random.randint(keys[3], (blocks, 1), 0, DEVICES)
    owner = (bucket + rotate) % DEVICES
    local_row = jax.random.randint(keys[4], (blocks, requests), 0, ROWS_DEV)
    wanted = owner * ROWS_DEV + local_row
    wanted = wanted.reshape(N_DP, N_MP, S_DEV, tables_here).transpose(0, 2, 1, 3)
    return wanted.reshape(N_DP * S_DEV, TABLES).astype(jnp.int32)


def draw_counts(key, part):
    place = jnp.arange(N_DP)
    base = S_DEV * (N_DP - 1 + 2 * place) // (3 * (N_DP - 1))
    jitter = jax.random.randint(key, (N_DP,), -(S_DEV // 16), S_DEV // 16 + 1)
    used = jnp.clip(base + jitter, S_DEV // 4, S_DEV)
    used = jnp.where(place == N_DP - 1, S_DEV, used)
    return used.astype(jnp.int32)


def touch_ends(drawn, stream_key, smallest, high):
    longest = drawn.shape.index(max(drawn.shape))
    spots = []
    for shift in (0, 1):
        where = [jax.random.randint(jax.random.fold_in(stream_key, axis), (), 0, length) for axis, length in enumerate(drawn.shape)]
        where[longest] = (where[longest] + shift) % drawn.shape[longest]
        spots.append(tuple(where))
    return drawn.at[spots[0]].set(smallest).at[spots[1]].set(high)


def block_scale(own_key, shape, cuts, least, top_value):
    gain, own = 1.0, jax.random.fold_in(own_key, 6)
    for dim, shards_of in cuts:
        draws = jnp.exp(jax.random.uniform(jax.random.fold_in(own, dim), (shards_of,), jnp.float32, least / len(cuts), top_value / len(cuts)))
        gain = gain * jnp.repeat(draws, shape[dim] // shards_of).reshape([-1 if axis == dim else 1 for axis in range(len(shape))])
    return gain


def centred(key, dims, scale, reach, shards=(), kind=jnp.bfloat16):
    array = scale * jax.random.normal(key, dims, jnp.float32)
    if shards:
        array = array * block_scale(key, dims, shards, -0.22, 0.18)
    return jnp.clip(array, -reach, reach).astype(kind)


def setup_inputs(seed: int = 0) -> dict:
    streams_of = jax.random.split(jax.random.key(seed), 26)
    return {
        "row_ids": draw_row_ids(jax.random.fold_in(streams_of[25], 71), 0),
        "counts": draw_counts(jax.random.fold_in(streams_of[25], 71), 0),
        "labels": touch_ends(jax.random.randint(streams_of[2], (SAMPLES, TASKS), 0, 2), jax.random.fold_in(streams_of[2], 1), 0, 1).astype(jnp.int32),
        "label_mask": touch_ends((jax.random.randint(streams_of[3], (SAMPLES, TASKS), 0, 4) < 3).astype(jnp.int32), jax.random.fold_in(streams_of[3], 1), 0, 1),
        "embeddings": centred(streams_of[4], (TABLES, ROWS, D_EMB), 1.0, 6.0, ((1, 32),), jnp.float32),
        "embed_first": centred(streams_of[5], (TABLES, ROWS, D_EMB), (0.0016 / (2 * EXPERTS * IN * HID * SAMPLES) ** 0.5), 8.940696716308594e-08, ((1, 32),), jnp.float32),
        "embed_second": jnp.clip(jnp.exp(math.log(1.4901161103286282e-16) - 1.3862944 * jax.random.uniform(streams_of[6], (TABLES, ROWS, D_EMB), jnp.float32) ** block_scale(streams_of[6], (TABLES, ROWS, D_EMB), ((1, 32),), -0.2, 0.2)), 3.7252902758215704e-17, 1.4901161103286282e-16),
        "expert_in": centred(streams_of[7], (IN, EXPERTS, HID), IN ** -0.5, 0.1875, ((0, 8), (2, 4)), jnp.float32),
        "in_first": centred(streams_of[8], (IN, EXPERTS, HID), (0.002 / (2 * EXPERTS * IN * HID) ** 0.5), 9.5367431640625e-06, ((0, 8), (2, 4)), jnp.float32),
        "in_second": jnp.clip(jnp.exp(math.log(1.9073486279969076e-12) - 1.3862944 * jax.random.uniform(streams_of[9], (IN, EXPERTS, HID), jnp.float32) ** block_scale(streams_of[9], (IN, EXPERTS, HID), ((0, 8), (2, 4)), -0.2, 0.2)), 4.768371569992269e-13, 1.9073486279969076e-12),
        "expert_out": centred(streams_of[10], (OUT, EXPERTS, HID), HID ** -0.5, 0.25, ((0, 8), (2, 4)), jnp.float32),
        "out_first": centred(streams_of[11], (OUT, EXPERTS, HID), (0.002 / (2 * EXPERTS * IN * HID) ** 0.5), 9.5367431640625e-06, ((0, 8), (2, 4)), jnp.float32),
        "out_second": jnp.clip(jnp.exp(math.log(1.9073486279969076e-12) - 1.3862944 * jax.random.uniform(streams_of[12], (OUT, EXPERTS, HID), jnp.float32) ** block_scale(streams_of[12], (OUT, EXPERTS, HID), ((0, 8), (2, 4)), -0.2, 0.2)), 4.768371569992269e-13, 1.9073486279969076e-12),
        "gating": centred(streams_of[13], (IN, TASKS * EXPERTS), (4 * IN) ** -0.5, 0.09375, (), jnp.float32),
        "gating_first": centred(streams_of[14], (IN, TASKS * EXPERTS), (0.006 / (2 * EXPERTS * IN * HID) ** 0.5), 3.0517578125e-05, (), jnp.float32),
        "gating_second": jnp.clip(jnp.exp(jax.random.uniform(streams_of[15], (IN, TASKS * EXPERTS), jnp.float32, math.log(4.291534575623368e-12), math.log(1.7166138302493472e-11))), 4.291534575623368e-12, 1.7166138302493472e-11),
        "towers": centred(streams_of[16], (OUT, TASKS * TH), (OUT // 16) ** -0.5, 1.0, (), jnp.float32),
        "towers_first": centred(streams_of[17], (OUT, TASKS * TH), (0.006 / (2 * EXPERTS * IN * HID) ** 0.5), 3.0517578125e-05, (), jnp.float32),
        "towers_second": jnp.clip(jnp.exp(jax.random.uniform(streams_of[18], (OUT, TASKS * TH), jnp.float32, math.log(4.291534575623368e-12), math.log(1.7166138302493472e-11))), 4.291534575623368e-12, 1.7166138302493472e-11),
        "heads": centred(streams_of[19], (TASKS, TH), (TH // 4) ** -0.5, 0.75, (), jnp.float32),
        "heads_first": centred(streams_of[20], (TASKS, TH), (0.006 / (2 * EXPERTS * IN * HID) ** 0.5), 3.0517578125e-05, (), jnp.float32),
        "heads_second": jnp.clip(jnp.exp(jax.random.uniform(streams_of[21], (TASKS, TH), jnp.float32, math.log(4.291534575623368e-12), math.log(1.7166138302493472e-11))), 4.291534575623368e-12, 1.7166138302493472e-11),
        "biases": centred(streams_of[22], (BIAS_LEN,), 0.2, 1.0, (), jnp.float32),
        "biases_first": centred(streams_of[23], (BIAS_LEN,), (0.02 / (2 * EXPERTS * IN * HID) ** 0.5), 0.00010681152, (), jnp.float32),
        "biases_second": jnp.clip(jnp.exp(jax.random.uniform(streams_of[24], (BIAS_LEN,), jnp.float32, math.log(4.768371461572052e-11), math.log(1.9073485846288207e-10))), 4.768371461572052e-11, 1.9073485846288207e-10),
    }


HIGH = lax.Precision.HIGHEST
beta_one = 0.5
beta_two = 0.5
adam_eps = 1e-08
decay = 0.01
clip_max = 0.002
rate_table = 0.5
rate_dense = 0.02
stat_eps = 1e-06

@jax.custom_vjp
def low(v):
    return lax.optimization_barrier(v.astype(jnp.bfloat16)).astype(jnp.float32)

@jax.custom_vjp
def low_back(v):
    return v

def low_keep(v):
    return (low(v), None)

def low_pass(kept, grad):
    return (grad,)

def back_keep(v):
    return (v, None)

def back_low(kept, grad):
    return (low(grad),)
low.defvjp(low_keep, low_pass)
low_back.defvjp(back_keep, back_low)

def unpack(vector):
    first = EXPERTS * HID
    second = first + EXPERTS * OUT
    third = second + TASKS * EXPERTS
    fourth = third + TASKS * TH
    return (vector[:first].reshape(EXPERTS, HID), vector[first:second].reshape(EXPERTS, OUT), vector[second:third].reshape(TASKS, EXPERTS), vector[third:fourth].reshape(TASKS, TH), vector[fourth:])

def adamw(weight, first, second, gradient, rate):
    first_next = beta_one * first + (1.0 - beta_one) * gradient
    second_next = beta_two * second + (1.0 - beta_two) * gradient * gradient
    corrected = first_next / (1.0 - beta_one ** STEP)
    scaled = jnp.sqrt(second_next / (1.0 - beta_two ** STEP))
    return (weight - rate * (corrected / (scaled + adam_eps) + decay * weight), first_next, second_next)

def block_loss(params, rows, target, present, valid):
    w_in, w_out, gating, towers, heads, biases = params
    samples = rows.shape[0]
    inputs = low(rows).reshape(samples, TABLES * D_EMB)
    inner_bias, outer_bias, gate_bias, tower_bias, head_bias = unpack(biases)
    preact = low_back(jnp.einsum('si,ieh->seh', inputs, low(w_in), precision=HIGH) + inner_bias)
    hidden = low(jax.nn.gelu(preact))
    expert_y = low_back(jnp.einsum('seh,oeh->seo', hidden, low(w_out), precision=HIGH) + outer_bias)
    gate_logit = low_back(jnp.dot(inputs, low(gating), precision=HIGH) + gate_bias.reshape(-1))
    gates = jax.nn.softmax(gate_logit.reshape(samples, TASKS, EXPERTS), axis=-1)
    mixed = jnp.einsum('ske,seo->sko', gates, expert_y, precision=HIGH)
    tower_pre = low_back(jnp.einsum('sko,okj->skj', low(mixed), low(towers).reshape(OUT, TASKS, TH), precision=HIGH) + tower_bias)
    tower_act = jax.nn.gelu(tower_pre)
    logits = lax.optimization_barrier(jnp.sum(tower_act * heads, axis=-1)) + head_bias
    weights = valid[:, None] * present
    loss_sum = jnp.sum(weights * (jax.nn.softplus(logits) - target * logits))
    valid_rows = valid[:, None, None]
    sums = jnp.concatenate([jnp.sum(valid[:, None] * inputs * inputs)[None], lax.optimization_barrier(jnp.sum(valid_rows * expert_y * expert_y, axis=(0, 2))), lax.optimization_barrier(jnp.sum(valid_rows * mixed * mixed, axis=(0, 2))), jnp.sum(weights)[None]])
    return (loss_sum, sums)

def reference(row_ids, counts, labels, label_mask, embeddings, embed_first, embed_second, expert_in, in_first, in_second, expert_out, out_first, out_second, gating, gating_first, gating_second, towers, towers_first, towers_second, heads, heads_first, heads_second, biases, biases_first, biases_second):
    table_index = jnp.arange(TABLES, dtype=jnp.int32)[None, :]
    rows_all, gather_back = jax.vjp(lambda a: a[table_index, row_ids], embeddings)
    params = (expert_in, expert_out, gating, towers, heads, biases)
    valid_all = (jnp.arange(S_DEV, dtype=jnp.int32)[None, :] < counts[:, None]).astype(jnp.float32)
    blocks = (rows_all.reshape(N_DP, S_DEV, TABLES, D_EMB), labels.astype(jnp.float32).reshape(N_DP, S_DEV, TASKS), label_mask.astype(jnp.float32).reshape(N_DP, S_DEV, TASKS), valid_all)

    def one_block(carry, inputs):
        grads_acc, sums_acc = carry
        rows_b, target_b, present_b, valid_b = inputs
        loss_b, back, sums_b = jax.vjp(lambda p, r: block_loss(p, r, target_b, present_b, valid_b), params, rows_b, has_aux=True)
        grad_params, grad_rows = back(jnp.ones_like(loss_b))
        grads_acc = jax.tree.map(jnp.add, grads_acc, grad_params)
        return ((grads_acc, sums_acc + jnp.concatenate([loss_b[None], sums_b])), grad_rows)
    init = (jax.tree.map(jnp.zeros_like, params), jnp.zeros((3 + EXPERTS + TASKS,), jnp.float32))
    (grads, sums), grad_rows = lax.scan(one_block, init, blocks)
    grad_table, = gather_back(grad_rows.reshape(N_DP * S_DEV, TABLES, D_EMB))
    weight_total = sums[-1]
    scaled = [g / weight_total for g in (grad_table,) + tuple(grads)]
    grad_norm = jnp.sqrt(sum((jnp.sum(g * g) for g in scaled)))
    clip = jnp.minimum(1.0, clip_max / grad_norm)
    clipped = [g * clip for g in scaled]
    embed_out = adamw(embeddings, embed_first, embed_second, clipped[0], rate_table)
    in_out = adamw(expert_in, in_first, in_second, clipped[1], rate_dense)
    out_out = adamw(expert_out, out_first, out_second, clipped[2], rate_dense)
    gating_out = adamw(gating, gating_first, gating_second, clipped[3], rate_dense)
    towers_out = adamw(towers, towers_first, towers_second, clipped[4], rate_dense)
    heads_out = adamw(heads, heads_first, heads_second, clipped[5], rate_dense)
    biases_out = adamw(biases, biases_first, biases_second, clipped[6], rate_dense)
    n_valid = jnp.sum(counts).astype(jnp.float32)
    widths = jnp.concatenate([jnp.full((1,), TABLES * D_EMB, jnp.float32), jnp.full((EXPERTS + TASKS,), OUT, jnp.float32)])
    stats = jnp.sqrt(sums[1:2 + EXPERTS + TASKS] / (n_valid * widths) + stat_eps)
    loss = jnp.stack([sums[0], weight_total])
    return (embed_out[0], embed_out[1], embed_out[2], in_out[0], in_out[1], in_out[2], in_out[0].astype(jnp.bfloat16), out_out[0], out_out[1], out_out[2], out_out[0].astype(jnp.bfloat16), gating_out[0], gating_out[1], gating_out[2], towers_out[0], towers_out[1], towers_out[2], heads_out[0], heads_out[1], heads_out[2], biases_out[0], biases_out[1], biases_out[2], grad_norm.reshape(1), loss, stats)
```

```python
import functools
import math

import jax
import jax.numpy as jnp
from jax import lax
from jax.experimental import pallas as pl
from jax.experimental.pallas import tpu as pltpu
from jax.sharding import PartitionSpec as P

EXPERTS = 8
TASKS = 5
STEP = 3

HIGH = lax.Precision.HIGHEST
beta_one = 0.5
beta_two = 0.5
adam_eps = 1e-08
decay = 0.01
clip_max = 0.002
rate_table = 0.5
rate_dense = 0.02
stat_eps = 1e-06

LOW = jnp.bfloat16
F32 = jnp.float32
I32 = jnp.int32
MIB = 1024 * 1024
AXES = ("dp", "mp")


def params(mib):
    return pltpu.CompilerParams(vmem_limit_bytes=mib * MIB)


VMEM = pl.BlockSpec(memory_space=pltpu.VMEM)
SMEM = pl.BlockSpec(memory_space=pltpu.SMEM)


def adamw(weight, first, second, gradient, rate):
    first_next = beta_one * first + (1.0 - beta_one) * gradient
    second_next = beta_two * second + (1.0 - beta_two) * gradient * gradient
    corrected = first_next / (1.0 - beta_one**STEP)
    scaled = jnp.sqrt(second_next / (1.0 - beta_two**STEP))
    return (
        weight - rate * (corrected / (scaled + adam_eps) + decay * weight),
        first_next,
        second_next,
    )


def gelu_pair(value):
    result, back = jax.vjp(jax.nn.gelu, value)
    return (result, back(jnp.ones_like(value))[0])


def route_kernel(row_bits, ids_ref, out_ref, place_ref, slot_ref):
    devices, capacity = out_ref.shape
    tables, samples = ids_ref.shape
    rows_dev = 1 << row_bits
    halves = devices * capacity // 2
    width = 256
    upper = (
        lax.broadcasted_iota(I32, (width, width), 0) <= lax.broadcasted_iota(I32, (width, width), 1)
    ).astype(LOW)
    owners = lax.broadcasted_iota(I32, (devices, width), 0)
    slots = lax.broadcasted_iota(I32, (capacity, width), 0)
    carry = jnp.zeros((devices, 1), F32)
    total = jnp.zeros((2 * devices, capacity), F32)
    for table in range(tables):
        parity = table % 2
        for part in range(samples // width):
            cols = pl.ds(part * width, width)
            ids = ids_ref[pl.ds(table, 1), cols]
            owner = ids >> row_bits
            code = (parity * (tables // 2) + table // 2) * rows_dev + (ids & (rows_dev - 1)) + 1
            onehot = (owner == owners).astype(F32)
            counted = jnp.dot(onehot.astype(LOW), upper, preferred_element_type=F32) + carry
            rank = jnp.sum(onehot * counted, axis=0, keepdims=True).astype(I32) - 1
            carry = counted[:, width - 1 :]
            at_slot = (rank == slots).astype(LOW)
            high = (code >> 7).astype(F32)
            low = (code & 127).astype(F32)
            pieces = jnp.concatenate([onehot * high, onehot * low], axis=0).astype(LOW)
            total += lax.dot_general(
                pieces, at_slot, (((1,), (1,)), ((), ())), preferred_element_type=F32
            )
            row = owner * (capacity // 2) + (rank >> 1)
            half = rank & 1
            place_ref[pl.ds(table, 1), cols] = (half ^ parity) * halves + row
            slot_ref[pl.ds(table, 1), cols] = half * halves + row
    codes = (total[:devices] * 128.0 + total[devices:]).astype(I32)
    first = lax.broadcasted_iota(I32, (devices, capacity), 1) == 0
    counted = jnp.where(first, carry * 65536.0, 0.0).astype(I32)
    out_ref[...] = codes + counted


def turn_kernel(table_ref, out_ref):
    pair, width, rows = table_ref.shape
    out_ref[0] = table_ref[...].reshape(pair * width, rows).T


def left_lanes(shape):
    return lax.broadcasted_iota(I32, shape, len(shape) - 1) < 64


def find_kernel(groups, code_bits, codes_ref, table_ref, out_ref, rows_ref):
    group = pl.program_id(0)
    blocks, _, height, lanes = out_ref.shape
    mask = (1 << code_bits) - 1
    left = left_lanes((1, lanes))

    def fetch(code, side):
        at = jnp.maximum((code & 65535) - 1, 0)
        row = table_ref[pl.ds(at & mask, 1), :]
        return pltpu.roll(row, ((at >> code_bits) ^ side) * 64, 1)

    def block_step(block, _):
        source = block * groups + group
        count = codes_ref[source, 0] >> 16

        def step(outer, _):
            for inner in range(8):
                at = outer * 8 + inner
                even = fetch(codes_ref[source, 2 * at], 0)
                odd = fetch(codes_ref[source, 2 * at + 1], 1)
                rows_ref[pl.ds(at, 1), :] = jnp.where(left, even, odd)
            return 0

        lax.fori_loop(0, (count + 15) // 16, step, 0)
        out_ref[block, 0] = rows_ref[...].astype(LOW)
        return 0

    lax.fori_loop(0, blocks, block_step, 0)


def place_kernel(place_ref, rows_ref, out_ref, both_ref, flat_ref):
    count, lanes = rows_ref.shape
    tables, samples = place_ref.shape
    rows = rows_ref[...].astype(F32)
    both_ref[pl.ds(0, count), :] = rows
    both_ref[pl.ds(count, count), :] = pltpu.roll(rows, 64, 1)
    left = left_lanes((1, lanes))

    def step(outer, _):
        for inner in range(8):
            sample = outer * 8 + inner
            for pair in range(tables // 2):
                even = both_ref[pl.ds(place_ref[2 * pair, sample], 1), :]
                odd = both_ref[pl.ds(place_ref[2 * pair + 1, sample], 1), :]
                flat_ref[pair, pl.ds(sample, 1), :] = jnp.where(left, even, odd)
        return 0

    lax.fori_loop(0, samples // 8, step, 0)
    for pair in range(tables // 2):
        out_ref[:, pair * lanes : (pair + 1) * lanes] = flat_ref[pair].astype(LOW)


def send_kernel(slot_ref, grad_ref, out_ref, both_ref, rows_ref):
    count, lanes = out_ref.shape
    tables, samples = slot_ref.shape
    for pair in range(tables // 2):
        rows = grad_ref[:, pair * lanes : (pair + 1) * lanes]
        both_ref[pair, pl.ds(0, samples), :] = rows
        both_ref[pair, pl.ds(samples, samples), :] = pltpu.roll(rows, 64, 1)
    bits = count.bit_length() - 1

    def step(outer, _):
        for inner in range(8):
            sample = outer * 8 + inner
            for table in range(tables):
                slot = slot_ref[table, sample]
                turned = (slot >> bits) ^ (table % 2)
                rows_ref[pl.ds(slot, 1), :] = both_ref[
                    table // 2, pl.ds(turned * samples + sample, 1), :
                ]
        return 0

    lax.fori_loop(0, samples // 8, step, 0)
    left = left_lanes((count, lanes))
    out_ref[...] = jnp.where(
        left, rows_ref[pl.ds(0, count), :], rows_ref[pl.ds(count, count), :]
    ).astype(LOW)


def add_kernel(groups, code_bits, codes_ref, rows_ref, out_ref, square_ref, parts_ref, sems, *sums):
    count, lanes = rows_ref.shape
    sources = codes_ref.shape[0]
    height = count // sources
    mask = (1 << code_bits) - 1
    table_rows = sums[0].shape[0]
    left = left_lanes((count, lanes))
    rows = rows_ref[...].astype(F32)
    turned = pltpu.roll(rows, 64, 1)
    parts_ref[pl.ds(0, count), :] = jnp.where(left, rows, 0.0)
    parts_ref[pl.ds(count, count), :] = jnp.where(left, 0.0, turned)
    parts_ref[pl.ds(2 * count, count), :] = jnp.where(left, turned, 0.0)
    parts_ref[pl.ds(3 * count, count), :] = jnp.where(left, 0.0, rows)
    parts_ref[pl.ds(4 * count, 8), :] = jnp.zeros((8, lanes), F32)

    def clear(at, _):
        for table in sums:
            table[pl.ds(pl.multiple_of(at * 64, 64), 64), :] = jnp.zeros((64, lanes), F32)
        return 0

    lax.fori_loop(0, table_rows // 64, clear, 0)

    def block_step(block, _):
        most = codes_ref[block * groups, 0] >> 16
        for group in range(1, groups):
            most = jnp.maximum(most, codes_ref[block * groups + group, 0] >> 16)

        def step(outer, _):
            for inner in range(4):
                for group in range(groups):
                    source = block * groups + group
                    code = codes_ref[source, outer * 4 + inner] & 65535
                    at = jnp.maximum(code - 1, 0)
                    parity = at >> code_bits
                    part = ((inner % 2) * 2 + parity) * count + source * height
                    part = part + outer * 2 + inner // 2
                    part = jnp.where(code > 0, part, 4 * count)
                    here = pl.ds(at & mask, 1)
                    sums[group][here, :] = sums[group][here, :] + parts_ref[pl.ds(part, 1), :]
            return 0

        lax.fori_loop(0, (most + 3) // 4, step, 0)
        return 0

    lax.fori_loop(0, sources // groups, block_step, 0)
    copies = [
        pltpu.make_async_copy(
            sums[group], out_ref.at[pl.ds(group * table_rows, table_rows)], sems.at[group]
        )
        for group in range(groups)
    ]
    for copy in copies:
        copy.start()

    def square(at, total):
        for table in sums:
            rows = table[pl.ds(pl.multiple_of(at * 64, 64), 64), :]
            total = total + jnp.sum((rows * rows).reshape(8, 8, lanes), axis=0)
        return total

    square_ref[...] = lax.fori_loop(0, table_rows // 64, square, jnp.zeros((8, lanes), F32))
    for copy in copies:
        copy.wait()


def table_kernel(factor_ref, weight_ref, first_ref, second_ref, grad_ref, *outs):
    pair, width, rows = weight_ref.shape
    gradient = grad_ref[0].T.reshape(pair, width, rows) * factor_ref[0]
    results = adamw(weight_ref[...], first_ref[...], second_ref[...], gradient, rate_table)
    for out, result in zip(outs, results):
        out[...] = result


def body(
    row_ids,
    counts,
    labels,
    label_mask,
    embeddings,
    embed_first,
    embed_second,
    expert_in,
    in_first,
    in_second,
    expert_out,
    out_first,
    out_second,
    gating,
    gating_first,
    gating_second,
    towers,
    towers_first,
    towers_second,
    heads,
    heads_first,
    heads_second,
    biases,
    biases_first,
    biases_second,
):
    devices = lax.axis_size(AXES)
    mp_count = lax.axis_size("mp")
    dp_count = lax.axis_size("dp")
    mp_index = lax.axis_index("mp")
    samples, tables_here = row_ids.shape
    tables, rows_dev, d_emb = embeddings.shape
    own = samples // mp_count
    requests = samples * tables_here
    capacity = 2 * requests // devices
    height = capacity // 2
    slots = devices * height
    row_bits = rows_dev.bit_length() - 1
    code_bits = row_bits + (tables_here // 2).bit_length() - 1
    pairs = tables // 2
    lanes = 2 * d_emb
    group_rows = tables_here // 2 * rows_dev
    in_rows, out_rows = expert_in.shape[0], expert_out.shape[0]
    experts_here = EXPERTS // mp_count
    hid = expert_in.shape[2] * mp_count
    features = tables * d_emb
    width_out = out_rows * dp_count
    tower_hid = towers.shape[1] // TASKS

    outgoing, place, slot = pl.pallas_call(
        functools.partial(route_kernel, row_bits),
        out_shape=(
            jax.ShapeDtypeStruct((devices, capacity), I32),
            jax.ShapeDtypeStruct((tables_here, samples), I32),
            jax.ShapeDtypeStruct((tables_here, samples), I32),
        ),
        in_specs=[VMEM],
        out_specs=(VMEM, VMEM, VMEM),
        compiler_params=params(32),
        name="route",
    )(row_ids.T)
    codes = lax.all_to_all(
        outgoing.reshape(devices, 1, capacity), AXES, split_axis=0, concat_axis=0, tiled=True
    ).reshape(devices, capacity)

    shard = jnp.concatenate([expert_in, expert_out], axis=0).astype(LOW)
    shard = lax.all_to_all(shard, "mp", split_axis=1, concat_axis=2, tiled=True)
    gathered = lax.all_gather(shard, "dp", axis=0, tiled=False)
    w_in = gathered[:, :in_rows].reshape(in_rows * dp_count, experts_here, hid)
    w_out = gathered[:, in_rows:].reshape(width_out, experts_here, hid)

    table_view = jnp.transpose(embeddings, (0, 2, 1))
    turned = pl.pallas_call(
        turn_kernel,
        grid=(pairs,),
        out_shape=jax.ShapeDtypeStruct((pairs, rows_dev, lanes), F32),
        in_specs=[pl.BlockSpec((2, d_emb, rows_dev), lambda p: (p, 0, 0))],
        out_specs=pl.BlockSpec((1, rows_dev, lanes), lambda p: (p, 0, 0)),
        compiler_params=params(32),
        name="turn",
    )(table_view)
    found = pl.pallas_call(
        functools.partial(find_kernel, mp_count, code_bits),
        grid=(mp_count,),
        out_shape=jax.ShapeDtypeStruct((dp_count, mp_count, height, lanes), LOW),
        in_specs=[SMEM, pl.BlockSpec((group_rows, lanes), lambda m: (m, 0))],
        out_specs=pl.BlockSpec((dp_count, 1, height, lanes), lambda m: (0, m, 0, 0)),
        scratch_shapes=[pltpu.VMEM((height, lanes), F32)],
        compiler_params=params(32),
        name="find",
    )(codes, turned.reshape(pairs * rows_dev, lanes))
    returned = lax.all_to_all(
        found.reshape(devices, height, lanes), AXES, split_axis=0, concat_axis=0, tiled=True
    )
    embedded = pl.pallas_call(
        place_kernel,
        out_shape=jax.ShapeDtypeStruct((samples, tables_here * d_emb), LOW),
        in_specs=[SMEM, VMEM],
        out_specs=VMEM,
        scratch_shapes=[
            pltpu.VMEM((2 * slots, lanes), F32),
            pltpu.VMEM((tables_here // 2, samples, lanes), F32),
        ],
        compiler_params=params(32),
        name="place",
    )(place, returned.reshape(slots, lanes))

    valid_all = (jnp.arange(samples, dtype=I32) < counts[lax.axis_index("dp")]).astype(F32)
    own_start = mp_index * own
    valid_own = lax.dynamic_slice_in_dim(valid_all, own_start, own, 0)
    embed_float = embedded.astype(F32)
    input_sq = jnp.sum(valid_all[:, None] * embed_float * embed_float)
    first = EXPERTS * hid
    second = first + EXPERTS * width_out
    third = second + TASKS * EXPERTS
    fourth = third + TASKS * tower_hid
    inner_bias = biases[:first].reshape(mp_count, experts_here, hid)
    outer_bias = biases[first:second].reshape(mp_count, experts_here, width_out)
    gate_bias = biases[second:third]
    tower_bias = biases[third:fourth].reshape(TASKS, tower_hid)
    head_bias = biases[fourth:]
    inner_here = lax.dynamic_index_in_dim(inner_bias, mp_index, 0, keepdims=False)
    outer_here = lax.dynamic_index_in_dim(outer_bias, mp_index, 0, keepdims=False)

    def exchange(parts):
        return lax.all_to_all(parts, "mp", split_axis=0, concat_axis=0, tiled=True)

    blocks = exchange(jnp.broadcast_to(embedded[None], (mp_count,) + embedded.shape))
    inputs = jnp.transpose(blocks, (1, 0, 2)).reshape(samples, features)
    own_inputs = lax.dynamic_slice_in_dim(inputs, own_start, own, 0)
    preact = jnp.einsum("si,ieh->seh", inputs, w_in, preferred_element_type=F32) + inner_here
    hidden_float, hidden_slope = gelu_pair(preact)
    hidden = hidden_float.astype(LOW)
    partial_y = jnp.einsum("seh,oeh->eso", hidden, w_out, preferred_element_type=F32)
    partial_y = (partial_y + outer_here[:, None, :]).astype(LOW)
    partial_y = partial_y.reshape(experts_here, mp_count, own, width_out).transpose(1, 0, 2, 3)
    expert_y = exchange(partial_y).reshape(EXPERTS, own, width_out).astype(F32)

    gating_low = gating.astype(LOW)
    gate_logit = jnp.dot(own_inputs, gating_low, preferred_element_type=F32) + gate_bias
    gates = jax.nn.softmax(gate_logit.reshape(own, TASKS, EXPERTS), axis=-1)
    mixed = jnp.einsum("ske,eso->sko", gates, expert_y, precision=HIGH)
    mixed_low = mixed.astype(LOW)
    tower_low = towers.astype(LOW).reshape(width_out, TASKS, tower_hid)
    tower_pre = (
        jnp.einsum("sko,okj->skj", mixed_low, tower_low, preferred_element_type=F32) + tower_bias
    )
    tower_act, tower_slope = gelu_pair(tower_pre)
    logits = jnp.sum(tower_act * heads, axis=-1) + head_bias
    target_float = labels.astype(F32)
    weights = valid_own[:, None] * label_mask.astype(F32)
    loss_here = jnp.sum(weights * (jax.nn.softplus(logits) - target_float * logits))
    expert_sq = jnp.sum(valid_own[None, :, None] * expert_y * expert_y, axis=(1, 2))
    mixed_sq = jnp.sum(valid_own[:, None, None] * mixed * mixed, axis=(0, 2))
    logit_grad = weights * (jax.nn.sigmoid(logits) - target_float)
    heads_grad = jnp.einsum("sk,skj->kj", logit_grad, tower_act, precision=HIGH)
    head_bias_grad = jnp.sum(logit_grad, axis=0)
    tower_grad = (logit_grad[:, :, None] * heads * tower_slope).astype(LOW)
    towers_grad = jnp.einsum(
        "sko,skj->okj", mixed_low, tower_grad, preferred_element_type=F32
    ).reshape(width_out, TASKS * tower_hid)
    tower_bias_grad = jnp.sum(tower_grad.astype(F32), axis=0)
    mixed_grad = jnp.einsum("skj,okj->sko", tower_grad, tower_low, preferred_element_type=F32)
    gate_grad = jnp.einsum("sko,eso->ske", mixed_grad, expert_y, precision=HIGH)
    gate_logit_grad = gates * (gate_grad - jnp.sum(gates * gate_grad, axis=-1, keepdims=True))
    gate_logit_grad = gate_logit_grad.reshape(own, TASKS * EXPERTS).astype(LOW)
    output_grad = jnp.einsum("ske,sko->eso", gates, mixed_grad, precision=HIGH).astype(LOW)
    gating_grad = jnp.einsum("si,sk->ki", own_inputs, gate_logit_grad, preferred_element_type=F32)
    gate_bias_grad = jnp.sum(gate_logit_grad.astype(F32), axis=0)
    outer_bias_grad = jnp.sum(output_grad.astype(F32), axis=1)
    input_gate_grad = jnp.einsum(
        "sk,ik->si", gate_logit_grad, gating_low, preferred_element_type=F32
    )
    output_rows = exchange(output_grad.reshape(mp_count, experts_here, own, width_out))
    output_rows = output_rows.transpose(1, 0, 2, 3).reshape(experts_here, samples, width_out)

    hidden_grad = jnp.einsum("eso,oeh->seh", output_rows, w_out, preferred_element_type=F32)
    preact_grad = (hidden_grad * hidden_slope).astype(LOW)
    out_grad = jnp.einsum("eso,seh->oeh", output_rows, hidden, preferred_element_type=F32)
    in_grad = jnp.einsum("si,seh->ieh", inputs, preact_grad, preferred_element_type=F32)
    inner_bias_part = jnp.sum(preact_grad.astype(F32), axis=0)
    input_grad = jnp.einsum("seh,ieh->si", preact_grad, w_in, preferred_element_type=F32)
    own_part = lax.dynamic_slice_in_dim(input_grad, own_start, own, 0) + input_gate_grad
    input_grad = lax.dynamic_update_slice_in_dim(input_grad, own_part, own_start, 0)
    input_parts = input_grad.astype(LOW).reshape(samples, mp_count, tables_here * d_emb)
    embed_grad = jnp.sum(exchange(input_parts.transpose(1, 0, 2)).astype(F32), axis=0)

    back_rows = pl.pallas_call(
        send_kernel,
        out_shape=jax.ShapeDtypeStruct((slots, lanes), LOW),
        in_specs=[SMEM, VMEM],
        out_specs=VMEM,
        scratch_shapes=[
            pltpu.VMEM((tables_here // 2, 2 * samples, lanes), F32),
            pltpu.VMEM((2 * slots, lanes), F32),
        ],
        compiler_params=params(32),
        name="send",
    )(slot, embed_grad)
    arrived = lax.all_to_all(
        back_rows.reshape(devices, height, lanes), AXES, split_axis=0, concat_axis=0, tiled=True
    )
    table_grad, table_sq = pl.pallas_call(
        functools.partial(add_kernel, mp_count, code_bits),
        out_shape=(
            jax.ShapeDtypeStruct((pairs * rows_dev, lanes), F32),
            jax.ShapeDtypeStruct((8, lanes), F32),
        ),
        in_specs=[SMEM, VMEM],
        out_specs=(pl.BlockSpec(memory_space=pl.ANY), VMEM),
        scratch_shapes=[
            pltpu.VMEM((4 * slots + 8, lanes), F32),
            pltpu.SemaphoreType.DMA((mp_count,)),
        ]
        + [pltpu.VMEM((group_rows, lanes), F32)] * mp_count,
        compiler_params=params(60),
        name="add",
    )(codes, arrived.reshape(slots, lanes))

    def scatter_grad(grad, rows):
        parts = grad.astype(LOW).reshape(dp_count, rows, experts_here, mp_count, hid // mp_count)
        return parts.transpose(0, 3, 1, 2, 4).reshape(devices, rows * experts_here, hid // mp_count)

    grad_parts = jnp.concatenate([scatter_grad(in_grad, in_rows), scatter_grad(out_grad, out_rows)], 1)
    grad_parts = lax.all_to_all(grad_parts, AXES, split_axis=0, concat_axis=0, tiled=True)
    grad_sum = jnp.sum(
        grad_parts.reshape(dp_count, mp_count, in_rows + out_rows, experts_here, -1).astype(F32), 0
    )
    grad_sum = grad_sum.transpose(1, 0, 2, 3).reshape(in_rows + out_rows, EXPERTS, -1)
    in_sum, out_sum = grad_sum[:in_rows], grad_sum[in_rows:]

    inner_bias_grad = lax.dynamic_update_slice_in_dim(
        jnp.zeros((mp_count, experts_here, hid), F32), inner_bias_part[None], mp_index, 0
    )
    bias_grad = jnp.concatenate(
        [
            inner_bias_grad.reshape(-1),
            outer_bias_grad.reshape(-1),
            gate_bias_grad,
            tower_bias_grad.reshape(-1),
            head_bias_grad,
        ]
    )

    def sum_over_all(value):
        size = value.size
        unit = devices * 1024
        padded = jnp.pad(value.reshape(-1), (0, -size % unit)).reshape(devices, -1, 128)
        parts = lax.all_to_all(padded.astype(LOW), AXES, split_axis=0, concat_axis=0, tiled=True)
        share = jnp.sum(parts.astype(F32), axis=0)
        share_sq = jnp.sum(share * share)
        spread = jnp.broadcast_to(share.astype(LOW)[None], padded.shape)
        whole = lax.all_to_all(spread, AXES, split_axis=0, concat_axis=0, tiled=True)
        return whole.astype(F32).reshape(-1)[:size].reshape(value.shape), share_sq

    towers_sum, towers_sq = sum_over_all(towers_grad)
    rest, rest_sq = sum_over_all(
        jnp.concatenate([gating_grad.reshape(-1), heads_grad.reshape(-1), bias_grad])
    )
    gating_sum = rest[: gating_grad.size].reshape(gating_grad.shape).T
    heads_sum = rest[gating_grad.size : gating_grad.size + heads_grad.size].reshape(heads.shape)
    bias_sum = rest[gating_grad.size + heads_grad.size :]
    squares = (
        jnp.sum(table_sq) + jnp.sum(in_sum * in_sum) + jnp.sum(out_sum * out_sum) + towers_sq + rest_sq
    )
    sums_here = jnp.concatenate(
        [loss_here[None], input_sq[None], expert_sq, mixed_sq, jnp.sum(weights)[None], squares[None]]
    )
    sums_here = jnp.pad(sums_here, (0, 128 - sums_here.size))
    sums = jnp.sum(
        lax.all_to_all(
            jnp.broadcast_to(sums_here, (devices, 1, 128)),
            AXES,
            split_axis=0,
            concat_axis=0,
            tiled=True,
        ),
        axis=(0, 1),
    )
    stat_end = 2 + EXPERTS + TASKS
    weight_total = sums[stat_end]
    grad_norm = jnp.sqrt(sums[stat_end + 1]) / weight_total
    factor = jnp.minimum(1.0, clip_max / grad_norm) / weight_total

    table_spec = pl.BlockSpec((2, d_emb, rows_dev // 2), lambda p, c: (p, 0, c))
    embed_out = pl.pallas_call(
        table_kernel,
        grid=(pairs, 2),
        out_shape=(jax.ShapeDtypeStruct(table_view.shape, F32),) * 3,
        in_specs=[
            SMEM,
            table_spec,
            table_spec,
            table_spec,
            pl.BlockSpec((1, rows_dev // 2, lanes), lambda p, c: (p, c, 0)),
        ],
        out_specs=(table_spec,) * 3,
        compiler_params=params(48),
        name="tables",
    )(
        factor.reshape(1),
        table_view,
        jnp.transpose(embed_first, (0, 2, 1)),
        jnp.transpose(embed_second, (0, 2, 1)),
        table_grad.reshape(pairs, rows_dev, lanes),
    )
    embed_out = [jnp.transpose(value, (0, 2, 1)) for value in embed_out]
    in_out = adamw(expert_in, in_first, in_second, in_sum * factor, rate_dense)
    out_out = adamw(expert_out, out_first, out_second, out_sum * factor, rate_dense)
    gating_out = adamw(gating, gating_first, gating_second, gating_sum * factor, rate_dense)
    towers_out = adamw(towers, towers_first, towers_second, towers_sum * factor, rate_dense)
    heads_out = adamw(heads, heads_first, heads_second, heads_sum * factor, rate_dense)
    biases_out = adamw(biases, biases_first, biases_second, bias_sum * factor, rate_dense)
    n_valid = jnp.sum(counts).astype(F32)
    widths = jnp.concatenate(
        [jnp.full((1,), features, F32), jnp.full((EXPERTS + TASKS,), width_out, F32)]
    )
    stats = jnp.sqrt(sums[1:stat_end] / (n_valid * widths) + stat_eps)
    loss = jnp.stack([sums[0], weight_total])
    return (
        *embed_out,
        *in_out,
        in_out[0].astype(LOW),
        *out_out,
        out_out[0].astype(LOW),
        *gating_out,
        *towers_out,
        *heads_out,
        *biases_out,
        grad_norm.reshape(1),
        loss,
        stats,
    )


def solution(mesh):
    rows = P(None, AXES, None)
    expert = P("dp", None, "mp")
    sample = P(AXES, None)
    placed = (P("dp", "mp"), P(), sample, sample) + (rows,) * 3 + (expert,) * 6 + (P(),) * 12
    results = (rows,) * 3 + (expert,) * 8 + (P(),) * 15
    return jax.shard_map(body, mesh=mesh, in_specs=placed, out_specs=results, check_vma=False)
```

```python
import functools
import math

import jax
import jax.numpy as jnp
from jax import lax
from jax.experimental import pallas as pl
from jax.experimental.pallas import tpu as pltpu
from jax.sharding import PartitionSpec as P

EXPERTS = 8
TASKS = 5
STEP = 3

HIGH = lax.Precision.HIGHEST
beta_one = 0.5
beta_two = 0.5
adam_eps = 1e-08
decay = 0.01
clip_max = 0.002
rate_table = 0.5
rate_dense = 0.02
stat_eps = 1e-06

LOW = jnp.bfloat16
F32 = jnp.float32
I32 = jnp.int32
MIB = 1024 * 1024
AXES = ("dp", "mp")


def params(mib):
    return pltpu.CompilerParams(vmem_limit_bytes=mib * MIB)


VMEM = pl.BlockSpec(memory_space=pltpu.VMEM)
SMEM = pl.BlockSpec(memory_space=pltpu.SMEM)


def adamw(weight, first, second, gradient, rate):
    first_next = beta_one * first + (1.0 - beta_one) * gradient
    second_next = beta_two * second + (1.0 - beta_two) * gradient * gradient
    corrected = first_next / (1.0 - beta_one**STEP)
    scaled = jnp.sqrt(second_next / (1.0 - beta_two**STEP))
    return (
        weight - rate * (corrected / (scaled + adam_eps) + decay * weight),
        first_next,
        second_next,
    )


def route_kernel(row_bits, ids_ref, out_ref, place_ref, slot_ref):
    devices, capacity = out_ref.shape
    tables, samples = ids_ref.shape
    rows_dev = 1 << row_bits
    halves = devices * capacity // 2
    width = 256
    upper = (
        lax.broadcasted_iota(I32, (width, width), 0) <= lax.broadcasted_iota(I32, (width, width), 1)
    ).astype(LOW)
    owners = lax.broadcasted_iota(I32, (devices, width), 0)
    slots = lax.broadcasted_iota(I32, (capacity, width), 0)
    carry = jnp.zeros((devices, 1), F32)
    total = jnp.zeros((2 * devices, capacity), F32)
    for table in range(tables):
        parity = table % 2
        for part in range(samples // width):
            cols = pl.ds(part * width, width)
            ids = ids_ref[pl.ds(table, 1), cols]
            owner = ids >> row_bits
            code = (parity * (tables // 2) + table // 2) * rows_dev + (ids & (rows_dev - 1)) + 1
            onehot = (owner == owners).astype(F32)
            counted = jnp.dot(onehot.astype(LOW), upper, preferred_element_type=F32) + carry
            rank = jnp.sum(onehot * counted, axis=0, keepdims=True).astype(I32) - 1
            carry = counted[:, width - 1 :]
            at_slot = (rank == slots).astype(LOW)
            high = (code >> 7).astype(F32)
            low = (code & 127).astype(F32)
            pieces = jnp.concatenate([onehot * high, onehot * low], axis=0).astype(LOW)
            total += lax.dot_general(
                pieces, at_slot, (((1,), (1,)), ((), ())), preferred_element_type=F32
            )
            row = owner * (capacity // 2) + (rank >> 1)
            half = rank & 1
            place_ref[pl.ds(table, 1), cols] = (half ^ parity) * halves + row
            slot_ref[pl.ds(table, 1), cols] = half * halves + row
    codes = (total[:devices] * 128.0 + total[devices:]).astype(I32)
    first = lax.broadcasted_iota(I32, (devices, capacity), 1) == 0
    counted = jnp.where(first, carry * 65536.0, 0.0).astype(I32)
    out_ref[...] = codes + counted


def turn_kernel(table_ref, out_ref):
    pair, width, rows = table_ref.shape
    out_ref[0] = table_ref[...].reshape(pair * width, rows).T


def left_lanes(shape):
    return lax.broadcasted_iota(I32, shape, len(shape) - 1) < 64


def find_kernel(groups, group_rows, code_bits, codes_ref, table_ref, out_ref, rows_ref):
    blocks, _, height, lanes = out_ref.shape
    mask = (1 << code_bits) - 1
    left = left_lanes((1, lanes))

    def fetch(code, base, side):
        at = jnp.maximum((code & 65535) - 1, 0)
        row = table_ref[pl.ds((at & mask) + base, 1), :]
        return row, ((at >> code_bits) ^ side) * 64

    def source_step(source, _):
        count = codes_ref[source, 0] >> 16
        group = lax.rem(source, groups)
        base = group * group_rows

        def step(outer, _):
            got = []
            for inner in range(8):
                at = outer * 8 + inner
                even = fetch(codes_ref[source, 2 * at], base, 0)
                odd = fetch(codes_ref[source, 2 * at + 1], base, 1)
                got.append((at, even, odd))
            got = [
                (at, jnp.where(left, pltpu.roll(*even, 1), pltpu.roll(*odd, 1)))
                for at, even, odd in got
            ]
            for at, row in got:
                rows_ref[pl.ds(at, 1), :] = row
            return 0

        lax.fori_loop(0, (count + 15) // 16, step, 0)
        out_ref[lax.div(source, groups), group] = rows_ref[...].astype(LOW)
        return 0

    lax.fori_loop(0, blocks * groups, source_step, 0)


def place_kernel(place_ref, rows_ref, out_ref, both_ref, flat_ref):
    count, lanes = rows_ref.shape
    tables, samples = place_ref.shape
    rows = rows_ref[...].astype(F32)
    both_ref[pl.ds(0, count), :] = rows
    both_ref[pl.ds(count, count), :] = pltpu.roll(rows, 64, 1)
    left = left_lanes((1, lanes))

    def step(outer, _):
        got = []
        for inner in range(8):
            sample = outer * 8 + inner
            for pair in range(tables // 2):
                even = both_ref[pl.ds(place_ref[2 * pair, sample], 1), :]
                odd = both_ref[pl.ds(place_ref[2 * pair + 1, sample], 1), :]
                got.append((pair, sample, jnp.where(left, even, odd)))
        for pair, sample, row in got:
            flat_ref[pair, pl.ds(sample, 1), :] = row
        return 0

    lax.fori_loop(0, samples // 8, step, 0)
    for pair in range(tables // 2):
        out_ref[:, pair * lanes : (pair + 1) * lanes] = flat_ref[pair].astype(LOW)


def send_kernel(slot_ref, grad_ref, out_ref, both_ref, rows_ref):
    count, lanes = out_ref.shape
    tables, samples = slot_ref.shape
    for pair in range(tables // 2):
        rows = grad_ref[:, pair * lanes : (pair + 1) * lanes]
        both_ref[pair, pl.ds(0, samples), :] = rows
        both_ref[pair, pl.ds(samples, samples), :] = pltpu.roll(rows, 64, 1)
    bits = count.bit_length() - 1

    def step(outer, _):
        got = []
        for inner in range(8):
            sample = outer * 8 + inner
            for table in range(tables):
                slot = slot_ref[table, sample]
                turned = (slot >> bits) ^ (table % 2)
                got.append(
                    (slot, both_ref[table // 2, pl.ds(turned * samples + sample, 1), :])
                )
        for slot, row in got:
            rows_ref[pl.ds(slot, 1), :] = row
        return 0

    lax.fori_loop(0, samples // 8, step, 0)
    left = left_lanes((count, lanes))
    out_ref[...] = jnp.where(
        left, rows_ref[pl.ds(0, count), :], rows_ref[pl.ds(count, count), :]
    ).astype(LOW)


def add_kernel(groups, code_bits, codes_ref, rows_ref, out_ref, square_ref, parts_ref, sems, *sums):
    count, lanes = rows_ref.shape
    sources = codes_ref.shape[0]
    height = count // sources
    mask = (1 << code_bits) - 1
    table_rows = sums[0].shape[0]
    left = left_lanes((count, lanes))
    rows = rows_ref[...].astype(F32)
    turned = pltpu.roll(rows, 64, 1)
    parts_ref[pl.ds(0, count), :] = jnp.where(left, rows, 0.0)
    parts_ref[pl.ds(count, count), :] = jnp.where(left, 0.0, turned)
    parts_ref[pl.ds(2 * count, count), :] = jnp.where(left, turned, 0.0)
    parts_ref[pl.ds(3 * count, count), :] = jnp.where(left, 0.0, rows)
    parts_ref[pl.ds(4 * count, 8), :] = jnp.zeros((8, lanes), F32)

    def clear(at, _):
        for table in sums:
            table[pl.ds(pl.multiple_of(at * 64, 64), 64), :] = jnp.zeros((64, lanes), F32)
        return 0

    lax.fori_loop(0, table_rows // 64, clear, 0)

    def block_step(block, _):
        most = codes_ref[block * groups, 0] >> 16
        for group in range(1, groups):
            most = jnp.maximum(most, codes_ref[block * groups + group, 0] >> 16)

        def step(outer, _):
            for inner in range(4):
                got = []
                for group in range(groups):
                    source = block * groups + group
                    code = codes_ref[source, outer * 4 + inner] & 65535
                    at = jnp.maximum(code - 1, 0)
                    parity = at >> code_bits
                    part = ((inner % 2) * 2 + parity) * count + source * height
                    part = part + outer * 2 + inner // 2
                    part = jnp.where(code > 0, part, 4 * count)
                    here = pl.ds(at & mask, 1)
                    got.append((here, sums[group][here, :] + parts_ref[pl.ds(part, 1), :]))
                for group, (here, row) in enumerate(got):
                    sums[group][here, :] = row
            return 0

        lax.fori_loop(0, (most + 3) // 4, step, 0)
        return 0

    lax.fori_loop(0, sources // groups, block_step, 0)
    copies = [
        pltpu.make_async_copy(
            sums[group], out_ref.at[pl.ds(group * table_rows, table_rows)], sems.at[group]
        )
        for group in range(groups)
    ]
    for copy in copies:
        copy.start()

    def square(at, total):
        for table in sums:
            rows = table[pl.ds(pl.multiple_of(at * 64, 64), 64), :]
            total = total + jnp.sum((rows * rows).reshape(8, 8, lanes), axis=0)
        return total

    square_ref[...] = lax.fori_loop(0, table_rows // 64, square, jnp.zeros((8, lanes), F32))
    for copy in copies:
        copy.wait()


def gelu_parts(value):
    scale = math.sqrt(2.0 / math.pi)
    square = value * value
    bend = jnp.tanh(scale * value * (1.0 + 0.044715 * square))
    half = 0.5 * (1.0 + bend)
    slope = half + 0.5 * value * (1.0 - bend * bend) * (scale * (1.0 + 3 * 0.044715 * square))
    return value * half, slope


def dot(a, b, axes=((1,), (0,)), precision=None):
    return lax.dot_general(
        a, b, (axes, ((), ())), preferred_element_type=F32, precision=precision
    )


NT = ((1,), (1,))
TN = ((0,), (0,))
MESH = pl.DeviceIdType.MESH


def meet(peers):
    me = lax.axis_index("mp")
    barrier = pltpu.get_barrier_semaphore()
    for step in range(1, peers):
        pl.semaphore_signal(
            barrier, inc=1, device_id={"mp": lax.rem(me + step, peers)}, device_id_type=MESH
        )
    pl.semaphore_wait(barrier, peers - 1)
    return me


def ahead_kernel(
    count_ref,
    x_ref,
    w_ref,
    b1_ref,
    b2_ref,
    wg_ref,
    bg_ref,
    w3_ref,
    tb1_ref,
    heads_ref,
    tb2_ref,
    labels_ref,
    mask_ref,
    blocks_ref,
    hid_ref,
    slope_ref,
    dy_ref,
    dgl_ref,
    small_ref,
    stats_ref,
    y_send,
    y_ref,
    gates_ref,
    mixb_ref,
    dmix_ref,
    dg_ref,
    dy_send,
    pack_ref,
    act_ref,
    x_out,
    x_in,
    y_out,
    y_in,
    d_out,
    d_in,
):
    peers, samples, width = blocks_ref.shape
    here = hid_ref.shape[0]
    out_width = y_ref.shape[3]
    own = y_ref.shape[2]
    experts = peers * here
    tasks, tower_hid = heads_ref.shape
    shards, hid = w_ref.shape[1], w_ref.shape[3]
    in_rows = peers * width // shards
    me = meet(peers)

    def other(step):
        return lax.rem(me + step, peers)

    def x_copy(turn, step):
        target = other(step)
        rows = pl.ds(pl.multiple_of(lax.rem(target + turn + 1, peers) * own, own), own)
        return pltpu.make_async_remote_copy(
            x_ref.at[rows],
            blocks_ref.at[me, rows],
            x_out.at[turn, step],
            x_in.at[turn, step],
            device_id={"mp": target},
            device_id_type=MESH,
        )

    def y_copy(turn):
        return pltpu.make_async_remote_copy(
            y_send.at[turn],
            y_ref.at[me],
            y_out.at[turn],
            y_in.at[turn],
            device_id={"mp": other(turn + 1)},
            device_id_type=MESH,
        )

    def d_copy(step):
        target = other(step)
        return pltpu.make_async_remote_copy(
            dy_send.at[pl.ds(target * here, here)],
            dy_ref.at[:, pl.ds(pl.multiple_of(me * own, own), own), :],
            d_out.at[step],
            d_in.at[step],
            device_id={"mp": target},
            device_id_type=MESH,
        )

    for turn in range(peers):
        for step in range(1, peers):
            x_copy(turn, step).start()
    blocks_ref[me] = x_ref[...]
    limit = count_ref[0]

    def expert_step(turn, _):
        for step in range(1, peers):
            x_copy(turn, step).wait_recv()
        chunk = lax.rem(me + turn + 1, peers)
        rows = pl.ds(pl.multiple_of(chunk * own, own), own)
        x = jnp.concatenate([blocks_ref[block, rows] for block in range(peers)], axis=1)
        for e in range(here):
            w_in = w_ref[e, :, :in_rows, :].reshape(peers * width, hid)
            act_ref[...] = dot(x, w_in) + b1_ref[e]

            def gelu_step(tile, _):
                at = pl.multiple_of(tile * 32, 32)
                value, slope = gelu_parts(act_ref[pl.ds(at, 32), :])
                there = pl.ds(pl.multiple_of(chunk * own + at, 32), 32)
                hid_ref[e, there, :] = value.astype(LOW)
                slope_ref[e, there, :] = slope
                return 0

            lax.fori_loop(0, own // 32, gelu_step, 0)
            w_out = w_ref[e, :, in_rows:, :].reshape(out_width, hid)
            y_send[turn, e] = (dot(hid_ref[e, rows, :], w_out, NT) + b2_ref[e]).astype(LOW)

        @pl.when(turn < peers - 1)
        def _():
            y_copy(turn).start()

        return 0

    lax.fori_loop(0, peers, expert_step, 0)
    y_ref[me] = y_send[peers - 1]

    own_rows = pl.ds(pl.multiple_of(me * own, own), own)
    x_own = jnp.concatenate([blocks_ref[block, own_rows] for block in range(peers)], axis=1)
    logits = dot(x_own, wg_ref[...], NT) + bg_ref[...]
    for k in range(tasks):
        part = logits[:, k * experts : (k + 1) * experts]
        part = jnp.exp(part - jnp.max(part, axis=1, keepdims=True))
        gates_ref[:, k * experts : (k + 1) * experts] = part / jnp.sum(part, axis=1, keepdims=True)

    stats_ref[...] = jnp.zeros_like(stats_ref)

    def square_step(tile, total):
        at = pl.multiple_of(tile * 64, 64)
        valid = (lax.broadcasted_iota(I32, (64, 1), 0) + at) < limit
        part = jnp.where(valid, x_ref[pl.ds(at, 64), :].astype(F32), 0.0)
        return total + jnp.sum((part * part).reshape(8, 8, width), axis=0)

    x_square = lax.fori_loop(0, samples // 64, square_step, jnp.zeros((8, width), F32))
    stats_ref[experts + tasks, :, :width] = x_square
    for turn in range(peers - 1):
        y_copy(turn).wait_recv()

    tile_rows = 16

    def tile_of(tile):
        at = pl.multiple_of(tile * tile_rows, tile_rows)
        return at, pl.ds(at, tile_rows)

    def mix_step(tile, _):
        at, rows = tile_of(tile)
        valid = (lax.broadcasted_iota(I32, (tile_rows, 1), 0) + (at + me * own)) < limit
        gates = gates_ref[rows, :]
        mixed = [None] * tasks
        for e in range(experts):
            y = y_ref[e // here, e % here, rows, :].astype(F32)
            square = jnp.where(valid, y * y, 0.0)
            stats_ref[e] += square[:8] + square[8:]
            for k in range(tasks):
                term = gates[:, k * experts + e : k * experts + e + 1] * y
                mixed[k] = term if e == 0 else mixed[k] + term
        for k in range(tasks):
            square = jnp.where(valid, mixed[k] * mixed[k], 0.0)
            stats_ref[experts + k] += square[:8] + square[8:]
            mixb_ref[k, rows, :] = mixed[k].astype(LOW)
        return 0

    lax.fori_loop(0, own // tile_rows, mix_step, 0)

    pack_ref[...] = jnp.zeros_like(pack_ref)
    blocks_x = peers * width // 128
    heads_at = blocks_x * tasks * experts
    tower_at = heads_at + tasks * tower_hid // 128
    outer_at = tower_at + tasks * tower_hid // 128
    rest_at = outer_at + experts * out_width // 128
    loss = jnp.zeros((1, 1), F32)
    weight_sum = jnp.zeros((1, 1), F32)
    row_id = lax.broadcasted_iota(I32, (own, 1), 0) + me * own
    for k in range(tasks):
        cols = slice(k * tower_hid, (k + 1) * tower_hid)
        z, slope = gelu_parts(dot(mixb_ref[k], w3_ref[:, cols]) + tb1_ref[k : k + 1, :])
        head = heads_ref[k : k + 1, :]
        logit = jnp.sum(z * head, axis=1, keepdims=True) + tb2_ref[0, k]
        small = jnp.exp(-jnp.abs(logit))
        label = labels_ref[:, k : k + 1].astype(F32)
        weight = jnp.where(row_id < limit, mask_ref[:, k : k + 1].astype(F32), 0.0)
        soft = jnp.maximum(logit, 0.0) + jnp.log1p(small)
        loss += jnp.sum(weight * (soft - label * logit), axis=0, keepdims=True)
        weight_sum += jnp.sum(weight, axis=0, keepdims=True)
        chance = jnp.where(logit >= 0.0, 1.0, small) / (1.0 + small)
        dl = weight * (chance - label)
        g_head = jnp.sum(dl * z, axis=0, keepdims=True)
        dz = (dl * head * slope).astype(LOW)
        g_bias = jnp.sum(dz.astype(F32), axis=0, keepdims=True)
        for part in range(tower_hid // 128):
            lane = slice(part * 128, (part + 1) * 128)
            at = k * (tower_hid // 128) + part
            pack_ref[heads_at + at : heads_at + at + 1, :] = g_head[:, lane]
            pack_ref[tower_at + at : tower_at + at + 1, :] = g_bias[:, lane]
        pack_ref[rest_at + 1 : rest_at + 2, k : k + 1] = jnp.sum(dl, axis=0, keepdims=True)
        dmix_ref[k] = dot(dz, w3_ref[:, cols], NT)
        small_ref[:, cols] = dot(mixb_ref[k], dz, TN).astype(LOW)
    stats_ref[experts + tasks + 1, :1, :1] = loss
    stats_ref[experts + tasks + 1, :1, 1:2] = weight_sum

    def dy_step(tile, _):
        at, rows = tile_of(tile)
        gates = gates_ref[rows, :]
        dmix = [dmix_ref[k, rows, :] for k in range(tasks)]
        for e in range(experts):
            total = None
            for k in range(tasks):
                term = gates[:, k * experts + e : k * experts + e + 1] * dmix[k]
                total = term if k == 0 else total + term
            dy_send[e, rows, :] = total.astype(LOW)
        return 0

    lax.fori_loop(0, own // tile_rows, dy_step, 0)
    for step in range(1, peers):
        d_copy(step).start()
    dy_ref[:, own_rows, :] = dy_send[pl.ds(me * here, here)]
    ones = jnp.ones((8, own), LOW)
    for e in range(experts):
        g_outer = dot(ones, dy_send[e])
        for part in range(out_width // 128):
            at = outer_at + e * (out_width // 128) + part
            pack_ref[at : at + 1, :] = g_outer[:1, part * 128 : (part + 1) * 128]

    lane = lax.broadcasted_iota(I32, (tile_rows, tasks * experts), 1)

    def dg_step(tile, _):
        at, rows = tile_of(tile)
        dmix = [dmix_ref[k, rows, :] for k in range(tasks)]
        found = jnp.zeros((tile_rows, tasks * experts), F32)
        for e in range(experts):
            y = y_ref[e // here, e % here, rows, :].astype(F32)
            for k in range(tasks):
                value = jnp.sum(dmix[k] * y, axis=1, keepdims=True)
                found = jnp.where(lane == k * experts + e, value, found)
        dg_ref[rows, :] = found
        return 0

    lax.fori_loop(0, own // tile_rows, dg_step, 0)
    gates = gates_ref[...]
    dg = dg_ref[...]
    flat = (tasks * experts, tasks * experts)
    same = lax.broadcasted_iota(I32, flat, 0) // experts == lax.broadcasted_iota(I32, flat, 1) // experts
    mean = dot(gates * dg, same.astype(F32), precision=HIGH)
    dgl = (gates * (dg - mean)).astype(LOW)
    dgl_ref[...] = dgl
    pack_ref[rest_at : rest_at + 1, : tasks * experts] = jnp.sum(
        dgl.astype(F32), axis=0, keepdims=True
    )
    g_gating = dot(dgl, x_own, TN)
    for part in range(blocks_x):
        at = part * tasks * experts
        pack_ref[at : at + tasks * experts, :] = g_gating[:, part * 128 : (part + 1) * 128]
    small_ref[:, tasks * tower_hid :] = pack_ref[...].astype(LOW)

    for turn in range(peers):
        for step in range(1, peers):
            x_copy(turn, step).wait_send()
    for turn in range(peers - 1):
        y_copy(turn).wait_send()
    for step in range(1, peers):
        d_copy(step).wait()


def back_kernel(
    dy_ref,
    hid_ref,
    slope_ref,
    blocks_ref,
    w_ref,
    dgl_ref,
    wg_ref,
    dx_ref,
    parts_ref,
    b1_ref,
    dpre_ref,
    dx_send,
    dx_recv,
    x_out,
    x_in,
):
    peers, samples, width = blocks_ref.shape
    here, _, out_width = dy_ref.shape
    own = samples // peers
    hid = hid_ref.shape[2]
    shards, rows_both = w_ref.shape[1], w_ref.shape[2]
    in_rows = peers * width // shards
    out_rows = rows_both - in_rows
    features = peers * width
    me = meet(peers)

    def chunk_rows(turn):
        return pl.ds(pl.multiple_of(lax.rem(me + turn, peers) * own, own), own)

    def x_copy(turn, step):
        target = lax.rem(me + step, peers)
        rows = chunk_rows(turn)
        return pltpu.make_async_remote_copy(
            dx_send.at[target, rows],
            dx_recv.at[me, rows],
            x_out.at[turn, step],
            x_in.at[turn, step],
            device_id={"mp": target},
            device_id_type=MESH,
        )

    b1_ref[...] = jnp.zeros_like(b1_ref)

    def chunk_step(turn, _):
        rows = chunk_rows(turn)
        mine = jnp.where(turn == 0, 1.0, 0.0)
        gate = (dgl_ref[...].astype(F32) * mine).astype(LOW)
        total = dot(gate, wg_ref[...])
        for e in range(here):
            w_out = w_ref[e, :, in_rows:, :].reshape(out_width, hid)
            dpre = (dot(dy_ref[e, rows, :], w_out) * slope_ref[e, rows, :]).astype(LOW)
            dpre_ref[e, rows, :] = dpre
            b1_ref[e] += dot(jnp.ones((8, own), LOW), dpre)
            w_in = w_ref[e, :, :in_rows, :].reshape(features, hid)
            total += dot(dpre, w_in, NT)
        for target in range(peers):
            dx_send[target, rows] = total[:, target * width : (target + 1) * width].astype(LOW)
        for step in range(1, peers):
            x_copy(turn, step).start()
        return 0

    lax.fori_loop(0, peers, chunk_step, 0)

    lanes = parts_ref.shape[3]
    blocks_in = width // 128
    per_in = 128 // in_rows
    per_out = 128 // out_rows
    for e in range(here):

        def in_step(block, _):
            cols = pl.ds(pl.multiple_of(lax.rem(block, blocks_in) * 128, 128), 128)
            x = blocks_ref[lax.div(block, blocks_in), :, cols]
            value = dot(x, dpre_ref[e], TN).astype(LOW)
            for shard in range(per_in):
                for target in range(peers):
                    parts_ref[
                        block * per_in + shard, target, e * rows_both : e * rows_both + in_rows, :
                    ] = value[
                        shard * in_rows : (shard + 1) * in_rows, target * lanes : (target + 1) * lanes
                    ]
            return 0

        lax.fori_loop(0, features // 128, in_step, 0)

        def out_step(block, _):
            cols = pl.ds(pl.multiple_of(block * 128, 128), 128)
            value = dot(dy_ref[e, :, cols], hid_ref[e], TN).astype(LOW)
            for shard in range(per_out):
                for target in range(peers):
                    parts_ref[
                        block * per_out + shard,
                        target,
                        e * rows_both + in_rows : (e + 1) * rows_both,
                        :,
                    ] = value[
                        shard * out_rows : (shard + 1) * out_rows,
                        target * lanes : (target + 1) * lanes,
                    ]
            return 0

        lax.fori_loop(0, out_width // 128, out_step, 0)

    for turn in range(peers):
        for step in range(1, peers):
            x_copy(turn, step).wait()
    total = dx_send[me].astype(F32)
    for step in range(1, peers):
        total = total + dx_recv[lax.rem(me + step, peers)].astype(F32)
    dx_ref[...] = total


def table_kernel(factor_ref, weight_ref, first_ref, second_ref, grad_ref, *outs):
    pair, width, rows = weight_ref.shape
    gradient = grad_ref[0].T.reshape(pair, width, rows) * factor_ref[0]
    results = adamw(weight_ref[...], first_ref[...], second_ref[...], gradient, rate_table)
    for out, result in zip(outs, results):
        out[...] = result


def body(
    row_ids,
    counts,
    labels,
    label_mask,
    embeddings,
    embed_first,
    embed_second,
    expert_in,
    in_first,
    in_second,
    expert_out,
    out_first,
    out_second,
    gating,
    gating_first,
    gating_second,
    towers,
    towers_first,
    towers_second,
    heads,
    heads_first,
    heads_second,
    biases,
    biases_first,
    biases_second,
):
    devices = lax.axis_size(AXES)
    mp_count = lax.axis_size("mp")
    dp_count = lax.axis_size("dp")
    mp_index = lax.axis_index("mp")
    samples, tables_here = row_ids.shape
    tables, rows_dev, d_emb = embeddings.shape
    own = samples // mp_count
    requests = samples * tables_here
    capacity = 2 * requests // devices
    height = capacity // 2
    slots = devices * height
    row_bits = rows_dev.bit_length() - 1
    code_bits = row_bits + (tables_here // 2).bit_length() - 1
    pairs = tables // 2
    lanes = 2 * d_emb
    group_rows = tables_here // 2 * rows_dev
    in_rows, out_rows = expert_in.shape[0], expert_out.shape[0]
    experts_here = EXPERTS // mp_count
    hid = expert_in.shape[2] * mp_count
    features = tables * d_emb
    width_out = out_rows * dp_count
    tower_hid = towers.shape[1] // TASKS

    outgoing, place, slot = pl.pallas_call(
        functools.partial(route_kernel, row_bits),
        out_shape=(
            jax.ShapeDtypeStruct((devices, capacity), I32),
            jax.ShapeDtypeStruct((tables_here, samples), I32),
            jax.ShapeDtypeStruct((tables_here, samples), I32),
        ),
        in_specs=[VMEM],
        out_specs=(VMEM, VMEM, VMEM),
        compiler_params=params(32),
        name="route",
    )(row_ids.T)
    codes = lax.all_to_all(
        outgoing.reshape(devices, 1, capacity), AXES, split_axis=0, concat_axis=0, tiled=True
    ).reshape(devices, capacity)

    shard = jnp.concatenate([expert_in, expert_out], axis=0).astype(LOW)
    shard = lax.all_to_all(shard, "mp", split_axis=1, concat_axis=2, tiled=True)
    gathered = lax.all_gather(shard, "dp", axis=0, tiled=False)
    expert_w = jnp.transpose(gathered, (2, 0, 1, 3))

    table_view = jnp.transpose(embeddings, (0, 2, 1))
    turned = pl.pallas_call(
        turn_kernel,
        grid=(pairs,),
        out_shape=jax.ShapeDtypeStruct((pairs, rows_dev, lanes), F32),
        in_specs=[pl.BlockSpec((2, d_emb, rows_dev), lambda p: (p, 0, 0))],
        out_specs=pl.BlockSpec((1, rows_dev, lanes), lambda p: (p, 0, 0)),
        compiler_params=params(32),
        name="turn",
    )(table_view)
    found = pl.pallas_call(
        functools.partial(find_kernel, mp_count, group_rows, code_bits),
        out_shape=jax.ShapeDtypeStruct((dp_count, mp_count, height, lanes), LOW),
        in_specs=[SMEM, VMEM],
        out_specs=VMEM,
        scratch_shapes=[pltpu.VMEM((height, lanes), F32)],
        compiler_params=params(32),
        name="find",
    )(codes, turned.reshape(pairs * rows_dev, lanes))
    returned = lax.all_to_all(
        found.reshape(devices, height, lanes), AXES, split_axis=0, concat_axis=0, tiled=True
    )
    embedded = pl.pallas_call(
        place_kernel,
        out_shape=jax.ShapeDtypeStruct((samples, tables_here * d_emb), LOW),
        in_specs=[SMEM, VMEM],
        out_specs=VMEM,
        scratch_shapes=[
            pltpu.VMEM((2 * slots, lanes), F32),
            pltpu.VMEM((tables_here // 2, samples, lanes), F32),
        ],
        compiler_params=params(32),
        name="place",
    )(place, returned.reshape(slots, lanes))

    first = EXPERTS * hid
    second = first + EXPERTS * width_out
    third = second + TASKS * EXPERTS
    fourth = third + TASKS * tower_hid
    inner_here = lax.dynamic_index_in_dim(
        biases[:first].reshape(mp_count, experts_here, 1, hid), mp_index, 0, keepdims=False
    )
    outer_here = lax.dynamic_index_in_dim(
        biases[first:second].reshape(mp_count, experts_here, 1, width_out),
        mp_index,
        0,
        keepdims=False,
    )
    gating_low = gating.T.astype(LOW)
    all_gates = TASKS * EXPERTS
    pack_rows = width_out

    def scratch(shape, kind=F32):
        return pltpu.VMEM(shape, kind)

    def sems(*shape):
        return pltpu.SemaphoreType.DMA(shape)

    blocks, hidden, slopes, output_rows, gate_logit_grad, small_grads, stat_parts = pl.pallas_call(
        ahead_kernel,
        out_shape=(
            jax.ShapeDtypeStruct((mp_count, samples, tables_here * d_emb), LOW),
            jax.ShapeDtypeStruct((experts_here, samples, hid), LOW),
            jax.ShapeDtypeStruct((experts_here, samples, hid), F32),
            jax.ShapeDtypeStruct((experts_here, samples, width_out), LOW),
            jax.ShapeDtypeStruct((own, all_gates), LOW),
            jax.ShapeDtypeStruct((pack_rows, TASKS * tower_hid + 128), LOW),
            jax.ShapeDtypeStruct((EXPERTS + TASKS + 2, 8, width_out), F32),
        ),
        in_specs=[SMEM] + [VMEM] * 9 + [SMEM] + [VMEM] * 2,
        out_specs=(VMEM,) * 7,
        scratch_shapes=[
            scratch((mp_count, experts_here, own, width_out), LOW),
            scratch((mp_count, experts_here, own, width_out), LOW),
            scratch((own, all_gates)),
            scratch((TASKS, own, width_out), LOW),
            scratch((TASKS, own, width_out)),
            scratch((own, all_gates)),
            scratch((EXPERTS, own, width_out), LOW),
            scratch((pack_rows, 128)),
            scratch((own, hid)),
            sems(mp_count, mp_count),
            sems(mp_count, mp_count),
            sems(mp_count),
            sems(mp_count),
            sems(mp_count),
            sems(mp_count),
        ],
        compiler_params=pltpu.CompilerParams(
            vmem_limit_bytes=56 * MIB, collective_id=0, has_side_effects=True
        ),
        name="ahead",
    )(
        lax.dynamic_slice_in_dim(counts, lax.axis_index("dp"), 1, 0),
        embedded,
        expert_w,
        inner_here,
        outer_here,
        gating_low,
        biases[second:third].reshape(1, all_gates),
        towers.astype(LOW),
        biases[third:fourth].reshape(TASKS, tower_hid),
        heads,
        biases[fourth:].reshape(1, TASKS),
        labels,
        label_mask,
    )
    in_out_rows = in_rows + out_rows
    embed_grad, grad_parts, inner_parts = pl.pallas_call(
        back_kernel,
        out_shape=(
            jax.ShapeDtypeStruct((samples, tables_here * d_emb), F32),
            jax.ShapeDtypeStruct(
                (dp_count, mp_count, experts_here * in_out_rows, hid // mp_count), LOW
            ),
            jax.ShapeDtypeStruct((experts_here, 8, hid), F32),
        ),
        in_specs=[VMEM] * 7,
        out_specs=(VMEM,) * 3,
        scratch_shapes=[
            scratch((experts_here, samples, hid), LOW),
            scratch((mp_count, samples, tables_here * d_emb), LOW),
            scratch((mp_count, samples, tables_here * d_emb), LOW),
            sems(mp_count, mp_count),
            sems(mp_count, mp_count),
        ],
        compiler_params=pltpu.CompilerParams(
            vmem_limit_bytes=56 * MIB, collective_id=1, has_side_effects=True
        ),
        name="back",
    )(output_rows, hidden, slopes, blocks, expert_w, gate_logit_grad, gating_low)

    back_rows = pl.pallas_call(
        send_kernel,
        out_shape=jax.ShapeDtypeStruct((slots, lanes), LOW),
        in_specs=[SMEM, VMEM],
        out_specs=VMEM,
        scratch_shapes=[
            pltpu.VMEM((tables_here // 2, 2 * samples, lanes), F32),
            pltpu.VMEM((2 * slots, lanes), F32),
        ],
        compiler_params=params(32),
        name="send",
    )(slot, embed_grad)
    arrived = lax.all_to_all(
        back_rows.reshape(devices, height, lanes), AXES, split_axis=0, concat_axis=0, tiled=True
    )
    table_grad, table_sq = pl.pallas_call(
        functools.partial(add_kernel, mp_count, code_bits),
        out_shape=(
            jax.ShapeDtypeStruct((pairs * rows_dev, lanes), F32),
            jax.ShapeDtypeStruct((8, lanes), F32),
        ),
        in_specs=[SMEM, VMEM],
        out_specs=(pl.BlockSpec(memory_space=pl.ANY), VMEM),
        scratch_shapes=[
            pltpu.VMEM((4 * slots + 8, lanes), F32),
            pltpu.SemaphoreType.DMA((mp_count,)),
        ]
        + [pltpu.VMEM((group_rows, lanes), F32)] * mp_count,
        compiler_params=params(60),
        name="add",
    )(codes, arrived.reshape(slots, lanes))

    def exchange_all(parts):
        return lax.all_to_all(parts, AXES, split_axis=0, concat_axis=0, tiled=True)

    small_grads = small_grads.reshape(devices, pack_rows // devices, -1)
    share = jnp.sum(exchange_all(small_grads).astype(F32), axis=0)
    share_sq = jnp.sum(share * share)
    whole = exchange_all(jnp.broadcast_to(share.astype(LOW)[None], small_grads.shape))
    whole = whole.reshape(pack_rows, -1)
    towers_sum = whole[:, : TASKS * tower_hid].astype(F32)
    packed = whole[:, TASKS * tower_hid :].astype(F32)
    blocks_x = features // 128
    heads_at = blocks_x * all_gates
    tower_at = heads_at + TASKS * tower_hid // 128
    outer_at = tower_at + TASKS * tower_hid // 128
    rest_at = outer_at + EXPERTS * width_out // 128
    gating_sum = packed[:heads_at].reshape(blocks_x, all_gates, 128).transpose(1, 0, 2)
    gating_sum = gating_sum.reshape(all_gates, features).T
    heads_sum = packed[heads_at:tower_at].reshape(TASKS, tower_hid)

    grad_parts = exchange_all(
        grad_parts.reshape(devices, experts_here * in_out_rows, hid // mp_count)
    )
    grad_sum = jnp.sum(
        grad_parts.reshape(dp_count, mp_count, experts_here, in_out_rows, -1).astype(F32), 0
    )
    grad_sum = grad_sum.reshape(EXPERTS, in_out_rows, -1).transpose(1, 0, 2)
    in_sum, out_sum = grad_sum[:in_rows], grad_sum[in_rows:]

    squares = jnp.sum(table_sq) + jnp.sum(grad_sum * grad_sum) + share_sq
    stat_end = EXPERTS + TASKS
    stat_sums = jnp.sum(stat_parts[: stat_end + 1], axis=(1, 2))
    scalars = jnp.concatenate(
        [stat_parts[stat_end + 1, 0, :2], stat_sums, squares[None]]
    )
    scalars = jnp.pad(scalars, (0, 128 - scalars.size))[None]
    final = jnp.concatenate(
        [inner_parts[:, 0, :].reshape(-1, 128), scalars], axis=0
    )
    final = exchange_all(jnp.broadcast_to(final[None], (devices,) + final.shape))
    sums = jnp.sum(final[:, -1, :], axis=0)
    inner_sum = jnp.sum(final[:, :-1, :].reshape(dp_count, -1), axis=0)
    bias_sum = jnp.concatenate(
        [
            inner_sum,
            packed[outer_at:rest_at].reshape(-1),
            packed[rest_at, :all_gates],
            packed[tower_at:outer_at].reshape(-1),
            packed[rest_at + 1, :TASKS],
        ]
    )
    weight_total = sums[1]
    grad_norm = jnp.sqrt(sums[stat_end + 3] + jnp.sum(inner_sum * inner_sum)) / weight_total
    factor = jnp.minimum(1.0, clip_max / grad_norm) / weight_total

    table_spec = pl.BlockSpec((2, d_emb, rows_dev // 2), lambda p, c: (p, 0, c))
    embed_out = pl.pallas_call(
        table_kernel,
        grid=(pairs, 2),
        out_shape=(jax.ShapeDtypeStruct(table_view.shape, F32),) * 3,
        in_specs=[
            SMEM,
            table_spec,
            table_spec,
            table_spec,
            pl.BlockSpec((1, rows_dev // 2, lanes), lambda p, c: (p, c, 0)),
        ],
        out_specs=(table_spec,) * 3,
        compiler_params=params(48),
        name="tables",
    )(
        factor.reshape(1),
        table_view,
        jnp.transpose(embed_first, (0, 2, 1)),
        jnp.transpose(embed_second, (0, 2, 1)),
        table_grad.reshape(pairs, rows_dev, lanes),
    )
    embed_out = [jnp.transpose(value, (0, 2, 1)) for value in embed_out]
    in_out = adamw(expert_in, in_first, in_second, in_sum * factor, rate_dense)
    out_out = adamw(expert_out, out_first, out_second, out_sum * factor, rate_dense)
    gating_out = adamw(gating, gating_first, gating_second, gating_sum * factor, rate_dense)
    towers_out = adamw(towers, towers_first, towers_second, towers_sum * factor, rate_dense)
    heads_out = adamw(heads, heads_first, heads_second, heads_sum * factor, rate_dense)
    biases_out = adamw(biases, biases_first, biases_second, bias_sum * factor, rate_dense)
    n_valid = jnp.sum(counts).astype(F32)
    widths = jnp.concatenate(
        [jnp.full((1,), features, F32), jnp.full((EXPERTS + TASKS,), width_out, F32)]
    )
    mean_sq = jnp.concatenate([sums[stat_end + 2][None], sums[2 : stat_end + 2]])
    stats = jnp.sqrt(mean_sq / (n_valid * widths) + stat_eps)
    loss = jnp.stack([sums[0], weight_total])
    return (
        *embed_out,
        *in_out,
        in_out[0].astype(LOW),
        *out_out,
        out_out[0].astype(LOW),
        *gating_out,
        *towers_out,
        *heads_out,
        *biases_out,
        grad_norm.reshape(1),
        loss,
        stats,
    )


def solution(mesh):
    rows = P(None, AXES, None)
    expert = P("dp", None, "mp")
    sample = P(AXES, None)
    placed = (P("dp", "mp"), P(), sample, sample) + (rows,) * 3 + (expert,) * 6 + (P(),) * 12
    results = (rows,) * 3 + (expert,) * 8 + (P(),) * 15
    return jax.shard_map(body, mesh=mesh, in_specs=placed, out_specs=results, check_vma=False)
```

```python
import functools
import math

import jax
import jax.numpy as jnp
from jax import lax
from jax.experimental import pallas as pl
from jax.experimental.pallas import tpu as pltpu
from jax.sharding import PartitionSpec as P

EXPERTS = 8
TASKS = 5
STEP = 3

HIGH = lax.Precision.HIGHEST
beta_one = 0.5
beta_two = 0.5
adam_eps = 1e-08
decay = 0.01
clip_max = 0.002
rate_table = 0.5
rate_dense = 0.02
stat_eps = 1e-06

LOW = jnp.bfloat16
F32 = jnp.float32
I32 = jnp.int32
MIB = 1024 * 1024
AXES = ("dp", "mp")


def params(mib):
    return pltpu.CompilerParams(vmem_limit_bytes=mib * MIB)


VMEM = pl.BlockSpec(memory_space=pltpu.VMEM)
SMEM = pl.BlockSpec(memory_space=pltpu.SMEM)


def adamw(weight, first, second, gradient, rate):
    first_next = beta_one * first + (1.0 - beta_one) * gradient
    second_next = beta_two * second + (1.0 - beta_two) * gradient * gradient
    corrected = first_next / (1.0 - beta_one**STEP)
    scaled = jnp.sqrt(second_next / (1.0 - beta_two**STEP))
    return (
        weight - rate * (corrected / (scaled + adam_eps) + decay * weight),
        first_next,
        second_next,
    )


def route_kernel(row_bits, ids_ref, out_ref, place_ref, slot_ref, from_ref):
    devices, _, capacity = out_ref.shape
    tables, samples = ids_ref.shape
    rows_dev = 1 << row_bits
    halves = devices * capacity // 2
    width = 256
    upper = (
        lax.broadcasted_iota(I32, (width, width), 0) <= lax.broadcasted_iota(I32, (width, width), 1)
    ).astype(LOW)
    owners = lax.broadcasted_iota(I32, (devices, width), 0)
    slots = lax.broadcasted_iota(I32, (capacity, width), 0)
    carry = jnp.zeros((devices, 1), F32)
    total = jnp.zeros((2 * devices, capacity), F32)
    for table in range(tables):
        parity = table % 2
        for part in range(samples // width):
            cols = pl.ds(part * width, width)
            ids = ids_ref[pl.ds(table, 1), cols]
            owner = ids >> row_bits
            code = table * rows_dev + (ids & (rows_dev - 1)) + 1
            onehot = (owner == owners).astype(F32)
            counted = jnp.dot(onehot.astype(LOW), upper, preferred_element_type=F32) + carry
            rank = jnp.sum(onehot * counted, axis=0, keepdims=True).astype(I32) - 1
            carry = counted[:, width - 1 :]
            at_slot = (rank == slots).astype(LOW)
            high = (code >> 7).astype(F32)
            low = (code & 127).astype(F32)
            pieces = jnp.concatenate([onehot * high, onehot * low], axis=0).astype(LOW)
            total += lax.dot_general(
                pieces, at_slot, (((1,), (1,)), ((), ())), preferred_element_type=F32
            )
            row = owner * (capacity // 2) + (rank >> 1)
            half = rank & 1
            place_ref[pl.ds(table, 1), cols] = (half ^ parity) * halves + row
            slot_ref[pl.ds(table, 1), cols] = half * halves + row
            sample = lax.broadcasted_iota(I32, (1, width), 1) + part * width
            from_ref[pl.ds(table, 1), cols] = (half ^ parity) * samples + sample
    codes = (total[:devices] * 128.0 + total[devices:]).astype(I32)
    first = lax.broadcasted_iota(I32, (devices, capacity), 1) == 0
    counted = jnp.where(first, carry * 65536.0, 0.0).astype(I32)
    out_ref[...] = (codes + counted).reshape(devices, 1, capacity)


def left_lanes(shape):
    return lax.broadcasted_iota(I32, shape, len(shape) - 1) < 64


def find_kernel(groups, at_ref, counts_ref, table_ref, out_ref, turned_ref, rows_ref):
    blocks, _, height, lanes = out_ref.shape
    tables, width, rows_dev = table_ref.shape
    group = pl.program_id(0)
    left = left_lanes((1, lanes))
    part = 512

    def turn_step(step, _):
        table = lax.div(step, rows_dev // part)
        first = pl.multiple_of(lax.rem(step, rows_dev // part) * part, part)
        columns = table_ref[table, :, pl.ds(first, part)]
        there = pl.ds(pl.multiple_of(step * part, part), part)
        turned_ref[there, :] = jnp.concatenate([columns, columns], axis=0).T
        return 0

    lax.fori_loop(0, tables * (rows_dev // part), turn_step, 0)

    def block_step(block, _):
        source = block * groups + group
        base = source * 2 * height

        def step(outer, _):
            got = []
            for inner in range(8):
                at = outer * 8 + inner
                even = turned_ref[pl.ds(at_ref[base + 2 * at], 1), :]
                odd = turned_ref[pl.ds(at_ref[base + 2 * at + 1], 1), :]
                got.append((at, jnp.where(left, even, odd)))
            for at, row in got:
                rows_ref[pl.ds(at, 1), :] = row
            return 0

        lax.fori_loop(0, (counts_ref[source] + 15) // 16, step, 0)
        out_ref[block, 0] = rows_ref[...].astype(LOW)
        return 0

    lax.fori_loop(0, blocks, block_step, 0)


def place_kernel(place_ref, rows_ref, out_ref, both_ref, flat_ref):
    count, lanes = rows_ref.shape
    samples = out_ref.shape[0]
    tables = place_ref.shape[0] // samples
    rows = rows_ref[...].astype(F32)
    both_ref[pl.ds(0, count), :] = rows
    both_ref[pl.ds(count, count), :] = pltpu.roll(rows, 64, 1)
    left = left_lanes((1, lanes))

    def step(outer, _):
        got = []
        for inner in range(8):
            sample = outer * 8 + inner
            for pair in range(tables // 2):
                even = both_ref[pl.ds(place_ref[2 * pair * samples + sample], 1), :]
                odd = both_ref[pl.ds(place_ref[(2 * pair + 1) * samples + sample], 1), :]
                got.append((pair, sample, jnp.where(left, even, odd)))
        for pair, sample, row in got:
            flat_ref[pair, pl.ds(sample, 1), :] = row
        return 0

    lax.fori_loop(0, samples // 8, step, 0)
    for pair in range(tables // 2):
        out_ref[:, pair * lanes : (pair + 1) * lanes] = flat_ref[pair].astype(LOW)


def send_kernel(slot_ref, from_ref, grad_ref, out_ref, both_ref, rows_ref):
    count, lanes = out_ref.shape
    samples = grad_ref.shape[0]
    tables = slot_ref.shape[0] // samples
    for pair in range(tables // 2):
        rows = grad_ref[:, pair * lanes : (pair + 1) * lanes]
        both_ref[pair, pl.ds(0, samples), :] = rows
        both_ref[pair, pl.ds(samples, samples), :] = pltpu.roll(rows, 64, 1)

    def step(outer, _):
        got = []
        for inner in range(8):
            sample = outer * 8 + inner
            for table in range(tables):
                row = both_ref[table // 2, pl.ds(from_ref[table * samples + sample], 1), :]
                got.append((slot_ref[table * samples + sample], row))
        for slot, row in got:
            rows_ref[pl.ds(slot, 1), :] = row
        return 0

    lax.fori_loop(0, samples // 8, step, 0)
    left = left_lanes((count, lanes))
    out_ref[...] = jnp.where(
        left, rows_ref[pl.ds(0, count), :], rows_ref[pl.ds(count, count), :]
    ).astype(LOW)


def swap_kernel(rows_ref, share_ref, out_ref, shares_ref, r_out, r_in, s_out, s_in):
    devices = rows_ref.shape[0]
    groups = share_ref.shape[0]
    peers = lax.axis_size("mp")
    dp, mp = lax.axis_index("dp"), lax.axis_index("mp")
    mine = lax.div(dp, 2) * (peers // 2) + lax.div(mp, 2)
    me = dp * peers + mp
    barrier = pltpu.get_barrier_semaphore()

    def place_of(device):
        return {"dp": lax.div(device, peers), "mp": lax.rem(device, peers)}

    def greet(step, _):
        target = lax.rem(me + step, devices)
        pl.semaphore_signal(barrier, inc=1, device_id=place_of(target), device_id_type=MESH)
        return 0

    lax.fori_loop(1, devices, greet, 0)
    pl.semaphore_wait(barrier, devices - 1)

    def r_copy(step):
        target = lax.rem(me + step, devices)
        return pltpu.make_async_remote_copy(
            rows_ref.at[target],
            out_ref.at[me],
            r_out.at[step],
            r_in.at[step],
            device_id=place_of(target),
            device_id_type=MESH,
        )

    def s_copy(step):
        target = lax.rem(mine + step, groups)
        to_dp = lax.div(target, peers // 2) * 2 + lax.rem(dp, 2)
        to_mp = lax.rem(target, peers // 2) * 2 + lax.rem(mp, 2)
        return pltpu.make_async_remote_copy(
            share_ref.at[target],
            shares_ref.at[mine],
            s_out.at[step],
            s_in.at[step],
            device_id={"dp": to_dp, "mp": to_mp},
            device_id_type=MESH,
        )

    def loop(first, copies, act):
        def step(at, _):
            act(copies(at))
            return 0

        lax.fori_loop(1, first, step, 0)

    loop(devices, r_copy, lambda copy: copy.start())
    loop(groups, s_copy, lambda copy: copy.start())
    out_ref[me] = rows_ref[me]
    shares_ref[mine] = share_ref[mine]
    loop(groups, s_copy, lambda copy: copy.wait())
    loop(devices, r_copy, lambda copy: copy.wait())


def add_kernel(
    groups, at_ref, part_at_ref, counts_ref, rows_ref, out_ref, square_ref, parts_ref, sems, *sums
):
    count, lanes = rows_ref.shape
    sources = counts_ref.shape[0]
    height = count // sources
    table_rows = sums[0].shape[0]
    left = left_lanes((count, lanes))
    rows = rows_ref[...].astype(F32)
    turned = pltpu.roll(rows, 64, 1)
    parts_ref[pl.ds(0, count), :] = jnp.where(left, rows, 0.0)
    parts_ref[pl.ds(count, count), :] = jnp.where(left, 0.0, turned)
    parts_ref[pl.ds(2 * count, count), :] = jnp.where(left, turned, 0.0)
    parts_ref[pl.ds(3 * count, count), :] = jnp.where(left, 0.0, rows)
    parts_ref[pl.ds(4 * count, 8), :] = jnp.zeros((8, lanes), F32)

    def clear(at, _):
        for table in sums:
            table[pl.ds(pl.multiple_of(at * 64, 64), 64), :] = jnp.zeros((64, lanes), F32)
        return 0

    lax.fori_loop(0, table_rows // 64, clear, 0)

    def block_step(block, _):
        most = counts_ref[block * groups]
        for group in range(1, groups):
            most = jnp.maximum(most, counts_ref[block * groups + group])

        def step(outer, _):
            for inner in range(4):
                got = []
                for group in range(groups):
                    at = (block * groups + group) * 2 * height + outer * 4 + inner
                    here = pl.ds(at_ref[at], 1)
                    part = pl.ds(part_at_ref[at], 1)
                    got.append((here, sums[group][here, :] + parts_ref[part, :]))
                for group, (here, row) in enumerate(got):
                    sums[group][here, :] = row
            return 0

        lax.fori_loop(0, (most + 3) // 4, step, 0)
        return 0

    lax.fori_loop(0, sources // groups, block_step, 0)
    copies = [
        pltpu.make_async_copy(
            sums[group], out_ref.at[pl.ds(group * table_rows, table_rows)], sems.at[group]
        )
        for group in range(groups)
    ]
    for copy in copies:
        copy.start()

    def square(at, total):
        for table in sums:
            rows = table[pl.ds(pl.multiple_of(at * 64, 64), 64), :]
            total = total + jnp.sum((rows * rows).reshape(8, 8, lanes), axis=0)
        return total

    square_ref[...] = lax.fori_loop(0, table_rows // 64, square, jnp.zeros((8, lanes), F32))
    for copy in copies:
        copy.wait()


def gelu_parts(value):
    scale = math.sqrt(2.0 / math.pi)
    square = value * value
    bend = jnp.tanh(scale * value * (1.0 + 0.044715 * square))
    half = 0.5 * (1.0 + bend)
    slope = half + 0.5 * value * (1.0 - bend * bend) * (scale * (1.0 + 3 * 0.044715 * square))
    return value * half, slope


def dot(a, b, axes=((1,), (0,)), precision=None):
    return lax.dot_general(
        a, b, (axes, ((), ())), preferred_element_type=F32, precision=precision
    )


NT = ((1,), (1,))
TN = ((0,), (0,))
MESH = pl.DeviceIdType.MESH


def meet(peers, partner=None):
    me = lax.axis_index("mp")
    barrier = pltpu.get_barrier_semaphore()
    if partner is not None:
        pl.semaphore_signal(
            barrier, inc=1, device_id={"dp": partner, "mp": me}, device_id_type=MESH
        )
    for step in range(1, peers):
        pl.semaphore_signal(
            barrier, inc=1, device_id={"mp": lax.rem(me + step, peers)}, device_id_type=MESH
        )
    pl.semaphore_wait(barrier, peers - 1 + (partner is not None))
    return me


def ask_kernel(codes_ref, shard_ref, out_ref, full_ref, c_out, c_in, w_out, w_in):
    devices = codes_ref.shape[0]
    here, _, full = full_ref.shape
    width = shard_ref.shape[2]
    peers = full // width
    mp = lax.axis_index("mp")
    me = lax.axis_index("dp") * peers + mp
    barrier = pltpu.get_barrier_semaphore()

    def place_of(device):
        return {"dp": lax.div(device, peers), "mp": lax.rem(device, peers)}

    def greet(step, _):
        target = lax.rem(me + step, devices)
        pl.semaphore_signal(barrier, inc=1, device_id=place_of(target), device_id_type=MESH)
        return 0

    lax.fori_loop(1, devices, greet, 0)
    columns = pl.ds(pl.multiple_of(mp * width, width), width)
    full_ref[:, :, columns] = shard_ref[pl.ds(mp * here, here)]
    out_ref[me] = codes_ref[me]
    pl.semaphore_wait(barrier, devices - 1)

    def c_copy(step):
        target = lax.rem(me + step, devices)
        return pltpu.make_async_remote_copy(
            codes_ref.at[target],
            out_ref.at[me],
            c_out.at[step],
            c_in.at[step],
            device_id=place_of(target),
            device_id_type=MESH,
        )

    def w_copy(step):
        target = lax.rem(mp + step, peers)
        return pltpu.make_async_remote_copy(
            shard_ref.at[pl.ds(target * here, here)],
            full_ref.at[:, :, columns],
            w_out.at[step],
            w_in.at[step],
            device_id={"mp": target},
            device_id_type=MESH,
        )

    def start(step, _):
        c_copy(step).start()
        return 0

    def finish(step, _):
        c_copy(step).wait()
        return 0

    lax.fori_loop(1, devices, start, 0)
    for step in range(1, peers):
        w_copy(step).start()
    lax.fori_loop(1, devices, finish, 0)
    for step in range(1, peers):
        w_copy(step).wait()


def ahead_kernel(
    count_ref,
    x_ref,
    w_ref,
    b1_ref,
    b2_ref,
    wg_ref,
    bg_ref,
    w3_ref,
    tb1_ref,
    heads_ref,
    tb2_ref,
    labels_ref,
    mask_ref,
    blocks_ref,
    hid_ref,
    slope_ref,
    dy_ref,
    dgl_ref,
    small_ref,
    stats_ref,
    y_send,
    y_ref,
    gates_ref,
    mixb_ref,
    dmix_ref,
    dg_ref,
    dy_send,
    pack_ref,
    act_ref,
    x_out,
    x_in,
    y_out,
    y_in,
    d_out,
    d_in,
):
    peers, samples, width = blocks_ref.shape
    here = hid_ref.shape[0]
    out_width = y_ref.shape[3]
    own = y_ref.shape[2]
    experts = peers * here
    tasks, tower_hid = heads_ref.shape
    shards, hid = w_ref.shape[0], w_ref.shape[3]
    in_rows = peers * width // shards
    me = meet(peers)

    def other(step):
        return lax.rem(me + step, peers)

    def x_copy(turn, step):
        target = other(step)
        rows = pl.ds(pl.multiple_of(lax.rem(target + turn + 1, peers) * own, own), own)
        return pltpu.make_async_remote_copy(
            x_ref.at[rows],
            blocks_ref.at[me, rows],
            x_out.at[turn, step],
            x_in.at[turn, step],
            device_id={"mp": target},
            device_id_type=MESH,
        )

    def y_copy(turn):
        return pltpu.make_async_remote_copy(
            y_send.at[turn],
            y_ref.at[me],
            y_out.at[turn],
            y_in.at[turn],
            device_id={"mp": other(turn + 1)},
            device_id_type=MESH,
        )

    def d_copy(step):
        target = other(step)
        return pltpu.make_async_remote_copy(
            dy_send.at[pl.ds(target * here, here)],
            dy_ref.at[:, pl.ds(pl.multiple_of(me * own, own), own), :],
            d_out.at[step],
            d_in.at[step],
            device_id={"mp": target},
            device_id_type=MESH,
        )

    for turn in range(peers):
        for step in range(1, peers):
            x_copy(turn, step).start()
    blocks_ref[me] = x_ref[...]
    limit = count_ref[0]

    def expert_step(turn, _):
        for step in range(1, peers):
            x_copy(turn, step).wait_recv()
        chunk = lax.rem(me + turn + 1, peers)
        rows = pl.ds(pl.multiple_of(chunk * own, own), own)
        x = jnp.concatenate([blocks_ref[block, rows] for block in range(peers)], axis=1)
        for e in range(here):
            w_in = w_ref[:, e, :in_rows, :].reshape(peers * width, hid)
            act_ref[...] = dot(x, w_in) + b1_ref[e]

            def gelu_step(tile, _):
                at = pl.multiple_of(tile * 32, 32)
                value, slope = gelu_parts(act_ref[pl.ds(at, 32), :])
                there = pl.ds(pl.multiple_of(chunk * own + at, 32), 32)
                hid_ref[e, there, :] = value.astype(LOW)
                slope_ref[e, there, :] = slope
                return 0

            lax.fori_loop(0, own // 32, gelu_step, 0)
            w_out = w_ref[:, e, in_rows:, :].reshape(out_width, hid)
            y_send[turn, e] = (dot(hid_ref[e, rows, :], w_out, NT) + b2_ref[e]).astype(LOW)

        @pl.when(turn < peers - 1)
        def _():
            y_copy(turn).start()

        return 0

    lax.fori_loop(0, peers, expert_step, 0)
    y_ref[me] = y_send[peers - 1]

    own_rows = pl.ds(pl.multiple_of(me * own, own), own)
    x_own = jnp.concatenate([blocks_ref[block, own_rows] for block in range(peers)], axis=1)
    logits = dot(x_own, wg_ref[...], NT) + bg_ref[...]
    for k in range(tasks):
        part = logits[:, k * experts : (k + 1) * experts]
        part = jnp.exp(part - jnp.max(part, axis=1, keepdims=True))
        gates_ref[:, k * experts : (k + 1) * experts] = part / jnp.sum(part, axis=1, keepdims=True)

    stats_ref[...] = jnp.zeros_like(stats_ref)

    def square_step(tile, total):
        at = pl.multiple_of(tile * 64, 64)
        valid = (lax.broadcasted_iota(I32, (64, 1), 0) + at) < limit
        part = jnp.where(valid, x_ref[pl.ds(at, 64), :].astype(F32), 0.0)
        return total + jnp.sum((part * part).reshape(8, 8, width), axis=0)

    x_square = lax.fori_loop(0, samples // 64, square_step, jnp.zeros((8, width), F32))
    stats_ref[experts + tasks, :, :width] = x_square
    for turn in range(peers - 1):
        y_copy(turn).wait_recv()

    tile_rows = 16

    def tile_of(tile):
        at = pl.multiple_of(tile * tile_rows, tile_rows)
        return at, pl.ds(at, tile_rows)

    def mix_step(tile, _):
        at, rows = tile_of(tile)
        valid = (lax.broadcasted_iota(I32, (tile_rows, 1), 0) + (at + me * own)) < limit
        gates = gates_ref[rows, :]
        mixed = [None] * tasks
        for e in range(experts):
            y = y_ref[e // here, e % here, rows, :].astype(F32)
            square = jnp.where(valid, y * y, 0.0)
            stats_ref[e] += square[:8] + square[8:]
            for k in range(tasks):
                term = gates[:, k * experts + e : k * experts + e + 1] * y
                mixed[k] = term if e == 0 else mixed[k] + term
        for k in range(tasks):
            square = jnp.where(valid, mixed[k] * mixed[k], 0.0)
            stats_ref[experts + k] += square[:8] + square[8:]
            mixb_ref[k, rows, :] = mixed[k].astype(LOW)
        return 0

    lax.fori_loop(0, own // tile_rows, mix_step, 0)

    pack_ref[...] = jnp.zeros_like(pack_ref)
    blocks_x = peers * width // 128
    heads_at = blocks_x * tasks * experts
    tower_at = heads_at + tasks * tower_hid // 128
    outer_at = tower_at + tasks * tower_hid // 128
    rest_at = outer_at + experts * out_width // 128
    loss = jnp.zeros((1, 1), F32)
    weight_sum = jnp.zeros((1, 1), F32)
    row_id = lax.broadcasted_iota(I32, (own, 1), 0) + me * own
    for k in range(tasks):
        cols = slice(k * tower_hid, (k + 1) * tower_hid)
        z, slope = gelu_parts(dot(mixb_ref[k], w3_ref[:, cols]) + tb1_ref[k : k + 1, :])
        head = heads_ref[k : k + 1, :]
        logit = jnp.sum(z * head, axis=1, keepdims=True) + tb2_ref[0, k]
        small = jnp.exp(-jnp.abs(logit))
        label = labels_ref[:, k : k + 1].astype(F32)
        weight = jnp.where(row_id < limit, mask_ref[:, k : k + 1].astype(F32), 0.0)
        soft = jnp.maximum(logit, 0.0) + jnp.log1p(small)
        loss += jnp.sum(weight * (soft - label * logit), axis=0, keepdims=True)
        weight_sum += jnp.sum(weight, axis=0, keepdims=True)
        chance = jnp.where(logit >= 0.0, 1.0, small) / (1.0 + small)
        dl = weight * (chance - label)
        g_head = jnp.sum(dl * z, axis=0, keepdims=True)
        dz = (dl * head * slope).astype(LOW)
        g_bias = jnp.sum(dz.astype(F32), axis=0, keepdims=True)
        for part in range(tower_hid // 128):
            lane = slice(part * 128, (part + 1) * 128)
            at = k * (tower_hid // 128) + part
            pack_ref[heads_at + at : heads_at + at + 1, :] = g_head[:, lane]
            pack_ref[tower_at + at : tower_at + at + 1, :] = g_bias[:, lane]
        pack_ref[rest_at + 1 : rest_at + 2, k : k + 1] = jnp.sum(dl, axis=0, keepdims=True)
        dmix_ref[k] = dot(dz, w3_ref[:, cols], NT)
        small_ref[:, cols] = dot(mixb_ref[k], dz, TN).astype(LOW)
    stats_ref[experts + tasks + 1, :1, :1] = loss
    stats_ref[experts + tasks + 1, :1, 1:2] = weight_sum

    def dy_step(tile, _):
        at, rows = tile_of(tile)
        gates = gates_ref[rows, :]
        dmix = [dmix_ref[k, rows, :] for k in range(tasks)]
        for e in range(experts):
            total = None
            for k in range(tasks):
                term = gates[:, k * experts + e : k * experts + e + 1] * dmix[k]
                total = term if k == 0 else total + term
            dy_send[e, rows, :] = total.astype(LOW)
        return 0

    lax.fori_loop(0, own // tile_rows, dy_step, 0)
    for step in range(1, peers):
        d_copy(step).start()
    dy_ref[:, own_rows, :] = dy_send[pl.ds(me * here, here)]
    ones = jnp.ones((8, own), LOW)
    for e in range(experts):
        g_outer = dot(ones, dy_send[e])
        for part in range(out_width // 128):
            at = outer_at + e * (out_width // 128) + part
            pack_ref[at : at + 1, :] = g_outer[:1, part * 128 : (part + 1) * 128]

    lane = lax.broadcasted_iota(I32, (tile_rows, tasks * experts), 1)

    def dg_step(tile, _):
        at, rows = tile_of(tile)
        dmix = [dmix_ref[k, rows, :] for k in range(tasks)]
        found = jnp.zeros((tile_rows, tasks * experts), F32)
        for e in range(experts):
            y = y_ref[e // here, e % here, rows, :].astype(F32)
            for k in range(tasks):
                value = jnp.sum(dmix[k] * y, axis=1, keepdims=True)
                found = jnp.where(lane == k * experts + e, value, found)
        dg_ref[rows, :] = found
        return 0

    lax.fori_loop(0, own // tile_rows, dg_step, 0)
    gates = gates_ref[...]
    dg = dg_ref[...]
    flat = (tasks * experts, tasks * experts)
    same = lax.broadcasted_iota(I32, flat, 0) // experts == lax.broadcasted_iota(I32, flat, 1) // experts
    mean = dot(gates * dg, same.astype(F32), precision=HIGH)
    dgl = (gates * (dg - mean)).astype(LOW)
    dgl_ref[...] = dgl
    pack_ref[rest_at : rest_at + 1, : tasks * experts] = jnp.sum(
        dgl.astype(F32), axis=0, keepdims=True
    )
    g_gating = dot(dgl, x_own, TN)
    for part in range(blocks_x):
        at = part * tasks * experts
        pack_ref[at : at + tasks * experts, :] = g_gating[:, part * 128 : (part + 1) * 128]
    small_ref[:, tasks * tower_hid :] = pack_ref[...].astype(LOW)

    for turn in range(peers):
        for step in range(1, peers):
            x_copy(turn, step).wait_send()
    for turn in range(peers - 1):
        y_copy(turn).wait_send()
    for step in range(1, peers):
        d_copy(step).wait()


def back_kernel(
    dy_ref,
    hid_ref,
    slope_ref,
    blocks_ref,
    w_ref,
    dgl_ref,
    wg_ref,
    small_ref,
    dx_ref,
    parts_ref,
    b1_ref,
    share_ref,
    dpre_ref,
    dx_send,
    dx_recv,
    core_recv,
    pair_send,
    pair_recv,
    x_out,
    x_in,
    s_out,
    s_in,
):
    peers, samples, width = blocks_ref.shape
    here, _, out_width = dy_ref.shape
    own = samples // peers
    hid = hid_ref.shape[2]
    shards, rows_both = w_ref.shape[0], w_ref.shape[2]
    in_rows = peers * width // shards
    out_rows = rows_both - in_rows
    features = peers * width
    dp = lax.axis_index("dp")
    dp_side = lax.rem(dp, 2)
    pair = dp + 1 - 2 * dp_side
    me = meet(peers, pair)
    side = lax.rem(me, 2)
    near = me + 1 - 2 * side

    def chunk_rows(turn):
        return pl.ds(pl.multiple_of(lax.rem(me + turn, peers) * own, own), own)

    def x_copy(turn, step):
        target = lax.rem(me + step, peers)
        rows = chunk_rows(turn)
        return pltpu.make_async_remote_copy(
            dx_send.at[target, rows],
            dx_recv.at[me, rows],
            x_out.at[turn, step],
            x_in.at[turn, step],
            device_id={"mp": target},
            device_id_type=MESH,
        )

    share = share_ref.shape[0]

    def share_rows(part):
        return pl.ds(pl.multiple_of(part * share, share), share)

    def core_copy():
        return pltpu.make_async_remote_copy(
            small_ref.at[pl.ds(pl.multiple_of((1 - side) * 2 * share, share), 2 * share)],
            core_recv,
            s_out.at[0],
            s_in.at[0],
            device_id={"dp": dp, "mp": near},
            device_id_type=MESH,
        )

    def pair_copy():
        return pltpu.make_async_remote_copy(
            pair_send,
            pair_recv,
            s_out.at[1],
            s_in.at[1],
            device_id={"dp": pair, "mp": me},
            device_id_type=MESH,
        )

    def core_sum(part):
        mine = small_ref[share_rows(side * 2 + part), :].astype(F32)
        return mine + core_recv[share_rows(part), :].astype(F32)

    core_copy().start()
    b1_ref[...] = jnp.zeros_like(b1_ref)

    def chunk_step(turn, _):
        rows = chunk_rows(turn)
        mine = jnp.where(turn == 0, 1.0, 0.0)
        gate = (dgl_ref[...].astype(F32) * mine).astype(LOW)
        total = dot(gate, wg_ref[...])
        for e in range(here):
            w_out = w_ref[:, e, in_rows:, :].reshape(out_width, hid)
            dpre = (dot(dy_ref[e, rows, :], w_out) * slope_ref[e, rows, :]).astype(LOW)
            dpre_ref[e, rows, :] = dpre
            b1_ref[e] += dot(jnp.ones((8, own), LOW), dpre)
            w_in = w_ref[:, e, :in_rows, :].reshape(features, hid)
            total += dot(dpre, w_in, NT)
        for target in range(peers):
            dx_send[target, rows] = total[:, target * width : (target + 1) * width].astype(LOW)
        for step in range(1, peers):
            x_copy(turn, step).start()
        return 0

    lax.fori_loop(0, peers, chunk_step, 0)

    core_copy().wait()
    pair_send[...] = core_sum(1 - dp_side).astype(LOW)
    pair_copy().start()

    lanes = parts_ref.shape[4]
    blocks_in = width // 128
    per_in = 128 // in_rows
    per_out = 128 // out_rows
    for e in range(here):

        def in_step(block, _):
            cols = pl.ds(pl.multiple_of(lax.rem(block, blocks_in) * 128, 128), 128)
            x = blocks_ref[lax.div(block, blocks_in), :, cols]
            value = dot(x, dpre_ref[e], TN).astype(LOW)
            for shard in range(per_in):
                for target in range(peers):
                    to = block * per_in + shard
                    away = lax.rem(to + dp, 2)
                    parts_ref[
                        away, lax.div(to, 2), target, e * rows_both : e * rows_both + in_rows, :
                    ] = value[
                        shard * in_rows : (shard + 1) * in_rows, target * lanes : (target + 1) * lanes
                    ]
            return 0

        lax.fori_loop(0, features // 128, in_step, 0)

        def out_step(block, _):
            cols = pl.ds(pl.multiple_of(block * 128, 128), 128)
            value = dot(dy_ref[e, :, cols], hid_ref[e], TN).astype(LOW)
            for shard in range(per_out):
                for target in range(peers):
                    to = block * per_out + shard
                    away = lax.rem(to + dp, 2)
                    parts_ref[
                        away,
                        lax.div(to, 2),
                        target,
                        e * rows_both + in_rows : (e + 1) * rows_both,
                        :,
                    ] = value[
                        shard * out_rows : (shard + 1) * out_rows,
                        target * lanes : (target + 1) * lanes,
                    ]
            return 0

        lax.fori_loop(0, out_width // 128, out_step, 0)

    for turn in range(peers):
        for step in range(1, peers):
            x_copy(turn, step).wait()
    pair_copy().wait()
    share_ref[...] = (core_sum(dp_side) + pair_recv[...].astype(F32)).astype(LOW)
    total = dx_send[me].astype(F32)
    for step in range(1, peers):
        total = total + dx_recv[lax.rem(me + step, peers)].astype(F32)
    dx_ref[...] = total


def total_kernel(
    features,
    width_out,
    valid_ref,
    inner_ref,
    stats_ref,
    tables_ref,
    shares_ref,
    grads_ref,
    inner_out,
    result_ref,
    pay_ref,
    got_ref,
    t_out,
    t_in,
):
    devices = got_ref.shape[0]
    peers = inner_out.shape[0]
    here, _, hid = inner_ref.shape
    inner_rows = inner_out.shape[1]
    number = stats_ref.shape[0] - 2
    me = lax.axis_index("dp") * peers + lax.axis_index("mp")
    barrier = pltpu.get_barrier_semaphore()

    def place_of(device):
        return {"dp": lax.div(device, peers), "mp": lax.rem(device, peers)}

    def greet(step, _):
        target = lax.rem(me + step, devices)
        pl.semaphore_signal(barrier, inc=1, device_id=place_of(target), device_id_type=MESH)
        return 0

    lax.fori_loop(1, devices, greet, 0)
    lane = lax.broadcasted_iota(I32, (1, 128), 1)

    def whole_sum(value):
        return jnp.sum(jnp.sum(value, axis=0, keepdims=True), axis=1, keepdims=True)

    def grad_step(at, total):
        rows = grads_ref[pl.ds(pl.multiple_of(at * 64, 64), 64), :]
        return total + jnp.sum((rows * rows).reshape(8, 8, 128), axis=0)

    squares = lax.fori_loop(0, grads_ref.shape[0] // 64, grad_step, tables_ref[...])
    share = shares_ref[...]
    vector = jnp.where(lane == 0, stats_ref[number + 1, :1, :1], 0.0)
    vector = jnp.where(lane == 1, stats_ref[number + 1, :1, 1:2], vector)
    for at in range(number + 1):
        vector = jnp.where(lane == at + 2, whole_sum(stats_ref[at]), vector)
    vector = jnp.where(lane == number + 3, whole_sum(squares) + whole_sum(share * share), vector)
    pay_ref[...] = jnp.zeros_like(pay_ref)
    for e in range(here):
        for part in range(hid // 128):
            at = e * (hid // 128) + part
            pay_ref[at : at + 1, :] = inner_ref[e, :1, part * 128 : (part + 1) * 128]
    pay_ref[inner_rows : inner_rows + 1, :] = vector
    got_ref[me] = pay_ref[...]
    pl.semaphore_wait(barrier, devices - 1)

    def t_copy(step):
        target = lax.rem(me + step, devices)
        return pltpu.make_async_remote_copy(
            pay_ref,
            got_ref.at[me],
            t_out.at[step],
            t_in.at[step],
            device_id=place_of(target),
            device_id_type=MESH,
        )

    def start(step, _):
        t_copy(step).start()
        return 0

    def finish(step, _):
        t_copy(step).wait()
        return 0

    lax.fori_loop(1, devices, start, 0)
    lax.fori_loop(1, devices, finish, 0)
    total = jnp.zeros((1, 128), F32)
    inner_sq = jnp.zeros((inner_rows, 128), F32)
    for group in range(peers):
        part = jnp.zeros((inner_rows, 128), F32)
        for block in range(devices // peers):
            source = block * peers + group
            part = part + got_ref[source, :inner_rows, :]
            total = total + got_ref[source, inner_rows : inner_rows + 1, :]
        inner_out[group] = part
        inner_sq = inner_sq + part * part

    def pick(at):
        return jnp.sum(jnp.where(lane == at, total, 0.0), axis=1, keepdims=True)

    weight = pick(1)
    grad_norm = jnp.sqrt(pick(number + 3) + whole_sum(inner_sq)) / weight
    factor = jnp.minimum(1.0, clip_max / grad_norm) / weight
    count = valid_ref[0].astype(F32)
    width = jnp.where(lane == number + 2, float(features), float(width_out))
    result_ref[...] = jnp.zeros_like(result_ref)
    result_ref[0:1, :] = jnp.broadcast_to(factor, (1, 128))
    result_ref[1:2, :] = jnp.broadcast_to(grad_norm, (1, 128))
    result_ref[2:3, :] = total
    result_ref[3:4, :] = jnp.sqrt(total / (count * width) + stat_eps)


def table_kernel(factor_ref, weight_ref, first_ref, second_ref, grad_ref, *outs):
    pair, width, rows = weight_ref.shape
    gradient = grad_ref[0].T.reshape(pair, width, rows) * factor_ref[:1, :1].reshape(1, 1, 1)
    results = adamw(weight_ref[...], first_ref[...], second_ref[...], gradient, rate_table)
    for out, result in zip(outs, results):
        out[...] = result


def body(
    row_ids,
    counts,
    labels,
    label_mask,
    embeddings,
    embed_first,
    embed_second,
    expert_in,
    in_first,
    in_second,
    expert_out,
    out_first,
    out_second,
    gating,
    gating_first,
    gating_second,
    towers,
    towers_first,
    towers_second,
    heads,
    heads_first,
    heads_second,
    biases,
    biases_first,
    biases_second,
):
    devices = lax.axis_size(AXES)
    mp_count = lax.axis_size("mp")
    dp_count = lax.axis_size("dp")
    mp_index = lax.axis_index("mp")
    samples, tables_here = row_ids.shape
    tables, rows_dev, d_emb = embeddings.shape
    own = samples // mp_count
    requests = samples * tables_here
    capacity = 2 * requests // devices
    height = capacity // 2
    slots = devices * height
    row_bits = rows_dev.bit_length() - 1
    pairs = tables // 2
    lanes = 2 * d_emb
    group_rows = tables_here // 2 * rows_dev
    in_rows, out_rows = expert_in.shape[0], expert_out.shape[0]
    experts_here = EXPERTS // mp_count
    hid = expert_in.shape[2] * mp_count
    features = tables * d_emb
    width_out = out_rows * dp_count
    tower_hid = towers.shape[1] // TASKS

    outgoing, place, slot, source = pl.pallas_call(
        functools.partial(route_kernel, row_bits),
        out_shape=(
            jax.ShapeDtypeStruct((devices, 1, capacity), I32),
            jax.ShapeDtypeStruct((tables_here, samples), I32),
            jax.ShapeDtypeStruct((tables_here, samples), I32),
            jax.ShapeDtypeStruct((tables_here, samples), I32),
        ),
        in_specs=[VMEM],
        out_specs=(VMEM,) * 4,
        compiler_params=params(32),
        name="route",
    )(row_ids.T)
    in_out_rows = in_rows + out_rows
    hid_here = hid // mp_count
    shard = jnp.concatenate([expert_in, expert_out], axis=0).astype(LOW).transpose(1, 0, 2)

    def sems(*shape):
        return pltpu.SemaphoreType.DMA(shape)

    codes, shard = pl.pallas_call(
        ask_kernel,
        out_shape=(
            jax.ShapeDtypeStruct((devices, 1, capacity), I32),
            jax.ShapeDtypeStruct((experts_here, in_out_rows, hid), LOW),
        ),
        in_specs=[VMEM, VMEM],
        out_specs=(VMEM, VMEM),
        scratch_shapes=[sems(devices), sems(devices), sems(mp_count), sems(mp_count)],
        compiler_params=pltpu.CompilerParams(
            vmem_limit_bytes=16 * MIB, collective_id=2, has_side_effects=True
        ),
        name="ask",
    )(outgoing, shard)
    expert_w = lax.all_gather(shard, "dp", axis=0, tiled=False)
    codes = codes.reshape(devices, capacity)
    asked = codes[:, 0] >> 16
    plain = codes & 65535
    found_at = jnp.maximum(plain - 1, 0)
    table_at = found_at >> row_bits
    sum_at = (table_at >> 1) * rows_dev + (found_at & (rows_dev - 1))
    number = jnp.arange(capacity, dtype=I32)[None, :]
    part_at = ((number & 1) * 2 + (table_at & 1)) * slots + (number >> 1)
    part_at = part_at + jnp.arange(devices, dtype=I32)[:, None] * height
    part_at = jnp.where(plain > 0, part_at, 4 * slots)

    table_view = jnp.transpose(embeddings, (0, 2, 1))
    found = pl.pallas_call(
        functools.partial(find_kernel, mp_count),
        grid=(mp_count,),
        out_shape=jax.ShapeDtypeStruct((dp_count, mp_count, height, lanes), LOW),
        in_specs=[
            SMEM,
            SMEM,
            pl.BlockSpec((tables_here, d_emb, rows_dev), lambda m: (m, 0, 0)),
        ],
        out_specs=pl.BlockSpec((dp_count, 1, height, lanes), lambda m: (0, m, 0, 0)),
        scratch_shapes=[
            pltpu.VMEM((tables_here * rows_dev, lanes), F32),
            pltpu.VMEM((height, lanes), F32),
        ],
        compiler_params=params(60),
        name="find",
    )(found_at.reshape(-1), asked, table_view)
    returned = lax.all_to_all(
        found.reshape(devices, height, lanes), AXES, split_axis=0, concat_axis=0, tiled=True
    )
    embedded = pl.pallas_call(
        place_kernel,
        out_shape=jax.ShapeDtypeStruct((samples, tables_here * d_emb), LOW),
        in_specs=[SMEM, VMEM],
        out_specs=VMEM,
        scratch_shapes=[
            pltpu.VMEM((2 * slots, lanes), F32),
            pltpu.VMEM((tables_here // 2, samples, lanes), F32),
        ],
        compiler_params=params(32),
        name="place",
    )(place.reshape(-1), returned.reshape(slots, lanes))

    first = EXPERTS * hid
    second = first + EXPERTS * width_out
    third = second + TASKS * EXPERTS
    fourth = third + TASKS * tower_hid
    inner_here = lax.dynamic_index_in_dim(
        biases[:first].reshape(mp_count, experts_here, 1, hid), mp_index, 0, keepdims=False
    )
    outer_here = lax.dynamic_index_in_dim(
        biases[first:second].reshape(mp_count, experts_here, 1, width_out),
        mp_index,
        0,
        keepdims=False,
    )
    gating_low = gating.T.astype(LOW)
    all_gates = TASKS * EXPERTS
    pack_rows = width_out

    def scratch(shape, kind=F32):
        return pltpu.VMEM(shape, kind)

    blocks, hidden, slopes, output_rows, gate_logit_grad, small_grads, stat_parts = pl.pallas_call(
        ahead_kernel,
        out_shape=(
            jax.ShapeDtypeStruct((mp_count, samples, tables_here * d_emb), LOW),
            jax.ShapeDtypeStruct((experts_here, samples, hid), LOW),
            jax.ShapeDtypeStruct((experts_here, samples, hid), F32),
            jax.ShapeDtypeStruct((experts_here, samples, width_out), LOW),
            jax.ShapeDtypeStruct((own, all_gates), LOW),
            jax.ShapeDtypeStruct((pack_rows, TASKS * tower_hid + 128), LOW),
            jax.ShapeDtypeStruct((EXPERTS + TASKS + 2, 8, width_out), F32),
        ),
        in_specs=[SMEM] + [VMEM] * 9 + [SMEM] + [VMEM] * 2,
        out_specs=(VMEM,) * 7,
        scratch_shapes=[
            scratch((mp_count, experts_here, own, width_out), LOW),
            scratch((mp_count, experts_here, own, width_out), LOW),
            scratch((own, all_gates)),
            scratch((TASKS, own, width_out), LOW),
            scratch((TASKS, own, width_out)),
            scratch((own, all_gates)),
            scratch((EXPERTS, own, width_out), LOW),
            scratch((pack_rows, 128)),
            scratch((own, hid)),
            sems(mp_count, mp_count),
            sems(mp_count, mp_count),
            sems(mp_count),
            sems(mp_count),
            sems(mp_count),
            sems(mp_count),
        ],
        compiler_params=pltpu.CompilerParams(
            vmem_limit_bytes=56 * MIB, collective_id=0, has_side_effects=True
        ),
        name="ahead",
    )(
        lax.dynamic_slice_in_dim(counts, lax.axis_index("dp"), 1, 0),
        embedded,
        expert_w,
        inner_here,
        outer_here,
        gating_low,
        biases[second:third].reshape(1, all_gates),
        towers.astype(LOW),
        biases[third:fourth].reshape(TASKS, tower_hid),
        heads,
        biases[fourth:].reshape(1, TASKS),
        labels,
        label_mask,
    )
    pack_shape = (pack_rows // 4, TASKS * tower_hid + 128)
    embed_grad, grad_parts, inner_parts, share = pl.pallas_call(
        back_kernel,
        out_shape=(
            jax.ShapeDtypeStruct((samples, tables_here * d_emb), F32),
            jax.ShapeDtypeStruct(
                (2, dp_count // 2, mp_count, experts_here * in_out_rows, hid_here), LOW
            ),
            jax.ShapeDtypeStruct((experts_here, 8, hid), F32),
            jax.ShapeDtypeStruct(pack_shape, LOW),
        ),
        in_specs=[VMEM] * 8,
        out_specs=(VMEM,) * 4,
        scratch_shapes=[
            scratch((experts_here, samples, hid), LOW),
            scratch((mp_count, samples, tables_here * d_emb), LOW),
            scratch((mp_count, samples, tables_here * d_emb), LOW),
            scratch((2 * pack_shape[0], pack_shape[1]), LOW),
            scratch(pack_shape, LOW),
            scratch(pack_shape, LOW),
            sems(mp_count, mp_count),
            sems(mp_count, mp_count),
            sems(2),
            sems(2),
        ],
        compiler_params=pltpu.CompilerParams(
            vmem_limit_bytes=56 * MIB, collective_id=1, has_side_effects=True
        ),
        name="back",
    )(output_rows, hidden, slopes, blocks, expert_w, gate_logit_grad, gating_low, small_grads)

    back_rows = pl.pallas_call(
        send_kernel,
        out_shape=jax.ShapeDtypeStruct((slots, lanes), LOW),
        in_specs=[SMEM, SMEM, VMEM],
        out_specs=VMEM,
        scratch_shapes=[
            pltpu.VMEM((tables_here // 2, 2 * samples, lanes), F32),
            pltpu.VMEM((2 * slots, lanes), F32),
        ],
        compiler_params=params(32),
        name="send",
    )(slot.reshape(-1), source.reshape(-1), embed_grad)
    share = share.reshape(devices // 4, pack_rows // devices, -1)
    arrived, shares = pl.pallas_call(
        swap_kernel,
        out_shape=(
            jax.ShapeDtypeStruct((devices, height, lanes), LOW),
            jax.ShapeDtypeStruct(share.shape, LOW),
        ),
        in_specs=[VMEM, VMEM],
        out_specs=(VMEM, VMEM),
        scratch_shapes=[sems(devices), sems(devices), sems(devices // 4), sems(devices // 4)],
        compiler_params=pltpu.CompilerParams(
            vmem_limit_bytes=16 * MIB, collective_id=3, has_side_effects=True
        ),
        name="swap",
    )(back_rows.reshape(devices, height, lanes), share)
    def exchange_all(parts):
        return lax.all_to_all(parts, AXES, split_axis=0, concat_axis=0, tiled=True)

    share = jnp.sum(shares.astype(F32), axis=0)
    whole = lax.all_gather(share.astype(LOW), AXES, axis=0, tiled=False)

    partner = lax.ppermute(grad_parts[1], "dp", [(d, d ^ 1) for d in range(dp_count)])
    partner, arrived = lax.optimization_barrier((partner, arrived))
    grad_parts = (grad_parts[0].astype(F32) + partner.astype(F32)).astype(LOW)
    sides = [
        [d * mp_count + m for d in range(x, dp_count, 2) for m in range(mp_count)] for x in range(2)
    ]
    grad_parts = lax.all_to_all(
        grad_parts.reshape(devices // 2, experts_here * in_out_rows, hid_here),
        AXES,
        split_axis=0,
        concat_axis=0,
        axis_index_groups=sides,
        tiled=True,
    )
    grad_sum = jnp.sum(
        grad_parts.reshape(dp_count // 2, mp_count, experts_here, in_out_rows, -1).astype(F32), 0
    )
    owned = grad_sum.reshape(EXPERTS, in_out_rows, -1).transpose(1, 0, 2)
    in_sum, out_sum = owned[:in_rows], owned[in_rows:]

    table_grad, table_sq = pl.pallas_call(
        functools.partial(add_kernel, mp_count),
        out_shape=(
            jax.ShapeDtypeStruct((pairs * rows_dev, lanes), F32),
            jax.ShapeDtypeStruct((8, lanes), F32),
        ),
        in_specs=[SMEM, SMEM, SMEM, VMEM],
        out_specs=(pl.BlockSpec(memory_space=pl.ANY), VMEM),
        scratch_shapes=[
            pltpu.VMEM((4 * slots + 8, lanes), F32),
            pltpu.SemaphoreType.DMA((mp_count,)),
        ]
        + [pltpu.VMEM((group_rows, lanes), F32)] * mp_count,
        compiler_params=params(60),
        name="add",
    )(sum_at.reshape(-1), part_at.reshape(-1), asked, arrived.reshape(slots, lanes))

    stat_end = EXPERTS + TASKS
    inner_rows = experts_here * hid // 128
    pay_rows = inner_rows + 8
    inner_sum, result = pl.pallas_call(
        functools.partial(total_kernel, features, width_out),
        out_shape=(
            jax.ShapeDtypeStruct((mp_count, inner_rows, 128), F32),
            jax.ShapeDtypeStruct((8, 128), F32),
        ),
        in_specs=[SMEM] + [VMEM] * 5,
        out_specs=(VMEM,) * 2,
        scratch_shapes=[
            scratch((pay_rows, 128)),
            scratch((devices, pay_rows, 128)),
            sems(devices),
            sems(devices),
        ],
        compiler_params=pltpu.CompilerParams(
            vmem_limit_bytes=16 * MIB, collective_id=4, has_side_effects=True
        ),
        name="total",
    )(
        jnp.sum(counts).reshape(1),
        inner_parts,
        stat_parts,
        table_sq,
        share,
        grad_sum.reshape(-1, 128),
    )
    factor = result[0, 0]

    table_spec = pl.BlockSpec((2, d_emb, rows_dev), lambda p: (p, 0, 0))
    embed_out = pl.pallas_call(
        table_kernel,
        grid=(pairs,),
        out_shape=(jax.ShapeDtypeStruct(table_view.shape, F32),) * 3,
        in_specs=[
            pl.BlockSpec((8, 128), lambda p: (0, 0)),
            table_spec,
            table_spec,
            table_spec,
            pl.BlockSpec((1, rows_dev, lanes), lambda p: (p, 0, 0)),
        ],
        out_specs=(table_spec,) * 3,
        compiler_params=params(58),
        name="tables",
    )(
        result,
        table_view,
        jnp.transpose(embed_first, (0, 2, 1)),
        jnp.transpose(embed_second, (0, 2, 1)),
        table_grad.reshape(pairs, rows_dev, lanes),
    )
    embed_out = [jnp.transpose(value, (0, 2, 1)) for value in embed_out]
    in_out = adamw(expert_in, in_first, in_second, in_sum * factor, rate_dense)
    out_out = adamw(expert_out, out_first, out_second, out_sum * factor, rate_dense)
    whole, embed_out = lax.optimization_barrier((whole, embed_out))
    whole = whole.reshape(dp_count // 2, 2, mp_count // 2, 2, pack_rows // devices, -1)
    whole = whole.transpose(3, 1, 0, 2, 4, 5).reshape(pack_rows, -1)
    towers_sum = whole[:, : TASKS * tower_hid].astype(F32)
    packed = whole[:, TASKS * tower_hid :].astype(F32)
    blocks_x = features // 128
    heads_at = blocks_x * all_gates
    tower_at = heads_at + TASKS * tower_hid // 128
    outer_at = tower_at + TASKS * tower_hid // 128
    rest_at = outer_at + EXPERTS * width_out // 128
    gating_sum = packed[:heads_at].reshape(blocks_x, all_gates, 128).transpose(1, 0, 2)
    gating_sum = gating_sum.reshape(all_gates, features).T
    heads_sum = packed[heads_at:tower_at].reshape(TASKS, tower_hid)
    bias_sum = jnp.concatenate(
        [
            inner_sum.reshape(-1),
            packed[outer_at:rest_at].reshape(-1),
            packed[rest_at, :all_gates],
            packed[tower_at:outer_at].reshape(-1),
            packed[rest_at + 1, :TASKS],
        ]
    )
    gating_out = adamw(gating, gating_first, gating_second, gating_sum * factor, rate_dense)
    towers_out = adamw(towers, towers_first, towers_second, towers_sum * factor, rate_dense)
    heads_out = adamw(heads, heads_first, heads_second, heads_sum * factor, rate_dense)
    biases_out = adamw(biases, biases_first, biases_second, bias_sum * factor, rate_dense)
    stats = jnp.concatenate([result[3, stat_end + 2][None], result[3, 2 : stat_end + 2]])
    loss = result[2, :2]
    return (
        *embed_out,
        *in_out,
        in_out[0].astype(LOW),
        *out_out,
        out_out[0].astype(LOW),
        *gating_out,
        *towers_out,
        *heads_out,
        *biases_out,
        result[1, :1],
        loss,
        stats,
    )


def solution(mesh):
    rows = P(None, AXES, None)
    expert = P("dp", None, "mp")
    sample = P(AXES, None)
    placed = (P("dp", "mp"), P(), sample, sample) + (rows,) * 3 + (expert,) * 6 + (P(),) * 12
    results = (rows,) * 3 + (expert,) * 8 + (P(),) * 15
    return jax.shard_map(body, mesh=mesh, in_specs=placed, out_specs=results, check_vma=False)
```

```python
import functools
import math

import jax
import jax.numpy as jnp
from jax import lax
from jax.experimental import pallas as pl
from jax.experimental.pallas import tpu as pltpu
from jax.sharding import PartitionSpec as P

EXPERTS = 8
TASKS = 5
STEP = 3

HIGH = lax.Precision.HIGHEST
beta_one = 0.5
beta_two = 0.5
adam_eps = 1e-08
decay = 0.01
clip_max = 0.002
rate_table = 0.5
rate_dense = 0.02
stat_eps = 1e-06

LOW = jnp.bfloat16
F32 = jnp.float32
I32 = jnp.int32
MIB = 1024 * 1024
AXES = ("dp", "mp")


def params(mib):
    return pltpu.CompilerParams(vmem_limit_bytes=mib * MIB)


VMEM = pl.BlockSpec(memory_space=pltpu.VMEM)
SMEM = pl.BlockSpec(memory_space=pltpu.SMEM)


def adamw(weight, first, second, gradient, rate):
    first_next = beta_one * first + (1.0 - beta_one) * gradient
    second_next = beta_two * second + (1.0 - beta_two) * gradient * gradient
    corrected = first_next / (1.0 - beta_one**STEP)
    scaled = jnp.sqrt(second_next / (1.0 - beta_two**STEP))
    return (
        weight - rate * (corrected / (scaled + adam_eps) + decay * weight),
        first_next,
        second_next,
    )


def route_kernel(row_bits, ids_ref, out_ref, place_ref, slot_ref, from_ref):
    devices, _, capacity = out_ref.shape
    tables, samples = ids_ref.shape
    rows_dev = 1 << row_bits
    halves = devices * capacity // 2
    width = 256
    upper = (
        lax.broadcasted_iota(I32, (width, width), 0) <= lax.broadcasted_iota(I32, (width, width), 1)
    ).astype(LOW)
    owners = lax.broadcasted_iota(I32, (devices, width), 0)
    slots = lax.broadcasted_iota(I32, (capacity, width), 0)
    carry = jnp.zeros((devices, 1), F32)
    total = jnp.zeros((2 * devices, capacity), F32)
    for table in range(tables):
        parity = table % 2
        for part in range(samples // width):
            cols = pl.ds(part * width, width)
            ids = ids_ref[pl.ds(table, 1), cols]
            owner = ids >> row_bits
            code = table * rows_dev + (ids & (rows_dev - 1)) + 1
            onehot = (owner == owners).astype(F32)
            counted = jnp.dot(onehot.astype(LOW), upper, preferred_element_type=F32) + carry
            rank = jnp.sum(onehot * counted, axis=0, keepdims=True).astype(I32) - 1
            carry = counted[:, width - 1 :]
            at_slot = (rank == slots).astype(LOW)
            high = (code >> 7).astype(F32)
            low = (code & 127).astype(F32)
            pieces = jnp.concatenate([onehot * high, onehot * low], axis=0).astype(LOW)
            total += lax.dot_general(
                pieces, at_slot, (((1,), (1,)), ((), ())), preferred_element_type=F32
            )
            row = owner * (capacity // 2) + (rank >> 1)
            half = rank & 1
            place_ref[pl.ds(table, 1), cols] = (half ^ parity) * halves + row
            slot_ref[pl.ds(table, 1), cols] = half * halves + row
            sample = lax.broadcasted_iota(I32, (1, width), 1) + part * width
            from_ref[pl.ds(table, 1), cols] = (half ^ parity) * samples + sample
    codes = (total[:devices] * 128.0 + total[devices:]).astype(I32)
    first = lax.broadcasted_iota(I32, (devices, capacity), 1) == 0
    counted = jnp.where(first, carry * 65536.0, 0.0).astype(I32)
    out_ref[...] = (codes + counted).reshape(devices, 1, capacity)


def left_lanes(shape):
    return lax.broadcasted_iota(I32, shape, len(shape) - 1) < 64


def find_kernel(groups, at_ref, counts_ref, table_ref, out_ref, turned_ref, rows_ref):
    blocks, _, height, lanes = out_ref.shape
    tables, width, rows_dev = table_ref.shape
    group = pl.program_id(0)
    left = left_lanes((1, lanes))
    part = 512

    def turn_step(step, _):
        table = lax.div(step, rows_dev // part)
        first = pl.multiple_of(lax.rem(step, rows_dev // part) * part, part)
        columns = table_ref[table, :, pl.ds(first, part)]
        there = pl.ds(pl.multiple_of(step * part, part), part)
        turned_ref[there, :] = jnp.concatenate([columns, columns], axis=0).T
        return 0

    lax.fori_loop(0, tables * (rows_dev // part), turn_step, 0)

    def block_step(block, _):
        source = block * groups + group
        base = source * 2 * height

        def step(outer, _):
            got = []
            for inner in range(8):
                at = outer * 8 + inner
                even = turned_ref[pl.ds(at_ref[base + 2 * at], 1), :]
                odd = turned_ref[pl.ds(at_ref[base + 2 * at + 1], 1), :]
                got.append((at, jnp.where(left, even, odd)))
            for at, row in got:
                rows_ref[pl.ds(at, 1), :] = row
            return 0

        lax.fori_loop(0, (counts_ref[source] + 15) // 16, step, 0)
        out_ref[block, 0] = rows_ref[...].astype(LOW)
        return 0

    lax.fori_loop(0, blocks, block_step, 0)


def place_kernel(place_ref, rows_ref, out_ref, both_ref, flat_ref):
    count, lanes = rows_ref.shape
    samples = out_ref.shape[0]
    tables = place_ref.shape[0] // samples
    rows = rows_ref[...].astype(F32)
    both_ref[pl.ds(0, count), :] = rows
    both_ref[pl.ds(count, count), :] = pltpu.roll(rows, 64, 1)
    left = left_lanes((1, lanes))

    def step(outer, _):
        got = []
        for inner in range(8):
            sample = outer * 8 + inner
            for pair in range(tables // 2):
                even = both_ref[pl.ds(place_ref[2 * pair * samples + sample], 1), :]
                odd = both_ref[pl.ds(place_ref[(2 * pair + 1) * samples + sample], 1), :]
                got.append((pair, sample, jnp.where(left, even, odd)))
        for pair, sample, row in got:
            flat_ref[pair, pl.ds(sample, 1), :] = row
        return 0

    lax.fori_loop(0, samples // 8, step, 0)
    for pair in range(tables // 2):
        out_ref[:, pair * lanes : (pair + 1) * lanes] = flat_ref[pair].astype(LOW)


def send_kernel(slot_ref, from_ref, grad_ref, out_ref, both_ref, rows_ref):
    count, lanes = out_ref.shape
    samples = grad_ref.shape[0]
    tables = slot_ref.shape[0] // samples
    for pair in range(tables // 2):
        rows = grad_ref[:, pair * lanes : (pair + 1) * lanes]
        both_ref[pair, pl.ds(0, samples), :] = rows
        both_ref[pair, pl.ds(samples, samples), :] = pltpu.roll(rows, 64, 1)

    def step(outer, _):
        got = []
        for inner in range(8):
            sample = outer * 8 + inner
            for table in range(tables):
                row = both_ref[table // 2, pl.ds(from_ref[table * samples + sample], 1), :]
                got.append((slot_ref[table * samples + sample], row))
        for slot, row in got:
            rows_ref[pl.ds(slot, 1), :] = row
        return 0

    lax.fori_loop(0, samples // 8, step, 0)
    left = left_lanes((count, lanes))
    out_ref[...] = jnp.where(
        left, rows_ref[pl.ds(0, count), :], rows_ref[pl.ds(count, count), :]
    ).astype(LOW)


def swap_kernel(rows_ref, share_ref, out_ref, shares_ref, r_out, r_in, s_out, s_in):
    devices = rows_ref.shape[0]
    groups = share_ref.shape[0]
    peers = lax.axis_size("mp")
    dp, mp = lax.axis_index("dp"), lax.axis_index("mp")
    mine = lax.div(dp, 2) * (peers // 2) + lax.div(mp, 2)
    me = dp * peers + mp
    barrier = pltpu.get_barrier_semaphore()

    def place_of(device):
        return {"dp": lax.div(device, peers), "mp": lax.rem(device, peers)}

    def greet(step, _):
        target = lax.rem(me + step, devices)
        pl.semaphore_signal(barrier, inc=1, device_id=place_of(target), device_id_type=MESH)
        return 0

    lax.fori_loop(1, devices, greet, 0)
    pl.semaphore_wait(barrier, devices - 1)

    def r_copy(step):
        target = lax.rem(me + step, devices)
        return pltpu.make_async_remote_copy(
            rows_ref.at[target],
            out_ref.at[me],
            r_out.at[step],
            r_in.at[step],
            device_id=place_of(target),
            device_id_type=MESH,
        )

    def s_copy(step):
        target = lax.rem(mine + step, groups)
        to_dp = lax.div(target, peers // 2) * 2 + lax.rem(dp, 2)
        to_mp = lax.rem(target, peers // 2) * 2 + lax.rem(mp, 2)
        return pltpu.make_async_remote_copy(
            share_ref.at[target],
            shares_ref.at[mine],
            s_out.at[step],
            s_in.at[step],
            device_id={"dp": to_dp, "mp": to_mp},
            device_id_type=MESH,
        )

    def loop(first, copies, act):
        def step(at, _):
            act(copies(at))
            return 0

        lax.fori_loop(1, first, step, 0)

    loop(devices, r_copy, lambda copy: copy.start())
    loop(groups, s_copy, lambda copy: copy.start())
    out_ref[me] = rows_ref[me]
    shares_ref[mine] = share_ref[mine]
    loop(groups, s_copy, lambda copy: copy.wait())
    loop(devices, r_copy, lambda copy: copy.wait())


def add_kernel(
    groups, at_ref, part_at_ref, counts_ref, rows_ref, out_ref, square_ref, parts_ref, sems, *sums
):
    count, lanes = rows_ref.shape
    sources = counts_ref.shape[0]
    height = count // sources
    table_rows = sums[0].shape[0]
    left = left_lanes((count, lanes))
    rows = rows_ref[...].astype(F32)
    turned = pltpu.roll(rows, 64, 1)
    parts_ref[pl.ds(0, count), :] = jnp.where(left, rows, 0.0)
    parts_ref[pl.ds(count, count), :] = jnp.where(left, 0.0, turned)
    parts_ref[pl.ds(2 * count, count), :] = jnp.where(left, turned, 0.0)
    parts_ref[pl.ds(3 * count, count), :] = jnp.where(left, 0.0, rows)
    parts_ref[pl.ds(4 * count, 8), :] = jnp.zeros((8, lanes), F32)

    def clear(at, _):
        for table in sums:
            table[pl.ds(pl.multiple_of(at * 64, 64), 64), :] = jnp.zeros((64, lanes), F32)
        return 0

    lax.fori_loop(0, table_rows // 64, clear, 0)

    def block_step(block, _):
        most = counts_ref[block * groups]
        for group in range(1, groups):
            most = jnp.maximum(most, counts_ref[block * groups + group])

        def step(outer, _):
            for inner in range(4):
                got = []
                for group in range(groups):
                    at = (block * groups + group) * 2 * height + outer * 4 + inner
                    here = pl.ds(at_ref[at], 1)
                    part = pl.ds(part_at_ref[at], 1)
                    got.append((here, sums[group][here, :] + parts_ref[part, :]))
                for group, (here, row) in enumerate(got):
                    sums[group][here, :] = row
            return 0

        lax.fori_loop(0, (most + 3) // 4, step, 0)
        return 0

    lax.fori_loop(0, sources // groups, block_step, 0)
    copies = [
        pltpu.make_async_copy(
            sums[group], out_ref.at[pl.ds(group * table_rows, table_rows)], sems.at[group]
        )
        for group in range(groups)
    ]
    for copy in copies:
        copy.start()

    def square(at, total):
        for table in sums:
            rows = table[pl.ds(pl.multiple_of(at * 64, 64), 64), :]
            total = total + jnp.sum((rows * rows).reshape(8, 8, lanes), axis=0)
        return total

    square_ref[...] = lax.fori_loop(0, table_rows // 64, square, jnp.zeros((8, lanes), F32))
    for copy in copies:
        copy.wait()


def gelu_parts(value):
    scale = math.sqrt(2.0 / math.pi)
    square = value * value
    bend = jnp.tanh(scale * value * (1.0 + 0.044715 * square))
    half = 0.5 * (1.0 + bend)
    slope = half + 0.5 * value * (1.0 - bend * bend) * (scale * (1.0 + 3 * 0.044715 * square))
    return value * half, slope


def dot(a, b, axes=((1,), (0,)), precision=None):
    return lax.dot_general(
        a, b, (axes, ((), ())), preferred_element_type=F32, precision=precision
    )


NT = ((1,), (1,))
TN = ((0,), (0,))
MESH = pl.DeviceIdType.MESH


def meet(peers, partner=None):
    me = lax.axis_index("mp")
    barrier = pltpu.get_barrier_semaphore()
    if partner is not None:
        pl.semaphore_signal(
            barrier, inc=1, device_id={"dp": partner, "mp": me}, device_id_type=MESH
        )
    for step in range(1, peers):
        pl.semaphore_signal(
            barrier, inc=1, device_id={"mp": lax.rem(me + step, peers)}, device_id_type=MESH
        )
    pl.semaphore_wait(barrier, peers - 1 + (partner is not None))
    return me


def ask_kernel(codes_ref, shard_ref, out_ref, full_ref, c_out, c_in, w_out, w_in):
    devices = codes_ref.shape[0]
    here, _, full = full_ref.shape
    width = shard_ref.shape[2]
    peers = full // width
    mp = lax.axis_index("mp")
    me = lax.axis_index("dp") * peers + mp
    barrier = pltpu.get_barrier_semaphore()

    def place_of(device):
        return {"dp": lax.div(device, peers), "mp": lax.rem(device, peers)}

    def greet(step, _):
        target = lax.rem(me + step, devices)
        pl.semaphore_signal(barrier, inc=1, device_id=place_of(target), device_id_type=MESH)
        return 0

    lax.fori_loop(1, devices, greet, 0)
    columns = pl.ds(pl.multiple_of(mp * width, width), width)
    full_ref[:, :, columns] = shard_ref[pl.ds(mp * here, here)]
    out_ref[me] = codes_ref[me]
    pl.semaphore_wait(barrier, devices - 1)

    def c_copy(step):
        target = lax.rem(me + step, devices)
        return pltpu.make_async_remote_copy(
            codes_ref.at[target],
            out_ref.at[me],
            c_out.at[step],
            c_in.at[step],
            device_id=place_of(target),
            device_id_type=MESH,
        )

    def w_copy(step):
        target = lax.rem(mp + step, peers)
        return pltpu.make_async_remote_copy(
            shard_ref.at[pl.ds(target * here, here)],
            full_ref.at[:, :, columns],
            w_out.at[step],
            w_in.at[step],
            device_id={"mp": target},
            device_id_type=MESH,
        )

    def start(step, _):
        c_copy(step).start()
        return 0

    def finish(step, _):
        c_copy(step).wait()
        return 0

    lax.fori_loop(1, devices, start, 0)
    for step in range(1, peers):
        w_copy(step).start()
    lax.fori_loop(1, devices, finish, 0)
    for step in range(1, peers):
        w_copy(step).wait()


def dense_kernel(
    count_ref,
    x_ref,
    w_ref,
    b1_ref,
    b2_ref,
    wg_ref,
    bg_ref,
    w3_ref,
    tb1_ref,
    heads_ref,
    tb2_ref,
    labels_ref,
    mask_ref,
    stats_ref,
    dx_ref,
    parts_ref,
    g_b1_ref,
    share_ref,
    blocks_ref,
    hid_ref,
    slope_ref,
    dy_ref,
    y_send,
    y_ref,
    gates_ref,
    mixb_ref,
    dmix_ref,
    dg_ref,
    dy_send,
    small_ref,
    pack_ref,
    act_ref,
    gate_ref,
    dpre_ref,
    dx_send,
    dx_near,
    dx_help,
    dx_sum,
    dx_far,
    core_recv,
    pair_send,
    pair_recv,
    x_out,
    x_in,
    y_out,
    y_in,
    d_out,
    d_in,
    g_out,
    g_in,
    s_out,
    s_in,
):
    peers, samples, width = blocks_ref.shape
    here = hid_ref.shape[0]
    out_width = y_ref.shape[3]
    own = y_ref.shape[2]
    experts = peers * here
    tasks, tower_hid = heads_ref.shape
    shards, hid = w_ref.shape[0], w_ref.shape[3]
    in_rows = peers * width // shards
    rows_both = w_ref.shape[2]
    out_rows = rows_both - in_rows
    features = peers * width
    dp = lax.axis_index("dp")
    dp_side = lax.rem(dp, 2)
    pair = dp + 1 - 2 * dp_side
    me = meet(peers, pair)
    side = lax.rem(me, 2)
    chip = lax.div(me, 2)
    near = me + 1 - 2 * side
    far = lax.rem(me + 2, peers)
    across = lax.rem(near + 2, peers)

    def rows_of(chunk):
        return pl.ds(pl.multiple_of(chunk * own, own), own)

    def ahead_chunk(turn):
        return lax.rem(2 * chip + 2 + turn, peers)

    def back_chunk(turn):
        return lax.rem(2 * chip + turn, peers)

    def remote(source, target, out_sem, in_sem, device):
        return pltpu.make_async_remote_copy(
            source, target, out_sem, in_sem, device_id={"dp": dp, "mp": device}, device_id_type=MESH
        )

    def x_far(turn):
        rows = rows_of(back_chunk(turn))
        return remote(
            x_ref.at[rows], blocks_ref.at[me, rows], x_out.at[0, turn], x_in.at[0, turn], far
        )

    def x_near(turn):
        rows = rows_of(ahead_chunk(turn))
        return remote(
            x_ref.at[rows], blocks_ref.at[me, rows], x_out.at[1, turn], x_in.at[1, turn], near
        )

    def x_hand(turn):
        rows = rows_of(ahead_chunk(turn))
        block = blocks_ref.at[far, rows]
        return remote(block, block, x_out.at[2, turn], x_in.at[2, turn], near)

    def y_copy(turn, relation, device):
        return remote(
            y_send.at[turn], y_ref.at[me], y_out.at[relation], y_in.at[relation], device
        )

    def d_copy(relation, device):
        return remote(
            dy_send.at[pl.ds(device * here, here)],
            dy_ref.at[:, rows_of(me), :],
            d_out.at[relation],
            d_in.at[relation],
            device,
        )

    def g_near(turn):
        rows = rows_of(back_chunk(turn))
        return remote(
            dx_send.at[near, rows], dx_near.at[rows], g_out.at[0, turn], g_in.at[0, turn], near
        )

    def g_help(turn):
        rows = rows_of(back_chunk(turn))
        return remote(
            dx_send.at[across, rows], dx_help.at[rows], g_out.at[1, turn], g_in.at[1, turn], near
        )

    def g_far(turn):
        rows = rows_of(back_chunk(turn))
        return remote(
            dx_sum.at[rows], dx_far.at[rows], g_out.at[2, turn], g_in.at[2, turn], far
        )

    for turn in range(peers):
        x_far(turn).start()
        x_near(turn).start()
    blocks_ref[me] = x_ref[...]
    limit = count_ref[0]

    x_far(0).wait_recv()
    x_hand(0).start()

    def expert_step(turn, _):
        x_near(turn).wait_recv()
        x_hand(turn).wait_recv()

        @pl.when(turn < peers - 1)
        def _():
            x_far(turn + 1).wait_recv()
            x_hand(turn + 1).start()

        chunk = ahead_chunk(turn)
        rows = rows_of(chunk)
        x = jnp.concatenate([blocks_ref[block, rows] for block in range(peers)], axis=1)
        for e in range(here):
            w_in = w_ref[:, e, :in_rows, :].reshape(peers * width, hid)
            act_ref[...] = dot(x, w_in) + b1_ref[e]

            def gelu_step(tile, _):
                at = pl.multiple_of(tile * 32, 32)
                value, slope = gelu_parts(act_ref[pl.ds(at, 32), :])
                there = pl.ds(pl.multiple_of(chunk * own + at, 32), 32)
                hid_ref[e, there, :] = value.astype(LOW)
                slope_ref[e, there, :] = slope
                return 0

            lax.fori_loop(0, own // 32, gelu_step, 0)
            w_out = w_ref[:, e, in_rows:, :].reshape(out_width, hid)
            y_send[turn, e] = (dot(hid_ref[e, rows, :], w_out, NT) + b2_ref[e]).astype(LOW)

        @pl.when(turn < 2)
        def _():
            y_copy(turn, 1 + lax.rem(side + turn, 2), chunk).start()

        @pl.when(jnp.logical_and(turn >= 2, chunk != me))
        def _():
            y_copy(turn, 0, chunk).start()

        @pl.when(chunk == me)
        def _():
            y_ref[me] = y_send[turn]

        return 0

    lax.fori_loop(0, peers, expert_step, 0)

    own_rows = rows_of(me)
    x_own = jnp.concatenate([blocks_ref[block, own_rows] for block in range(peers)], axis=1)
    logits = dot(x_own, wg_ref[...], NT) + bg_ref[...]
    for k in range(tasks):
        part = logits[:, k * experts : (k + 1) * experts]
        part = jnp.exp(part - jnp.max(part, axis=1, keepdims=True))
        gates_ref[:, k * experts : (k + 1) * experts] = part / jnp.sum(part, axis=1, keepdims=True)

    stats_ref[...] = jnp.zeros_like(stats_ref)

    def square_step(tile, total):
        at = pl.multiple_of(tile * 64, 64)
        valid = (lax.broadcasted_iota(I32, (64, 1), 0) + at) < limit
        part = jnp.where(valid, x_ref[pl.ds(at, 64), :].astype(F32), 0.0)
        return total + jnp.sum((part * part).reshape(8, 8, width), axis=0)

    x_square = lax.fori_loop(0, samples // 64, square_step, jnp.zeros((8, width), F32))
    stats_ref[experts + tasks, :, :width] = x_square
    for relation, device in enumerate((near, far, across)):
        y_copy(0, relation, device).wait_recv()

    tile_rows = 16

    def tile_of(tile):
        at = pl.multiple_of(tile * tile_rows, tile_rows)
        return at, pl.ds(at, tile_rows)

    def mix_step(tile, _):
        at, rows = tile_of(tile)
        valid = (lax.broadcasted_iota(I32, (tile_rows, 1), 0) + (at + me * own)) < limit
        gates = gates_ref[rows, :]
        mixed = [None] * tasks
        for e in range(experts):
            y = y_ref[e // here, e % here, rows, :].astype(F32)
            square = jnp.where(valid, y * y, 0.0)
            stats_ref[e] += square[:8] + square[8:]
            for k in range(tasks):
                term = gates[:, k * experts + e : k * experts + e + 1] * y
                mixed[k] = term if e == 0 else mixed[k] + term
        for k in range(tasks):
            square = jnp.where(valid, mixed[k] * mixed[k], 0.0)
            stats_ref[experts + k] += square[:8] + square[8:]
            mixb_ref[k, rows, :] = mixed[k].astype(LOW)
        return 0

    lax.fori_loop(0, own // tile_rows, mix_step, 0)

    pack_ref[...] = jnp.zeros_like(pack_ref)
    blocks_x = peers * width // 128
    heads_at = blocks_x * tasks * experts
    tower_at = heads_at + tasks * tower_hid // 128
    outer_at = tower_at + tasks * tower_hid // 128
    rest_at = outer_at + experts * out_width // 128
    loss = jnp.zeros((1, 1), F32)
    weight_sum = jnp.zeros((1, 1), F32)
    row_id = lax.broadcasted_iota(I32, (own, 1), 0) + me * own
    for k in range(tasks):
        cols = slice(k * tower_hid, (k + 1) * tower_hid)
        z, slope = gelu_parts(dot(mixb_ref[k], w3_ref[:, cols]) + tb1_ref[k : k + 1, :])
        head = heads_ref[k : k + 1, :]
        logit = jnp.sum(z * head, axis=1, keepdims=True) + tb2_ref[0, k]
        small = jnp.exp(-jnp.abs(logit))
        label = labels_ref[:, k : k + 1].astype(F32)
        weight = jnp.where(row_id < limit, mask_ref[:, k : k + 1].astype(F32), 0.0)
        soft = jnp.maximum(logit, 0.0) + jnp.log1p(small)
        loss += jnp.sum(weight * (soft - label * logit), axis=0, keepdims=True)
        weight_sum += jnp.sum(weight, axis=0, keepdims=True)
        chance = jnp.where(logit >= 0.0, 1.0, small) / (1.0 + small)
        dl = weight * (chance - label)
        g_head = jnp.sum(dl * z, axis=0, keepdims=True)
        dz = (dl * head * slope).astype(LOW)
        g_bias = jnp.sum(dz.astype(F32), axis=0, keepdims=True)
        for part in range(tower_hid // 128):
            lane = slice(part * 128, (part + 1) * 128)
            at = k * (tower_hid // 128) + part
            pack_ref[heads_at + at : heads_at + at + 1, :] = g_head[:, lane]
            pack_ref[tower_at + at : tower_at + at + 1, :] = g_bias[:, lane]
        pack_ref[rest_at + 1 : rest_at + 2, k : k + 1] = jnp.sum(dl, axis=0, keepdims=True)
        dmix_ref[k] = dot(dz, w3_ref[:, cols], NT)
        small_ref[:, cols] = dot(mixb_ref[k], dz, TN).astype(LOW)
    stats_ref[experts + tasks + 1, :1, :1] = loss
    stats_ref[experts + tasks + 1, :1, 1:2] = weight_sum

    def dy_step(tile, _):
        at, rows = tile_of(tile)
        gates = gates_ref[rows, :]
        dmix = [dmix_ref[k, rows, :] for k in range(tasks)]
        for e in range(experts):
            total = None
            for k in range(tasks):
                term = gates[:, k * experts + e : k * experts + e + 1] * dmix[k]
                total = term if k == 0 else total + term
            dy_send[e, rows, :] = total.astype(LOW)
        return 0

    lax.fori_loop(0, own // tile_rows, dy_step, 0)
    d_copy(1, far).start()
    d_copy(2, across).start()
    d_copy(0, near).start()
    dy_ref[:, own_rows, :] = dy_send[pl.ds(me * here, here)]
    ones = jnp.ones((8, own), LOW)
    for e in range(experts):
        g_outer = dot(ones, dy_send[e])
        for part in range(out_width // 128):
            at = outer_at + e * (out_width // 128) + part
            pack_ref[at : at + 1, :] = g_outer[:1, part * 128 : (part + 1) * 128]

    lane = lax.broadcasted_iota(I32, (tile_rows, tasks * experts), 1)

    def dg_step(tile, _):
        at, rows = tile_of(tile)
        dmix = [dmix_ref[k, rows, :] for k in range(tasks)]
        found = jnp.zeros((tile_rows, tasks * experts), F32)
        for e in range(experts):
            y = y_ref[e // here, e % here, rows, :].astype(F32)
            for k in range(tasks):
                value = jnp.sum(dmix[k] * y, axis=1, keepdims=True)
                found = jnp.where(lane == k * experts + e, value, found)
        dg_ref[rows, :] = found
        return 0

    lax.fori_loop(0, own // tile_rows, dg_step, 0)
    gates = gates_ref[...]
    dg = dg_ref[...]
    flat = (tasks * experts, tasks * experts)
    same = lax.broadcasted_iota(I32, flat, 0) // experts == lax.broadcasted_iota(I32, flat, 1) // experts
    mean = dot(gates * dg, same.astype(F32), precision=HIGH)
    dgl = (gates * (dg - mean)).astype(LOW)
    pack_ref[rest_at : rest_at + 1, : tasks * experts] = jnp.sum(
        dgl.astype(F32), axis=0, keepdims=True
    )
    g_gating = dot(dgl, x_own, TN)
    for part in range(blocks_x):
        at = part * tasks * experts
        pack_ref[at : at + tasks * experts, :] = g_gating[:, part * 128 : (part + 1) * 128]
    small_ref[:, tasks * tower_hid :] = pack_ref[...].astype(LOW)


    share = share_ref.shape[0]

    def share_rows(part):
        return pl.ds(pl.multiple_of(part * share, share), share)

    def core_copy():
        return pltpu.make_async_remote_copy(
            small_ref.at[pl.ds(pl.multiple_of((1 - side) * 2 * share, share), 2 * share)],
            core_recv,
            s_out.at[0],
            s_in.at[0],
            device_id={"dp": dp, "mp": near},
            device_id_type=MESH,
        )

    def pair_copy():
        return pltpu.make_async_remote_copy(
            pair_send,
            pair_recv,
            s_out.at[1],
            s_in.at[1],
            device_id={"dp": pair, "mp": me},
            device_id_type=MESH,
        )

    def core_sum(part):
        mine = small_ref[share_rows(side * 2 + part), :].astype(F32)
        return mine + core_recv[share_rows(part), :].astype(F32)

    core_copy().start()
    g_b1_ref[...] = jnp.zeros_like(g_b1_ref)

    gate_ref[...] = dot(dgl, wg_ref[...])

    def hand_on(turn):
        rows = rows_of(back_chunk(turn))
        g_help(turn).wait_recv()
        total = dx_send[far, rows].astype(F32) + dx_help[rows].astype(F32)
        dx_sum[rows] = total.astype(LOW)
        g_far(turn).start()

    act = jnp.ones((8, own), LOW)

    def chunk_step(turn, _):
        chunk = back_chunk(turn)
        rows = rows_of(chunk)

        @pl.when(jnp.logical_and(turn < 2, chunk != me))
        def _():
            d_copy(0, chunk).wait_recv()

        @pl.when(turn >= 2)
        def _():
            d_copy(1 + lax.rem(side + turn, 2), chunk).wait_recv()

        total = gate_ref[...] * jnp.where(chunk == me, 1.0, 0.0)
        for e in range(here):
            w_out = w_ref[:, e, in_rows:, :].reshape(out_width, hid)
            dpre = (dot(dy_ref[e, rows, :], w_out) * slope_ref[e, rows, :]).astype(LOW)
            dpre_ref[e, rows, :] = dpre
            g_b1_ref[e] += dot(act, dpre)
            w_in = w_ref[:, e, :in_rows, :].reshape(features, hid)
            total += dot(dpre, w_in, NT)
        for target in range(peers):
            dx_send[target, rows] = total[:, target * width : (target + 1) * width].astype(LOW)
        g_near(turn).start()
        g_help(turn).start()

        @pl.when(turn > 0)
        def _():
            hand_on(turn - 1)

        return 0

    lax.fori_loop(0, peers, chunk_step, 0)
    hand_on(peers - 1)
    core_copy().wait()
    pair_send[...] = core_sum(1 - dp_side).astype(LOW)
    pair_copy().start()

    lanes = parts_ref.shape[4]
    blocks_in = width // 128
    per_in = 128 // in_rows
    per_out = 128 // out_rows
    for e in range(here):

        def in_step(block, _):
            cols = pl.ds(pl.multiple_of(lax.rem(block, blocks_in) * 128, 128), 128)
            x = blocks_ref[lax.div(block, blocks_in), :, cols]
            value = dot(x, dpre_ref[e], TN).astype(LOW)
            for shard in range(per_in):
                for target in range(peers):
                    to = block * per_in + shard
                    away = lax.rem(to + dp, 2)
                    parts_ref[
                        away, lax.div(to, 2), target, e * rows_both : e * rows_both + in_rows, :
                    ] = value[
                        shard * in_rows : (shard + 1) * in_rows, target * lanes : (target + 1) * lanes
                    ]
            return 0

        lax.fori_loop(0, features // 128, in_step, 0)

        def out_step(block, _):
            cols = pl.ds(pl.multiple_of(block * 128, 128), 128)
            value = dot(dy_ref[e, :, cols], hid_ref[e], TN).astype(LOW)
            for shard in range(per_out):
                for target in range(peers):
                    to = block * per_out + shard
                    away = lax.rem(to + dp, 2)
                    parts_ref[
                        away,
                        lax.div(to, 2),
                        target,
                        e * rows_both + in_rows : (e + 1) * rows_both,
                        :,
                    ] = value[
                        shard * out_rows : (shard + 1) * out_rows,
                        target * lanes : (target + 1) * lanes,
                    ]
            return 0

        lax.fori_loop(0, out_width // 128, out_step, 0)

    pair_copy().wait()
    share_ref[...] = (core_sum(dp_side) + pair_recv[...].astype(F32)).astype(LOW)
    for turn in range(peers):
        g_near(turn).wait()
        g_far(turn).wait()
    dx_ref[...] = dx_send[me].astype(F32) + dx_near[...].astype(F32) + dx_far[...].astype(F32)
    for turn in range(peers):
        g_help(turn).wait_send()
        x_far(turn).wait_send()
        x_near(turn).wait_send()
        x_hand(turn).wait_send()
    for relation, device in enumerate((near, far, across)):
        y_copy(0, relation, device).wait_send()
        d_copy(relation, device).wait_send()


def total_kernel(
    features,
    width_out,
    valid_ref,
    inner_ref,
    stats_ref,
    tables_ref,
    shares_ref,
    grads_ref,
    inner_out,
    result_ref,
    pay_ref,
    got_ref,
    t_out,
    t_in,
):
    devices = got_ref.shape[0]
    peers = inner_out.shape[0]
    here, _, hid = inner_ref.shape
    inner_rows = inner_out.shape[1]
    number = stats_ref.shape[0] - 2
    me = lax.axis_index("dp") * peers + lax.axis_index("mp")
    barrier = pltpu.get_barrier_semaphore()

    def place_of(device):
        return {"dp": lax.div(device, peers), "mp": lax.rem(device, peers)}

    def greet(step, _):
        target = lax.rem(me + step, devices)
        pl.semaphore_signal(barrier, inc=1, device_id=place_of(target), device_id_type=MESH)
        return 0

    lax.fori_loop(1, devices, greet, 0)
    lane = lax.broadcasted_iota(I32, (1, 128), 1)

    def whole_sum(value):
        return jnp.sum(jnp.sum(value, axis=0, keepdims=True), axis=1, keepdims=True)

    def grad_step(at, total):
        rows = grads_ref[pl.ds(pl.multiple_of(at * 64, 64), 64), :]
        return total + jnp.sum((rows * rows).reshape(8, 8, 128), axis=0)

    squares = lax.fori_loop(0, grads_ref.shape[0] // 64, grad_step, tables_ref[...])
    share = shares_ref[...]
    vector = jnp.where(lane == 0, stats_ref[number + 1, :1, :1], 0.0)
    vector = jnp.where(lane == 1, stats_ref[number + 1, :1, 1:2], vector)
    for at in range(number + 1):
        vector = jnp.where(lane == at + 2, whole_sum(stats_ref[at]), vector)
    vector = jnp.where(lane == number + 3, whole_sum(squares) + whole_sum(share * share), vector)
    pay_ref[...] = jnp.zeros_like(pay_ref)
    for e in range(here):
        for part in range(hid // 128):
            at = e * (hid // 128) + part
            pay_ref[at : at + 1, :] = inner_ref[e, :1, part * 128 : (part + 1) * 128]
    pay_ref[inner_rows : inner_rows + 1, :] = vector
    got_ref[me] = pay_ref[...]
    pl.semaphore_wait(barrier, devices - 1)

    def t_copy(step):
        target = lax.rem(me + step, devices)
        return pltpu.make_async_remote_copy(
            pay_ref,
            got_ref.at[me],
            t_out.at[step],
            t_in.at[step],
            device_id=place_of(target),
            device_id_type=MESH,
        )

    def start(step, _):
        t_copy(step).start()
        return 0

    def finish(step, _):
        t_copy(step).wait()
        return 0

    lax.fori_loop(1, devices, start, 0)
    lax.fori_loop(1, devices, finish, 0)
    total = jnp.zeros((1, 128), F32)
    inner_sq = jnp.zeros((inner_rows, 128), F32)
    for group in range(peers):
        part = jnp.zeros((inner_rows, 128), F32)
        for block in range(devices // peers):
            source = block * peers + group
            part = part + got_ref[source, :inner_rows, :]
            total = total + got_ref[source, inner_rows : inner_rows + 1, :]
        inner_out[group] = part
        inner_sq = inner_sq + part * part

    def pick(at):
        return jnp.sum(jnp.where(lane == at, total, 0.0), axis=1, keepdims=True)

    weight = pick(1)
    grad_norm = jnp.sqrt(pick(number + 3) + whole_sum(inner_sq)) / weight
    factor = jnp.minimum(1.0, clip_max / grad_norm) / weight
    count = valid_ref[0].astype(F32)
    width = jnp.where(lane == number + 2, float(features), float(width_out))
    result_ref[...] = jnp.zeros_like(result_ref)
    result_ref[0:1, :] = jnp.broadcast_to(factor, (1, 128))
    result_ref[1:2, :] = jnp.broadcast_to(grad_norm, (1, 128))
    result_ref[2:3, :] = total
    result_ref[3:4, :] = jnp.sqrt(total / (count * width) + stat_eps)


def table_kernel(factor_ref, weight_ref, first_ref, second_ref, grad_ref, *outs):
    pair, width, rows = weight_ref.shape
    gradient = grad_ref[0].T.reshape(pair, width, rows) * factor_ref[:1, :1].reshape(1, 1, 1)
    results = adamw(weight_ref[...], first_ref[...], second_ref[...], gradient, rate_table)
    for out, result in zip(outs, results):
        out[...] = result


def body(
    row_ids,
    counts,
    labels,
    label_mask,
    embeddings,
    embed_first,
    embed_second,
    expert_in,
    in_first,
    in_second,
    expert_out,
    out_first,
    out_second,
    gating,
    gating_first,
    gating_second,
    towers,
    towers_first,
    towers_second,
    heads,
    heads_first,
    heads_second,
    biases,
    biases_first,
    biases_second,
):
    devices = lax.axis_size(AXES)
    mp_count = lax.axis_size("mp")
    dp_count = lax.axis_size("dp")
    mp_index = lax.axis_index("mp")
    samples, tables_here = row_ids.shape
    tables, rows_dev, d_emb = embeddings.shape
    own = samples // mp_count
    requests = samples * tables_here
    capacity = 2 * requests // devices
    height = capacity // 2
    slots = devices * height
    row_bits = rows_dev.bit_length() - 1
    pairs = tables // 2
    lanes = 2 * d_emb
    group_rows = tables_here // 2 * rows_dev
    in_rows, out_rows = expert_in.shape[0], expert_out.shape[0]
    experts_here = EXPERTS // mp_count
    hid = expert_in.shape[2] * mp_count
    features = tables * d_emb
    width_out = out_rows * dp_count
    tower_hid = towers.shape[1] // TASKS

    outgoing, place, slot, source = pl.pallas_call(
        functools.partial(route_kernel, row_bits),
        out_shape=(
            jax.ShapeDtypeStruct((devices, 1, capacity), I32),
            jax.ShapeDtypeStruct((tables_here, samples), I32),
            jax.ShapeDtypeStruct((tables_here, samples), I32),
            jax.ShapeDtypeStruct((tables_here, samples), I32),
        ),
        in_specs=[VMEM],
        out_specs=(VMEM,) * 4,
        compiler_params=params(32),
        name="route",
    )(row_ids.T)
    in_out_rows = in_rows + out_rows
    hid_here = hid // mp_count
    shard = jnp.concatenate([expert_in, expert_out], axis=0).astype(LOW).transpose(1, 0, 2)

    def sems(*shape):
        return pltpu.SemaphoreType.DMA(shape)

    codes, shard = pl.pallas_call(
        ask_kernel,
        out_shape=(
            jax.ShapeDtypeStruct((devices, 1, capacity), I32),
            jax.ShapeDtypeStruct((experts_here, in_out_rows, hid), LOW),
        ),
        in_specs=[VMEM, VMEM],
        out_specs=(VMEM, VMEM),
        scratch_shapes=[sems(devices), sems(devices), sems(mp_count), sems(mp_count)],
        compiler_params=pltpu.CompilerParams(
            vmem_limit_bytes=16 * MIB, collective_id=2, has_side_effects=True
        ),
        name="ask",
    )(outgoing, shard)
    expert_w = lax.all_gather(shard, "dp", axis=0, tiled=False)
    codes = codes.reshape(devices, capacity)
    asked = codes[:, 0] >> 16
    plain = codes & 65535
    found_at = jnp.maximum(plain - 1, 0)
    table_at = found_at >> row_bits
    sum_at = (table_at >> 1) * rows_dev + (found_at & (rows_dev - 1))
    number = jnp.arange(capacity, dtype=I32)[None, :]
    part_at = ((number & 1) * 2 + (table_at & 1)) * slots + (number >> 1)
    part_at = part_at + jnp.arange(devices, dtype=I32)[:, None] * height
    part_at = jnp.where(plain > 0, part_at, 4 * slots)

    table_view = jnp.transpose(embeddings, (0, 2, 1))
    found = pl.pallas_call(
        functools.partial(find_kernel, mp_count),
        grid=(mp_count,),
        out_shape=jax.ShapeDtypeStruct((dp_count, mp_count, height, lanes), LOW),
        in_specs=[
            SMEM,
            SMEM,
            pl.BlockSpec((tables_here, d_emb, rows_dev), lambda m: (m, 0, 0)),
        ],
        out_specs=pl.BlockSpec((dp_count, 1, height, lanes), lambda m: (0, m, 0, 0)),
        scratch_shapes=[
            pltpu.VMEM((tables_here * rows_dev, lanes), F32),
            pltpu.VMEM((height, lanes), F32),
        ],
        compiler_params=params(60),
        name="find",
    )(found_at.reshape(-1), asked, table_view)
    returned = lax.all_to_all(
        found.reshape(devices, height, lanes), AXES, split_axis=0, concat_axis=0, tiled=True
    )
    embedded = pl.pallas_call(
        place_kernel,
        out_shape=jax.ShapeDtypeStruct((samples, tables_here * d_emb), LOW),
        in_specs=[SMEM, VMEM],
        out_specs=VMEM,
        scratch_shapes=[
            pltpu.VMEM((2 * slots, lanes), F32),
            pltpu.VMEM((tables_here // 2, samples, lanes), F32),
        ],
        compiler_params=params(32),
        name="place",
    )(place.reshape(-1), returned.reshape(slots, lanes))

    first = EXPERTS * hid
    second = first + EXPERTS * width_out
    third = second + TASKS * EXPERTS
    fourth = third + TASKS * tower_hid
    inner_here = lax.dynamic_index_in_dim(
        biases[:first].reshape(mp_count, experts_here, 1, hid), mp_index, 0, keepdims=False
    )
    outer_here = lax.dynamic_index_in_dim(
        biases[first:second].reshape(mp_count, experts_here, 1, width_out),
        mp_index,
        0,
        keepdims=False,
    )
    gating_low = gating.T.astype(LOW)
    all_gates = TASKS * EXPERTS
    pack_rows = width_out

    def scratch(shape, kind=F32):
        return pltpu.VMEM(shape, kind)

    pack_shape = (pack_rows // 4, TASKS * tower_hid + 128)
    x_shape = (samples, tables_here * d_emb)
    stat_parts, embed_grad, grad_parts, inner_parts, share = pl.pallas_call(
        dense_kernel,
        out_shape=(
            jax.ShapeDtypeStruct((EXPERTS + TASKS + 2, 8, width_out), F32),
            jax.ShapeDtypeStruct(x_shape, F32),
            jax.ShapeDtypeStruct(
                (2, dp_count // 2, mp_count, experts_here * in_out_rows, hid_here), LOW
            ),
            jax.ShapeDtypeStruct((experts_here, 8, hid), F32),
            jax.ShapeDtypeStruct(pack_shape, LOW),
        ),
        in_specs=[SMEM] + [VMEM] * 9 + [SMEM] + [VMEM] * 2,
        out_specs=(VMEM,) * 5,
        scratch_shapes=[
            scratch((mp_count,) + x_shape, LOW),
            scratch((experts_here, samples, hid), LOW),
            scratch((experts_here, samples, hid)),
            scratch((experts_here, samples, width_out), LOW),
            scratch((mp_count, experts_here, own, width_out), LOW),
            scratch((mp_count, experts_here, own, width_out), LOW),
            scratch((own, all_gates)),
            scratch((TASKS, own, width_out), LOW),
            scratch((TASKS, own, width_out)),
            scratch((own, all_gates)),
            scratch((EXPERTS, own, width_out), LOW),
            scratch((pack_rows, TASKS * tower_hid + 128), LOW),
            scratch((pack_rows, 128)),
            scratch((own, hid)),
            scratch((own, features)),
            scratch((experts_here, samples, hid), LOW),
            scratch((mp_count,) + x_shape, LOW),
            scratch(x_shape, LOW),
            scratch(x_shape, LOW),
            scratch(x_shape, LOW),
            scratch(x_shape, LOW),
            scratch((2 * pack_shape[0], pack_shape[1]), LOW),
            scratch(pack_shape, LOW),
            scratch(pack_shape, LOW),
            sems(3, mp_count),
            sems(3, mp_count),
            sems(3),
            sems(3),
            sems(3),
            sems(3),
            sems(3, mp_count),
            sems(3, mp_count),
            sems(2),
            sems(2),
        ],
        compiler_params=pltpu.CompilerParams(
            vmem_limit_bytes=60 * MIB, collective_id=0, has_side_effects=True
        ),
        name="dense",
    )(
        lax.dynamic_slice_in_dim(counts, lax.axis_index("dp"), 1, 0),
        embedded,
        expert_w,
        inner_here,
        outer_here,
        gating_low,
        biases[second:third].reshape(1, all_gates),
        towers.astype(LOW),
        biases[third:fourth].reshape(TASKS, tower_hid),
        heads,
        biases[fourth:].reshape(1, TASKS),
        labels,
        label_mask,
    )

    back_rows = pl.pallas_call(
        send_kernel,
        out_shape=jax.ShapeDtypeStruct((slots, lanes), LOW),
        in_specs=[SMEM, SMEM, VMEM],
        out_specs=VMEM,
        scratch_shapes=[
            pltpu.VMEM((tables_here // 2, 2 * samples, lanes), F32),
            pltpu.VMEM((2 * slots, lanes), F32),
        ],
        compiler_params=params(32),
        name="send",
    )(slot.reshape(-1), source.reshape(-1), embed_grad)
    share = share.reshape(devices // 4, pack_rows // devices, -1)
    arrived, shares = pl.pallas_call(
        swap_kernel,
        out_shape=(
            jax.ShapeDtypeStruct((devices, height, lanes), LOW),
            jax.ShapeDtypeStruct(share.shape, LOW),
        ),
        in_specs=[VMEM, VMEM],
        out_specs=(VMEM, VMEM),
        scratch_shapes=[sems(devices), sems(devices), sems(devices // 4), sems(devices // 4)],
        compiler_params=pltpu.CompilerParams(
            vmem_limit_bytes=16 * MIB, collective_id=3, has_side_effects=True
        ),
        name="swap",
    )(back_rows.reshape(devices, height, lanes), share)
    def exchange_all(parts):
        return lax.all_to_all(parts, AXES, split_axis=0, concat_axis=0, tiled=True)

    share = jnp.sum(shares.astype(F32), axis=0)
    whole = lax.all_gather(share.astype(LOW), AXES, axis=0, tiled=False)

    partner = lax.ppermute(grad_parts[1], "dp", [(d, d ^ 1) for d in range(dp_count)])
    partner, arrived = lax.optimization_barrier((partner, arrived))
    grad_parts = (grad_parts[0].astype(F32) + partner.astype(F32)).astype(LOW)
    sides = [
        [d * mp_count + m for d in range(x, dp_count, 2) for m in range(mp_count)] for x in range(2)
    ]
    grad_parts = lax.all_to_all(
        grad_parts.reshape(devices // 2, experts_here * in_out_rows, hid_here),
        AXES,
        split_axis=0,
        concat_axis=0,
        axis_index_groups=sides,
        tiled=True,
    )
    grad_sum = jnp.sum(
        grad_parts.reshape(dp_count // 2, mp_count, experts_here, in_out_rows, -1).astype(F32), 0
    )
    owned = grad_sum.reshape(EXPERTS, in_out_rows, -1).transpose(1, 0, 2)
    in_sum, out_sum = owned[:in_rows], owned[in_rows:]

    table_grad, table_sq = pl.pallas_call(
        functools.partial(add_kernel, mp_count),
        out_shape=(
            jax.ShapeDtypeStruct((pairs * rows_dev, lanes), F32),
            jax.ShapeDtypeStruct((8, lanes), F32),
        ),
        in_specs=[SMEM, SMEM, SMEM, VMEM],
        out_specs=(pl.BlockSpec(memory_space=pl.ANY), VMEM),
        scratch_shapes=[
            pltpu.VMEM((4 * slots + 8, lanes), F32),
            pltpu.SemaphoreType.DMA((mp_count,)),
        ]
        + [pltpu.VMEM((group_rows, lanes), F32)] * mp_count,
        compiler_params=params(60),
        name="add",
    )(sum_at.reshape(-1), part_at.reshape(-1), asked, arrived.reshape(slots, lanes))

    stat_end = EXPERTS + TASKS
    inner_rows = experts_here * hid // 128
    pay_rows = inner_rows + 8
    inner_sum, result = pl.pallas_call(
        functools.partial(total_kernel, features, width_out),
        out_shape=(
            jax.ShapeDtypeStruct((mp_count, inner_rows, 128), F32),
            jax.ShapeDtypeStruct((8, 128), F32),
        ),
        in_specs=[SMEM] + [VMEM] * 5,
        out_specs=(VMEM,) * 2,
        scratch_shapes=[
            scratch((pay_rows, 128)),
            scratch((devices, pay_rows, 128)),
            sems(devices),
            sems(devices),
        ],
        compiler_params=pltpu.CompilerParams(
            vmem_limit_bytes=16 * MIB, collective_id=4, has_side_effects=True
        ),
        name="total",
    )(
        jnp.sum(counts).reshape(1),
        inner_parts,
        stat_parts,
        table_sq,
        share,
        grad_sum.reshape(-1, 128),
    )
    factor = result[0, 0]

    table_spec = pl.BlockSpec((2, d_emb, rows_dev), lambda p: (p, 0, 0))
    embed_out = pl.pallas_call(
        table_kernel,
        grid=(pairs,),
        out_shape=(jax.ShapeDtypeStruct(table_view.shape, F32),) * 3,
        in_specs=[
            pl.BlockSpec((8, 128), lambda p: (0, 0)),
            table_spec,
            table_spec,
            table_spec,
            pl.BlockSpec((1, rows_dev, lanes), lambda p: (p, 0, 0)),
        ],
        out_specs=(table_spec,) * 3,
        compiler_params=params(58),
        name="tables",
    )(
        result,
        table_view,
        jnp.transpose(embed_first, (0, 2, 1)),
        jnp.transpose(embed_second, (0, 2, 1)),
        table_grad.reshape(pairs, rows_dev, lanes),
    )
    embed_out = [jnp.transpose(value, (0, 2, 1)) for value in embed_out]
    in_out = adamw(expert_in, in_first, in_second, in_sum * factor, rate_dense)
    out_out = adamw(expert_out, out_first, out_second, out_sum * factor, rate_dense)
    whole, embed_out = lax.optimization_barrier((whole, embed_out))
    whole = whole.reshape(dp_count // 2, 2, mp_count // 2, 2, pack_rows // devices, -1)
    whole = whole.transpose(3, 1, 0, 2, 4, 5).reshape(pack_rows, -1)
    towers_sum = whole[:, : TASKS * tower_hid].astype(F32)
    packed = whole[:, TASKS * tower_hid :].astype(F32)
    blocks_x = features // 128
    heads_at = blocks_x * all_gates
    tower_at = heads_at + TASKS * tower_hid // 128
    outer_at = tower_at + TASKS * tower_hid // 128
    rest_at = outer_at + EXPERTS * width_out // 128
    gating_sum = packed[:heads_at].reshape(blocks_x, all_gates, 128).transpose(1, 0, 2)
    gating_sum = gating_sum.reshape(all_gates, features).T
    heads_sum = packed[heads_at:tower_at].reshape(TASKS, tower_hid)
    bias_sum = jnp.concatenate(
        [
            inner_sum.reshape(-1),
            packed[outer_at:rest_at].reshape(-1),
            packed[rest_at, :all_gates],
            packed[tower_at:outer_at].reshape(-1),
            packed[rest_at + 1, :TASKS],
        ]
    )
    gating_out = adamw(gating, gating_first, gating_second, gating_sum * factor, rate_dense)
    towers_out = adamw(towers, towers_first, towers_second, towers_sum * factor, rate_dense)
    heads_out = adamw(heads, heads_first, heads_second, heads_sum * factor, rate_dense)
    biases_out = adamw(biases, biases_first, biases_second, bias_sum * factor, rate_dense)
    stats = jnp.concatenate([result[3, stat_end + 2][None], result[3, 2 : stat_end + 2]])
    loss = result[2, :2]
    return (
        *embed_out,
        *in_out,
        in_out[0].astype(LOW),
        *out_out,
        out_out[0].astype(LOW),
        *gating_out,
        *towers_out,
        *heads_out,
        *biases_out,
        result[1, :1],
        loss,
        stats,
    )


def solution(mesh):
    rows = P(None, AXES, None)
    expert = P("dp", None, "mp")
    sample = P(AXES, None)
    placed = (P("dp", "mp"), P(), sample, sample) + (rows,) * 3 + (expert,) * 6 + (P(),) * 12
    results = (rows,) * 3 + (expert,) * 8 + (P(),) * 15
    return jax.shard_map(body, mesh=mesh, in_specs=placed, out_specs=results, check_vma=False)
```

```python
import functools
import math

import jax
import jax.numpy as jnp
from jax import lax
from jax.experimental import pallas as pl
from jax.experimental.pallas import tpu as pltpu
from jax.sharding import PartitionSpec as P

EXPERTS = 8
TASKS = 5
STEP = 3

HIGH = lax.Precision.HIGHEST
beta_one = 0.5
beta_two = 0.5
adam_eps = 1e-08
decay = 0.01
clip_max = 0.002
rate_table = 0.5
rate_dense = 0.02
stat_eps = 1e-06

LOW = jnp.bfloat16
F32 = jnp.float32
I32 = jnp.int32
MIB = 1024 * 1024
AXES = ("dp", "mp")


def params(mib):
    return pltpu.CompilerParams(vmem_limit_bytes=mib * MIB)


VMEM = pl.BlockSpec(memory_space=pltpu.VMEM)
SMEM = pl.BlockSpec(memory_space=pltpu.SMEM)


def adamw(weight, first, second, gradient, rate):
    first_next = beta_one * first + (1.0 - beta_one) * gradient
    second_next = beta_two * second + (1.0 - beta_two) * gradient * gradient
    corrected = first_next / (1.0 - beta_one**STEP)
    scaled = jnp.sqrt(second_next / (1.0 - beta_two**STEP))
    return (
        weight - rate * (corrected / (scaled + adam_eps) + decay * weight),
        first_next,
        second_next,
    )


def route_kernel(row_bits, ids_ref, out_ref, place_ref, slot_ref, from_ref):
    devices, _, capacity = out_ref.shape
    tables, samples = ids_ref.shape
    rows_dev = 1 << row_bits
    halves = devices * capacity // 2
    width = 256
    upper = (
        lax.broadcasted_iota(I32, (width, width), 0) <= lax.broadcasted_iota(I32, (width, width), 1)
    ).astype(LOW)
    owners = lax.broadcasted_iota(I32, (devices, width), 0)
    slots = lax.broadcasted_iota(I32, (capacity, width), 0)
    carry = jnp.zeros((devices, 1), F32)
    total = jnp.zeros((2 * devices, capacity), F32)
    for table in range(tables):
        parity = table % 2
        for part in range(samples // width):
            cols = pl.ds(part * width, width)
            ids = ids_ref[pl.ds(table, 1), cols]
            owner = ids >> row_bits
            code = table * rows_dev + (ids & (rows_dev - 1)) + 1
            onehot = (owner == owners).astype(F32)
            counted = jnp.dot(onehot.astype(LOW), upper, preferred_element_type=F32) + carry
            rank = jnp.sum(onehot * counted, axis=0, keepdims=True).astype(I32) - 1
            carry = counted[:, width - 1 :]
            at_slot = (rank == slots).astype(LOW)
            high = (code >> 7).astype(F32)
            low = (code & 127).astype(F32)
            pieces = jnp.concatenate([onehot * high, onehot * low], axis=0).astype(LOW)
            total += lax.dot_general(
                pieces, at_slot, (((1,), (1,)), ((), ())), preferred_element_type=F32
            )
            row = owner * (capacity // 2) + (rank >> 1)
            half = rank & 1
            place_ref[pl.ds(table, 1), cols] = (half ^ parity) * halves + row
            slot_ref[pl.ds(table, 1), cols] = half * halves + row
            sample = lax.broadcasted_iota(I32, (1, width), 1) + part * width
            from_ref[pl.ds(table, 1), cols] = (half ^ parity) * samples + sample
    codes = (total[:devices] * 128.0 + total[devices:]).astype(I32)
    first = lax.broadcasted_iota(I32, (devices, capacity), 1) == 0
    counted = jnp.where(first, carry * 65536.0, 0.0).astype(I32)
    out_ref[...] = (codes + counted).reshape(devices, 1, capacity)


def left_lanes(shape):
    return lax.broadcasted_iota(I32, shape, len(shape) - 1) < 64


def find_kernel(groups, at_ref, counts_ref, table_ref, out_ref, turned_ref, rows_ref):
    blocks, _, height, lanes = out_ref.shape
    tables, width, rows_dev = table_ref.shape
    group = pl.program_id(0)
    left = left_lanes((1, lanes))
    part = 512

    def turn_step(step, _):
        table = lax.div(step, rows_dev // part)
        first = pl.multiple_of(lax.rem(step, rows_dev // part) * part, part)
        columns = table_ref[table, :, pl.ds(first, part)]
        there = pl.ds(pl.multiple_of(step * part, part), part)
        turned_ref[there, :] = jnp.concatenate([columns, columns], axis=0).T
        return 0

    lax.fori_loop(0, tables * (rows_dev // part), turn_step, 0)

    def block_step(block, _):
        source = block * groups + group
        base = source * 2 * height

        def step(outer, _):
            got = []
            for inner in range(8):
                at = outer * 8 + inner
                even = turned_ref[pl.ds(at_ref[base + 2 * at], 1), :]
                odd = turned_ref[pl.ds(at_ref[base + 2 * at + 1], 1), :]
                got.append((at, jnp.where(left, even, odd)))
            for at, row in got:
                rows_ref[pl.ds(at, 1), :] = row
            return 0

        lax.fori_loop(0, (counts_ref[source] + 15) // 16, step, 0)
        out_ref[block, 0] = rows_ref[...].astype(LOW)
        return 0

    lax.fori_loop(0, blocks, block_step, 0)


def place_kernel(place_ref, rows_ref, out_ref, both_ref, flat_ref):
    count, lanes = rows_ref.shape
    samples = out_ref.shape[0]
    tables = place_ref.shape[0] // samples
    rows = rows_ref[...].astype(F32)
    both_ref[pl.ds(0, count), :] = rows
    both_ref[pl.ds(count, count), :] = pltpu.roll(rows, 64, 1)
    left = left_lanes((1, lanes))

    def step(outer, _):
        got = []
        for inner in range(8):
            sample = outer * 8 + inner
            for pair in range(tables // 2):
                even = both_ref[pl.ds(place_ref[2 * pair * samples + sample], 1), :]
                odd = both_ref[pl.ds(place_ref[(2 * pair + 1) * samples + sample], 1), :]
                got.append((pair, sample, jnp.where(left, even, odd)))
        for pair, sample, row in got:
            flat_ref[pair, pl.ds(sample, 1), :] = row
        return 0

    lax.fori_loop(0, samples // 8, step, 0)
    for pair in range(tables // 2):
        out_ref[:, pair * lanes : (pair + 1) * lanes] = flat_ref[pair].astype(LOW)


def send_kernel(slot_ref, from_ref, grad_ref, out_ref, both_ref, rows_ref):
    count, lanes = out_ref.shape
    samples = grad_ref.shape[0]
    tables = slot_ref.shape[0] // samples
    for pair in range(tables // 2):
        rows = grad_ref[:, pair * lanes : (pair + 1) * lanes]
        both_ref[pair, pl.ds(0, samples), :] = rows
        both_ref[pair, pl.ds(samples, samples), :] = pltpu.roll(rows, 64, 1)

    def step(outer, _):
        got = []
        for inner in range(8):
            sample = outer * 8 + inner
            for table in range(tables):
                row = both_ref[table // 2, pl.ds(from_ref[table * samples + sample], 1), :]
                got.append((slot_ref[table * samples + sample], row))
        for slot, row in got:
            rows_ref[pl.ds(slot, 1), :] = row
        return 0

    lax.fori_loop(0, samples // 8, step, 0)
    left = left_lanes((count, lanes))
    out_ref[...] = jnp.where(
        left, rows_ref[pl.ds(0, count), :], rows_ref[pl.ds(count, count), :]
    ).astype(LOW)


def swap_kernel(rows_ref, share_ref, out_ref, shares_ref, r_out, r_in, s_out, s_in):
    devices = rows_ref.shape[0]
    groups = share_ref.shape[0]
    peers = lax.axis_size("mp")
    dp, mp = lax.axis_index("dp"), lax.axis_index("mp")
    mine = lax.div(dp, 2) * (peers // 2) + lax.div(mp, 2)
    me = dp * peers + mp
    greet_all(devices, peers, me)

    def r_copy(step):
        target = lax.rem(me + step, devices)
        return pltpu.make_async_remote_copy(
            rows_ref.at[target],
            out_ref.at[me],
            r_out.at[step],
            r_in.at[step],
            device_id=place_of(target, peers),
            device_id_type=MESH,
        )

    def s_copy(step):
        target = lax.rem(mine + step, groups)
        to_dp = lax.div(target, peers // 2) * 2 + lax.rem(dp, 2)
        to_mp = lax.rem(target, peers // 2) * 2 + lax.rem(mp, 2)
        return pltpu.make_async_remote_copy(
            share_ref.at[target],
            shares_ref.at[mine],
            s_out.at[step],
            s_in.at[step],
            device_id={"dp": to_dp, "mp": to_mp},
            device_id_type=MESH,
        )

    def loop(first, copies, act):
        def step(at, _):
            act(copies(at))
            return 0

        lax.fori_loop(1, first, step, 0)

    loop(devices, r_copy, lambda copy: copy.start())
    loop(groups, s_copy, lambda copy: copy.start())
    out_ref[me] = rows_ref[me]
    shares_ref[mine] = share_ref[mine]
    loop(groups, s_copy, lambda copy: copy.wait())
    loop(devices, r_copy, lambda copy: copy.wait())


def add_kernel(
    groups, at_ref, part_at_ref, counts_ref, rows_ref, out_ref, square_ref, parts_ref, sems, *sums
):
    count, lanes = rows_ref.shape
    sources = counts_ref.shape[0]
    height = count // sources
    table_rows = sums[0].shape[0]
    left = left_lanes((count, lanes))
    rows = rows_ref[...].astype(F32)
    turned = pltpu.roll(rows, 64, 1)
    parts_ref[pl.ds(0, count), :] = jnp.where(left, rows, 0.0)
    parts_ref[pl.ds(count, count), :] = jnp.where(left, 0.0, turned)
    parts_ref[pl.ds(2 * count, count), :] = jnp.where(left, turned, 0.0)
    parts_ref[pl.ds(3 * count, count), :] = jnp.where(left, 0.0, rows)
    parts_ref[pl.ds(4 * count, 8), :] = jnp.zeros((8, lanes), F32)

    def clear(at, _):
        for table in sums:
            table[pl.ds(pl.multiple_of(at * 64, 64), 64), :] = jnp.zeros((64, lanes), F32)
        return 0

    lax.fori_loop(0, table_rows // 64, clear, 0)

    def block_step(block, _):
        most = counts_ref[block * groups]
        for group in range(1, groups):
            most = jnp.maximum(most, counts_ref[block * groups + group])

        def step(outer, _):
            for inner in range(4):
                got = []
                for group in range(groups):
                    at = (block * groups + group) * 2 * height + outer * 4 + inner
                    here = pl.ds(at_ref[at], 1)
                    part = pl.ds(part_at_ref[at], 1)
                    got.append((here, sums[group][here, :] + parts_ref[part, :]))
                for group, (here, row) in enumerate(got):
                    sums[group][here, :] = row
            return 0

        lax.fori_loop(0, (most + 3) // 4, step, 0)
        return 0

    lax.fori_loop(0, sources // groups, block_step, 0)
    copies = [
        pltpu.make_async_copy(
            sums[group], out_ref.at[pl.ds(group * table_rows, table_rows)], sems.at[group]
        )
        for group in range(groups)
    ]
    for copy in copies:
        copy.start()

    def square(at, total):
        for table in sums:
            rows = table[pl.ds(pl.multiple_of(at * 64, 64), 64), :]
            total = total + jnp.sum((rows * rows).reshape(8, 8, lanes), axis=0)
        return total

    square_ref[...] = lax.fori_loop(0, table_rows // 64, square, jnp.zeros((8, lanes), F32))
    for copy in copies:
        copy.wait()


def gelu_parts(value):
    scale = math.sqrt(2.0 / math.pi)
    square = value * value
    bend = jnp.tanh(scale * value * (1.0 + 0.044715 * square))
    half = 0.5 * (1.0 + bend)
    slope = half + 0.5 * value * (1.0 - bend * bend) * (scale * (1.0 + 3 * 0.044715 * square))
    return value * half, slope


def dot(a, b, axes=((1,), (0,)), precision=None):
    return lax.dot_general(
        a, b, (axes, ((), ())), preferred_element_type=F32, precision=precision
    )


NT = ((1,), (1,))
TN = ((0,), (0,))
MESH = pl.DeviceIdType.MESH


def meet(peers, partner=None):
    me = lax.axis_index("mp")
    barrier = pltpu.get_barrier_semaphore()
    if partner is not None:
        pl.semaphore_signal(
            barrier, inc=1, device_id={"dp": partner, "mp": me}, device_id_type=MESH
        )
    for step in range(1, peers):
        pl.semaphore_signal(
            barrier, inc=1, device_id={"mp": lax.rem(me + step, peers)}, device_id_type=MESH
        )
    pl.semaphore_wait(barrier, peers - 1 + (partner is not None))
    return me


def greet_all(devices, peers, me):
    barrier = pltpu.get_barrier_semaphore()

    def greet(step, _):
        target = lax.rem(me + step, devices)
        pl.semaphore_signal(
            barrier, inc=1, device_id=place_of(target, peers), device_id_type=MESH
        )
        return 0

    lax.fori_loop(1, devices, greet, 0)
    pl.semaphore_wait(barrier, devices - 1)


def place_of(device, peers):
    return {"dp": lax.div(device, peers), "mp": lax.rem(device, peers)}


def ask_kernel(codes_ref, shard_ref, out_ref, full_ref, c_out, c_in, w_out, w_in):
    devices = codes_ref.shape[0]
    here, _, full = full_ref.shape
    width = shard_ref.shape[2]
    peers = full // width
    mp = lax.axis_index("mp")
    me = lax.axis_index("dp") * peers + mp
    columns = pl.ds(pl.multiple_of(mp * width, width), width)
    full_ref[:, :, columns] = shard_ref[pl.ds(mp * here, here)]
    out_ref[me] = codes_ref[me]
    greet_all(devices, peers, me)

    def c_copy(step):
        target = lax.rem(me + step, devices)
        return pltpu.make_async_remote_copy(
            codes_ref.at[target],
            out_ref.at[me],
            c_out.at[step],
            c_in.at[step],
            device_id=place_of(target, peers),
            device_id_type=MESH,
        )

    def w_copy(step):
        target = lax.rem(mp + step, peers)
        return pltpu.make_async_remote_copy(
            shard_ref.at[pl.ds(target * here, here)],
            full_ref.at[:, :, columns],
            w_out.at[step],
            w_in.at[step],
            device_id={"mp": target},
            device_id_type=MESH,
        )

    def start(step, _):
        c_copy(step).start()
        return 0

    def finish(step, _):
        c_copy(step).wait()
        return 0

    lax.fori_loop(1, devices, start, 0)
    for step in range(1, peers):
        w_copy(step).start()
    lax.fori_loop(1, devices, finish, 0)
    for step in range(1, peers):
        w_copy(step).wait()


def dense_kernel(
    lines,
    *refs,
):
    mine, theirs = refs[:lines], refs[lines : 2 * lines]
    dense_part(mine, theirs, *refs[2 * lines :])


def dense_part(
    mine_refs,
    theirs_refs,
    count_ref,
    x_ref,
    b1_ref,
    b2_ref,
    wg_ref,
    bg_ref,
    w3_ref,
    tb1_ref,
    heads_ref,
    tb2_ref,
    labels_ref,
    mask_ref,
    stats_ref,
    dx_ref,
    parts_ref,
    g_b1_ref,
    share_ref,
    w_ref,
    blocks_ref,
    hid_ref,
    slope_ref,
    dy_ref,
    y_send,
    y_ref,
    gates_ref,
    mixb_ref,
    dmix_ref,
    dg_ref,
    dy_send,
    small_ref,
    pack_ref,
    act_ref,
    gate_ref,
    dpre_ref,
    dx_send,
    dx_near,
    dx_help,
    dx_sum,
    dx_far,
    core_recv,
    pair_send,
    pair_recv,
    x_out,
    x_in,
    y_out,
    y_in,
    d_out,
    d_in,
    g_out,
    g_in,
    s_out,
    s_in,
    w_in_sem,
):
    peers, samples, width = blocks_ref.shape
    here = hid_ref.shape[0]
    out_width = y_ref.shape[3]
    own = y_ref.shape[2]
    experts = peers * here
    tasks, tower_hid = heads_ref.shape
    shards, hid = w_ref.shape[0], w_ref.shape[3]
    in_rows = peers * width // shards
    rows_both = w_ref.shape[2]
    out_rows = rows_both - in_rows
    features = peers * width
    dp = lax.axis_index("dp")
    dp_side = lax.rem(dp, 2)
    pair = dp + 1 - 2 * dp_side
    lines = len(mine_refs)
    w_copies = []
    for at in range(lines):
        first = lax.rem(lax.div(dp, 2) + lines - at, lines) * 2
        w_copies += [
            pltpu.make_async_copy(
                mine_refs[at], w_ref.at[first + dp_side], w_in_sem.at[0, at]
            ),
            pltpu.make_async_copy(
                theirs_refs[at], w_ref.at[first + 1 - dp_side], w_in_sem.at[1, at]
            ),
        ]
    for copy in w_copies:
        copy.start()
    me = meet(peers, pair)
    side = lax.rem(me, 2)
    chip = lax.div(me, 2)
    near = me + 1 - 2 * side
    far = lax.rem(me + 2, peers)
    across = lax.rem(near + 2, peers)

    def rows_of(chunk):
        return pl.ds(pl.multiple_of(chunk * own, own), own)

    def ahead_chunk(turn):
        return lax.rem(2 * chip + 2 + turn, peers)

    def back_chunk(turn):
        return lax.rem(2 * chip + turn, peers)

    def remote(source, target, out_sem, in_sem, device):
        return pltpu.make_async_remote_copy(
            source, target, out_sem, in_sem, device_id={"dp": dp, "mp": device}, device_id_type=MESH
        )

    def x_far(turn):
        rows = rows_of(back_chunk(turn))
        return remote(
            x_ref.at[rows], blocks_ref.at[me, rows], x_out.at[0, turn], x_in.at[0, turn], far
        )

    def x_near(turn):
        rows = rows_of(ahead_chunk(turn))
        return remote(
            x_ref.at[rows], blocks_ref.at[me, rows], x_out.at[1, turn], x_in.at[1, turn], near
        )

    def x_hand(turn):
        rows = rows_of(ahead_chunk(turn))
        block = blocks_ref.at[far, rows]
        return remote(block, block, x_out.at[2, turn], x_in.at[2, turn], near)

    def y_copy(turn, relation, device):
        return remote(
            y_send.at[turn], y_ref.at[me], y_out.at[relation], y_in.at[relation], device
        )

    def d_copy(relation, device):
        return remote(
            dy_send.at[pl.ds(device * here, here)],
            dy_ref.at[:, rows_of(me), :],
            d_out.at[relation],
            d_in.at[relation],
            device,
        )

    def g_near(turn):
        rows = rows_of(back_chunk(turn))
        return remote(
            dx_send.at[near, rows], dx_near.at[rows], g_out.at[0, turn], g_in.at[0, turn], near
        )

    def g_help(turn):
        rows = rows_of(back_chunk(turn))
        return remote(
            dx_send.at[across, rows], dx_help.at[rows], g_out.at[1, turn], g_in.at[1, turn], near
        )

    def g_far(turn):
        rows = rows_of(back_chunk(turn))
        return remote(
            dx_sum.at[rows], dx_far.at[rows], g_out.at[2, turn], g_in.at[2, turn], far
        )

    for turn in range(peers):
        x_far(turn).start()
        x_near(turn).start()
    blocks_ref[me] = x_ref[...]
    limit = count_ref[0]
    for copy in w_copies:
        copy.wait()

    x_far(0).wait_recv()
    x_hand(0).start()

    def expert_step(turn, _):
        x_near(turn).wait_recv()
        x_hand(turn).wait_recv()

        @pl.when(turn < peers - 1)
        def _():
            x_far(turn + 1).wait_recv()
            x_hand(turn + 1).start()

        chunk = ahead_chunk(turn)
        rows = rows_of(chunk)
        x = jnp.concatenate([blocks_ref[block, rows] for block in range(peers)], axis=1)
        for e in range(here):
            w_in = w_ref[:, e, :in_rows, :].reshape(peers * width, hid)
            act_ref[...] = dot(x, w_in) + b1_ref[e]

            def gelu_step(tile, _):
                at = pl.multiple_of(tile * 32, 32)
                value, slope = gelu_parts(act_ref[pl.ds(at, 32), :])
                there = pl.ds(pl.multiple_of(chunk * own + at, 32), 32)
                hid_ref[e, there, :] = value.astype(LOW)
                slope_ref[e, there, :] = slope
                return 0

            lax.fori_loop(0, own // 32, gelu_step, 0)
            w_out = w_ref[:, e, in_rows:, :].reshape(out_width, hid)
            y_send[turn, e] = (dot(hid_ref[e, rows, :], w_out, NT) + b2_ref[e]).astype(LOW)

        @pl.when(turn < 2)
        def _():
            y_copy(turn, 1 + lax.rem(side + turn, 2), chunk).start()

        @pl.when(jnp.logical_and(turn >= 2, chunk != me))
        def _():
            y_copy(turn, 0, chunk).start()

        @pl.when(chunk == me)
        def _():
            y_ref[me] = y_send[turn]

        return 0

    lax.fori_loop(0, peers, expert_step, 0)

    own_rows = rows_of(me)
    x_own = jnp.concatenate([blocks_ref[block, own_rows] for block in range(peers)], axis=1)
    logits = dot(x_own, wg_ref[...], NT) + bg_ref[...]
    for k in range(tasks):
        part = logits[:, k * experts : (k + 1) * experts]
        part = jnp.exp(part - jnp.max(part, axis=1, keepdims=True))
        gates_ref[:, k * experts : (k + 1) * experts] = part / jnp.sum(part, axis=1, keepdims=True)

    stats_ref[...] = jnp.zeros_like(stats_ref)

    def square_step(tile, total):
        at = pl.multiple_of(tile * 64, 64)
        valid = (lax.broadcasted_iota(I32, (64, 1), 0) + at) < limit
        part = jnp.where(valid, x_ref[pl.ds(at, 64), :].astype(F32), 0.0)
        return total + jnp.sum((part * part).reshape(8, 8, width), axis=0)

    x_square = lax.fori_loop(0, samples // 64, square_step, jnp.zeros((8, width), F32))
    stats_ref[experts + tasks, :, :width] = x_square
    for relation, device in enumerate((near, far, across)):
        y_copy(0, relation, device).wait_recv()

    tile_rows = 16

    def tile_of(tile):
        at = pl.multiple_of(tile * tile_rows, tile_rows)
        return at, pl.ds(at, tile_rows)

    def mix_step(tile, _):
        at, rows = tile_of(tile)
        valid = (lax.broadcasted_iota(I32, (tile_rows, 1), 0) + (at + me * own)) < limit
        gates = gates_ref[rows, :]
        mixed = [None] * tasks
        for e in range(experts):
            y = y_ref[e // here, e % here, rows, :].astype(F32)
            square = jnp.where(valid, y * y, 0.0)
            stats_ref[e] += square[:8] + square[8:]
            for k in range(tasks):
                term = gates[:, k * experts + e : k * experts + e + 1] * y
                mixed[k] = term if e == 0 else mixed[k] + term
        for k in range(tasks):
            square = jnp.where(valid, mixed[k] * mixed[k], 0.0)
            stats_ref[experts + k] += square[:8] + square[8:]
            mixb_ref[k, rows, :] = mixed[k].astype(LOW)
        return 0

    lax.fori_loop(0, own // tile_rows, mix_step, 0)

    pack_ref[...] = jnp.zeros_like(pack_ref)
    blocks_x = peers * width // 128
    heads_at = blocks_x * tasks * experts
    tower_at = heads_at + tasks * tower_hid // 128
    outer_at = tower_at + tasks * tower_hid // 128
    rest_at = outer_at + experts * out_width // 128
    loss = jnp.zeros((1, 1), F32)
    weight_sum = jnp.zeros((1, 1), F32)
    row_id = lax.broadcasted_iota(I32, (own, 1), 0) + me * own
    for k in range(tasks):
        cols = slice(k * tower_hid, (k + 1) * tower_hid)
        z, slope = gelu_parts(dot(mixb_ref[k], w3_ref[:, cols]) + tb1_ref[k : k + 1, :])
        head = heads_ref[k : k + 1, :]
        logit = jnp.sum(z * head, axis=1, keepdims=True) + tb2_ref[0, k]
        small = jnp.exp(-jnp.abs(logit))
        label = labels_ref[:, k : k + 1].astype(F32)
        weight = jnp.where(row_id < limit, mask_ref[:, k : k + 1].astype(F32), 0.0)
        soft = jnp.maximum(logit, 0.0) + jnp.log1p(small)
        loss += jnp.sum(weight * (soft - label * logit), axis=0, keepdims=True)
        weight_sum += jnp.sum(weight, axis=0, keepdims=True)
        chance = jnp.where(logit >= 0.0, 1.0, small) / (1.0 + small)
        dl = weight * (chance - label)
        g_head = jnp.sum(dl * z, axis=0, keepdims=True)
        dz = (dl * head * slope).astype(LOW)
        g_bias = jnp.sum(dz.astype(F32), axis=0, keepdims=True)
        for part in range(tower_hid // 128):
            lane = slice(part * 128, (part + 1) * 128)
            at = k * (tower_hid // 128) + part
            pack_ref[heads_at + at : heads_at + at + 1, :] = g_head[:, lane]
            pack_ref[tower_at + at : tower_at + at + 1, :] = g_bias[:, lane]
        pack_ref[rest_at + 1 : rest_at + 2, k : k + 1] = jnp.sum(dl, axis=0, keepdims=True)
        dmix_ref[k] = dot(dz, w3_ref[:, cols], NT)
        small_ref[:, cols] = dot(mixb_ref[k], dz, TN).astype(LOW)
    stats_ref[experts + tasks + 1, :1, :1] = loss
    stats_ref[experts + tasks + 1, :1, 1:2] = weight_sum

    def dy_step(tile, _):
        at, rows = tile_of(tile)
        gates = gates_ref[rows, :]
        dmix = [dmix_ref[k, rows, :] for k in range(tasks)]
        for e in range(experts):
            total = None
            for k in range(tasks):
                term = gates[:, k * experts + e : k * experts + e + 1] * dmix[k]
                total = term if k == 0 else total + term
            dy_send[e, rows, :] = total.astype(LOW)
        return 0

    lax.fori_loop(0, own // tile_rows, dy_step, 0)
    d_copy(1, far).start()
    d_copy(2, across).start()
    d_copy(0, near).start()
    dy_ref[:, own_rows, :] = dy_send[pl.ds(me * here, here)]
    ones = jnp.ones((8, own), LOW)
    for e in range(experts):
        g_outer = dot(ones, dy_send[e])
        for part in range(out_width // 128):
            at = outer_at + e * (out_width // 128) + part
            pack_ref[at : at + 1, :] = g_outer[:1, part * 128 : (part + 1) * 128]

    lane = lax.broadcasted_iota(I32, (tile_rows, tasks * experts), 1)

    def dg_step(tile, _):
        at, rows = tile_of(tile)
        dmix = [dmix_ref[k, rows, :] for k in range(tasks)]
        found = jnp.zeros((tile_rows, tasks * experts), F32)
        for e in range(experts):
            y = y_ref[e // here, e % here, rows, :].astype(F32)
            for k in range(tasks):
                value = jnp.sum(dmix[k] * y, axis=1, keepdims=True)
                found = jnp.where(lane == k * experts + e, value, found)
        dg_ref[rows, :] = found
        return 0

    lax.fori_loop(0, own // tile_rows, dg_step, 0)
    gates = gates_ref[...]
    dg = dg_ref[...]
    flat = (tasks * experts, tasks * experts)
    same = lax.broadcasted_iota(I32, flat, 0) // experts == lax.broadcasted_iota(I32, flat, 1) // experts
    mean = dot(gates * dg, same.astype(F32), precision=HIGH)
    dgl = (gates * (dg - mean)).astype(LOW)
    pack_ref[rest_at : rest_at + 1, : tasks * experts] = jnp.sum(
        dgl.astype(F32), axis=0, keepdims=True
    )
    g_gating = dot(dgl, x_own, TN)
    for part in range(blocks_x):
        at = part * tasks * experts
        pack_ref[at : at + tasks * experts, :] = g_gating[:, part * 128 : (part + 1) * 128]
    small_ref[:, tasks * tower_hid :] = pack_ref[...].astype(LOW)


    share = share_ref.shape[0]

    def share_rows(part):
        return pl.ds(pl.multiple_of(part * share, share), share)

    def core_copy():
        return pltpu.make_async_remote_copy(
            small_ref.at[pl.ds(pl.multiple_of((1 - side) * 2 * share, share), 2 * share)],
            core_recv,
            s_out.at[0],
            s_in.at[0],
            device_id={"dp": dp, "mp": near},
            device_id_type=MESH,
        )

    def pair_copy():
        return pltpu.make_async_remote_copy(
            pair_send,
            pair_recv,
            s_out.at[1],
            s_in.at[1],
            device_id={"dp": pair, "mp": me},
            device_id_type=MESH,
        )

    def core_sum(part):
        mine = small_ref[share_rows(side * 2 + part), :].astype(F32)
        return mine + core_recv[share_rows(part), :].astype(F32)

    core_copy().start()
    g_b1_ref[...] = jnp.zeros_like(g_b1_ref)

    gate_ref[...] = dot(dgl, wg_ref[...])

    def hand_on(turn):
        rows = rows_of(back_chunk(turn))
        g_help(turn).wait_recv()
        total = dx_send[far, rows].astype(F32) + dx_help[rows].astype(F32)
        dx_sum[rows] = total.astype(LOW)
        g_far(turn).start()

    act = jnp.ones((8, own), LOW)

    def chunk_step(turn, _):
        chunk = back_chunk(turn)
        rows = rows_of(chunk)

        @pl.when(jnp.logical_and(turn < 2, chunk != me))
        def _():
            d_copy(0, chunk).wait_recv()

        @pl.when(turn >= 2)
        def _():
            d_copy(1 + lax.rem(side + turn, 2), chunk).wait_recv()

        total = gate_ref[...] * jnp.where(chunk == me, 1.0, 0.0)
        for e in range(here):
            w_out = w_ref[:, e, in_rows:, :].reshape(out_width, hid)
            dpre = (dot(dy_ref[e, rows, :], w_out) * slope_ref[e, rows, :]).astype(LOW)
            dpre_ref[e, rows, :] = dpre
            g_b1_ref[e] += dot(act, dpre)
            w_in = w_ref[:, e, :in_rows, :].reshape(features, hid)
            total += dot(dpre, w_in, NT)
        for target in range(peers):
            dx_send[target, rows] = total[:, target * width : (target + 1) * width].astype(LOW)
        g_near(turn).start()
        g_help(turn).start()

        @pl.when(turn > 0)
        def _():
            hand_on(turn - 1)

        return 0

    lax.fori_loop(0, peers, chunk_step, 0)
    hand_on(peers - 1)
    core_copy().wait()
    pair_send[...] = core_sum(1 - dp_side).astype(LOW)
    pair_copy().start()

    lanes = parts_ref.shape[4]
    blocks_in = width // 128
    per_in = 128 // in_rows
    per_out = 128 // out_rows
    for e in range(here):

        def in_step(block, _):
            cols = pl.ds(pl.multiple_of(lax.rem(block, blocks_in) * 128, 128), 128)
            x = blocks_ref[lax.div(block, blocks_in), :, cols]
            value = dot(x, dpre_ref[e], TN).astype(LOW)
            for shard in range(per_in):
                for target in range(peers):
                    to = block * per_in + shard
                    away = lax.rem(to + dp, 2)
                    parts_ref[
                        away, lax.div(to, 2), target, e * rows_both : e * rows_both + in_rows, :
                    ] = value[
                        shard * in_rows : (shard + 1) * in_rows, target * lanes : (target + 1) * lanes
                    ]
            return 0

        lax.fori_loop(0, features // 128, in_step, 0)

        def out_step(block, _):
            cols = pl.ds(pl.multiple_of(block * 128, 128), 128)
            value = dot(dy_ref[e, :, cols], hid_ref[e], TN).astype(LOW)
            for shard in range(per_out):
                for target in range(peers):
                    to = block * per_out + shard
                    away = lax.rem(to + dp, 2)
                    parts_ref[
                        away,
                        lax.div(to, 2),
                        target,
                        e * rows_both + in_rows : (e + 1) * rows_both,
                        :,
                    ] = value[
                        shard * out_rows : (shard + 1) * out_rows,
                        target * lanes : (target + 1) * lanes,
                    ]
            return 0

        lax.fori_loop(0, out_width // 128, out_step, 0)

    pair_copy().wait()
    share_ref[...] = (core_sum(dp_side) + pair_recv[...].astype(F32)).astype(LOW)
    for turn in range(peers):
        g_near(turn).wait()
        g_far(turn).wait()
    dx_ref[...] = dx_send[me].astype(F32) + dx_near[...].astype(F32) + dx_far[...].astype(F32)
    for turn in range(peers):
        g_help(turn).wait_send()
        x_far(turn).wait_send()
        x_near(turn).wait_send()
        x_hand(turn).wait_send()
    for relation, device in enumerate((near, far, across)):
        y_copy(0, relation, device).wait_send()
        d_copy(relation, device).wait_send()


def total_kernel(
    features,
    width_out,
    valid_ref,
    inner_ref,
    stats_ref,
    tables_ref,
    shares_ref,
    grads_ref,
    inner_out,
    result_ref,
    pay_ref,
    got_ref,
    t_out,
    t_in,
):
    devices = got_ref.shape[0]
    peers = inner_out.shape[0]
    here, _, hid = inner_ref.shape
    inner_rows = inner_out.shape[1]
    number = stats_ref.shape[0] - 2
    me = lax.axis_index("dp") * peers + lax.axis_index("mp")
    barrier = pltpu.get_barrier_semaphore()

    def greet(step, _):
        target = lax.rem(me + step, devices)
        pl.semaphore_signal(barrier, inc=1, device_id=place_of(target, peers), device_id_type=MESH)
        return 0

    lax.fori_loop(1, devices, greet, 0)
    lane = lax.broadcasted_iota(I32, (1, 128), 1)

    def whole_sum(value):
        return jnp.sum(jnp.sum(value, axis=0, keepdims=True), axis=1, keepdims=True)

    def grad_step(at, total):
        rows = grads_ref[pl.ds(pl.multiple_of(at * 64, 64), 64), :]
        return total + jnp.sum((rows * rows).reshape(8, 8, 128), axis=0)

    squares = lax.fori_loop(0, grads_ref.shape[0] // 64, grad_step, tables_ref[...])
    share = shares_ref[...]
    vector = jnp.where(lane == 0, stats_ref[number + 1, :1, :1], 0.0)
    vector = jnp.where(lane == 1, stats_ref[number + 1, :1, 1:2], vector)
    for at in range(number + 1):
        vector = jnp.where(lane == at + 2, whole_sum(stats_ref[at]), vector)
    vector = jnp.where(lane == number + 3, whole_sum(squares) + whole_sum(share * share), vector)
    pay_ref[...] = jnp.zeros_like(pay_ref)
    for e in range(here):
        for part in range(hid // 128):
            at = e * (hid // 128) + part
            pay_ref[at : at + 1, :] = inner_ref[e, :1, part * 128 : (part + 1) * 128]
    pay_ref[inner_rows : inner_rows + 1, :] = vector
    got_ref[me] = pay_ref[...]
    pl.semaphore_wait(barrier, devices - 1)

    def t_copy(step):
        target = lax.rem(me + step, devices)
        return pltpu.make_async_remote_copy(
            pay_ref,
            got_ref.at[me],
            t_out.at[step],
            t_in.at[step],
            device_id=place_of(target, peers),
            device_id_type=MESH,
        )

    def start(step, _):
        t_copy(step).start()
        return 0

    def finish(step, _):
        t_copy(step).wait()
        return 0

    lax.fori_loop(1, devices, start, 0)
    lax.fori_loop(1, devices, finish, 0)
    total = jnp.zeros((1, 128), F32)
    inner_sq = jnp.zeros((inner_rows, 128), F32)
    for group in range(peers):
        part = jnp.zeros((inner_rows, 128), F32)
        for block in range(devices // peers):
            source = block * peers + group
            part = part + got_ref[source, :inner_rows, :]
            total = total + got_ref[source, inner_rows : inner_rows + 1, :]
        inner_out[group] = part
        inner_sq = inner_sq + part * part

    def pick(at):
        return jnp.sum(jnp.where(lane == at, total, 0.0), axis=1, keepdims=True)

    weight = pick(1)
    grad_norm = jnp.sqrt(pick(number + 3) + whole_sum(inner_sq)) / weight
    factor = jnp.minimum(1.0, clip_max / grad_norm) / weight
    count = valid_ref[0].astype(F32)
    width = jnp.where(lane == number + 2, float(features), float(width_out))
    result_ref[...] = jnp.zeros_like(result_ref)
    result_ref[0:1, :] = jnp.broadcast_to(factor, (1, 128))
    result_ref[1:2, :] = jnp.broadcast_to(grad_norm, (1, 128))
    result_ref[2:3, :] = total
    result_ref[3:4, :] = jnp.sqrt(total / (count * width) + stat_eps)


def table_kernel(factor_ref, weight_ref, first_ref, second_ref, grad_ref, *outs):
    pair, width, rows = weight_ref.shape
    gradient = grad_ref[0].T.reshape(pair, width, rows) * factor_ref[:1, :1].reshape(1, 1, 1)
    results = adamw(weight_ref[...], first_ref[...], second_ref[...], gradient, rate_table)
    for out, result in zip(outs, results):
        out[...] = result


def small_kernel(
    tasks,
    experts,
    result_ref,
    whole_ref,
    t0_ref,
    t1_ref,
    t2_ref,
    g0_ref,
    g1_ref,
    g2_ref,
    h0_ref,
    h1_ref,
    h2_ref,
    t0_out,
    t1_out,
    t2_out,
    g0_out,
    g1_out,
    g2_out,
    h0_out,
    h1_out,
    h2_out,
    pack_ref,
):
    step = pl.program_id(0)
    peers = lax.axis_size("mp")
    groups = lax.axis_size("dp")
    rows, width = t0_ref.shape
    unit = whole_ref.shape[1]
    factor = result_ref[:1, :1]
    core, side = lax.div(step, 2), lax.rem(step, 2)
    for first in range(groups // 2):
        for second in range(peers // 2):
            source = (2 * first + side) * peers + 2 * second + core
            at = (first * (peers // 2) + second) * unit
            value = whole_ref[source]
            here = slice(at, at + unit)
            results = adamw(
                t0_ref[here, :],
                t1_ref[here, :],
                t2_ref[here, :],
                value[:, :width].astype(F32) * factor,
                rate_dense,
            )
            for out, result in zip((t0_out, t1_out, t2_out), results):
                out[here, :] = result
            pack_ref[pl.ds(step * rows + at, unit), :] = value[:, width:].astype(F32)

    @pl.when(step == pl.num_programs(0) - 1)
    def _():
        gates = tasks * experts
        features = g0_ref.shape[1]
        for part in range(features // 128):
            lane = slice(part * 128, (part + 1) * 128)
            results = adamw(
                g0_ref[:, lane],
                g1_ref[:, lane],
                g2_ref[:, lane],
                pack_ref[part * gates : (part + 1) * gates, :] * factor,
                rate_dense,
            )
            for out, result in zip((g0_out, g1_out, g2_out), results):
                out[:, lane] = result
        heads_at = features // 128 * gates
        parts = h0_ref.shape[1] // 128
        for task in range(tasks):
            for part in range(parts):
                lane = slice(part * 128, (part + 1) * 128)
                at = heads_at + task * parts + part
                row = slice(task, task + 1)
                results = adamw(
                    h0_ref[row, lane],
                    h1_ref[row, lane],
                    h2_ref[row, lane],
                    pack_ref[at : at + 1, :] * factor,
                    rate_dense,
                )
                for out, result in zip((h0_out, h1_out, h2_out), results):
                    out[row, lane] = result


def body(
    row_ids,
    counts,
    labels,
    label_mask,
    embeddings,
    embed_first,
    embed_second,
    expert_in,
    in_first,
    in_second,
    expert_out,
    out_first,
    out_second,
    gating,
    gating_first,
    gating_second,
    towers,
    towers_first,
    towers_second,
    heads,
    heads_first,
    heads_second,
    biases,
    biases_first,
    biases_second,
):
    devices = lax.axis_size(AXES)
    mp_count = lax.axis_size("mp")
    dp_count = lax.axis_size("dp")
    mp_index = lax.axis_index("mp")
    samples, tables_here = row_ids.shape
    tables, rows_dev, d_emb = embeddings.shape
    own = samples // mp_count
    requests = samples * tables_here
    capacity = 2 * requests // devices
    height = capacity // 2
    slots = devices * height
    row_bits = rows_dev.bit_length() - 1
    pairs = tables // 2
    lanes = 2 * d_emb
    group_rows = tables_here // 2 * rows_dev
    in_rows, out_rows = expert_in.shape[0], expert_out.shape[0]
    experts_here = EXPERTS // mp_count
    hid = expert_in.shape[2] * mp_count
    features = tables * d_emb
    width_out = out_rows * dp_count
    tower_hid = towers.shape[1] // TASKS

    outgoing, place, slot, source = pl.pallas_call(
        functools.partial(route_kernel, row_bits),
        out_shape=(
            jax.ShapeDtypeStruct((devices, 1, capacity), I32),
            jax.ShapeDtypeStruct((tables_here, samples), I32),
            jax.ShapeDtypeStruct((tables_here, samples), I32),
            jax.ShapeDtypeStruct((tables_here, samples), I32),
        ),
        in_specs=[VMEM],
        out_specs=(VMEM,) * 4,
        compiler_params=params(32),
        name="route",
    )(row_ids.T)
    in_out_rows = in_rows + out_rows
    hid_here = hid // mp_count
    shard = jnp.concatenate([expert_in, expert_out], axis=0).astype(LOW).transpose(1, 0, 2)
    sides = [
        [d * mp_count + m for d in range(x, dp_count, 2) for m in range(mp_count)] for x in range(2)
    ]
    partners = [(d, d ^ 1) for d in range(dp_count)]

    def exchange_side(parts):
        return lax.all_to_all(
            parts, AXES, split_axis=0, concat_axis=0, axis_index_groups=sides, tiled=True
        )

    def exchange_all(parts):
        return lax.all_to_all(parts, AXES, split_axis=0, concat_axis=0, tiled=True)

    def sems(*shape):
        return pltpu.SemaphoreType.DMA(shape)

    codes, shard = pl.pallas_call(
        ask_kernel,
        out_shape=(
            jax.ShapeDtypeStruct((devices, 1, capacity), I32),
            jax.ShapeDtypeStruct((experts_here, in_out_rows, hid), LOW),
        ),
        in_specs=[VMEM, VMEM],
        out_specs=(VMEM, VMEM),
        scratch_shapes=[sems(devices), sems(devices), sems(mp_count), sems(mp_count)],
        compiler_params=pltpu.CompilerParams(
            vmem_limit_bytes=16 * MIB, collective_id=2, has_side_effects=True
        ),
        name="ask",
    )(outgoing, shard)
    w_far = []
    for ahead in range(1, dp_count // 2):
        steps = [(d, (d + 2 * ahead) % dp_count) for d in range(dp_count)]
        w_far.append(lax.ppermute(shard, "dp", steps))
    w_near = lax.ppermute(shard, "dp", partners)
    codes = codes.reshape(devices, capacity)
    asked = codes[:, 0] >> 16
    plain = codes & 65535
    found_at = jnp.maximum(plain - 1, 0)
    table_at = found_at >> row_bits
    sum_at = (table_at >> 1) * rows_dev + (found_at & (rows_dev - 1))
    number = jnp.arange(capacity, dtype=I32)[None, :]
    part_at = ((number & 1) * 2 + (table_at & 1)) * slots + (number >> 1)
    part_at = part_at + jnp.arange(devices, dtype=I32)[:, None] * height
    part_at = jnp.where(plain > 0, part_at, 4 * slots)

    table_view = jnp.transpose(embeddings, (0, 2, 1))
    found = pl.pallas_call(
        functools.partial(find_kernel, mp_count),
        grid=(mp_count,),
        out_shape=jax.ShapeDtypeStruct((dp_count, mp_count, height, lanes), LOW),
        in_specs=[
            SMEM,
            SMEM,
            pl.BlockSpec((tables_here, d_emb, rows_dev), lambda m: (m, 0, 0)),
        ],
        out_specs=pl.BlockSpec((dp_count, 1, height, lanes), lambda m: (0, m, 0, 0)),
        scratch_shapes=[
            pltpu.VMEM((tables_here * rows_dev, lanes), F32),
            pltpu.VMEM((height, lanes), F32),
        ],
        compiler_params=params(60),
        name="find",
    )(found_at.reshape(-1), asked, table_view)
    w_far, w_near, found = lax.optimization_barrier((w_far, w_near, found))
    w_mine = [shard] + w_far
    w_theirs = [w_near] + [lax.ppermute(line, "dp", partners) for line in w_far]
    returned = exchange_all(found.reshape(devices, height, lanes))
    embedded = pl.pallas_call(
        place_kernel,
        out_shape=jax.ShapeDtypeStruct((samples, tables_here * d_emb), LOW),
        in_specs=[SMEM, VMEM],
        out_specs=VMEM,
        scratch_shapes=[
            pltpu.VMEM((2 * slots, lanes), F32),
            pltpu.VMEM((tables_here // 2, samples, lanes), F32),
        ],
        compiler_params=params(32),
        name="place",
    )(place.reshape(-1), returned.reshape(slots, lanes))

    first = EXPERTS * hid
    second = first + EXPERTS * width_out
    third = second + TASKS * EXPERTS
    fourth = third + TASKS * tower_hid
    inner_here = lax.dynamic_index_in_dim(
        biases[:first].reshape(mp_count, experts_here, 1, hid), mp_index, 0, keepdims=False
    )
    outer_here = lax.dynamic_index_in_dim(
        biases[first:second].reshape(mp_count, experts_here, 1, width_out),
        mp_index,
        0,
        keepdims=False,
    )
    gating_low = gating.T.astype(LOW)
    all_gates = TASKS * EXPERTS
    pack_rows = width_out

    def scratch(shape, kind=F32):
        return pltpu.VMEM(shape, kind)

    pack_shape = (pack_rows // 4, TASKS * tower_hid + 128)
    x_shape = (samples, tables_here * d_emb)
    stat_parts, embed_grad, grad_parts, inner_parts, share = pl.pallas_call(
        functools.partial(dense_kernel, dp_count // 2),
        out_shape=(
            jax.ShapeDtypeStruct((EXPERTS + TASKS + 2, 8, width_out), F32),
            jax.ShapeDtypeStruct(x_shape, F32),
            jax.ShapeDtypeStruct(
                (2, dp_count // 2, mp_count, experts_here * in_out_rows, hid_here), LOW
            ),
            jax.ShapeDtypeStruct((experts_here, 8, hid), F32),
            jax.ShapeDtypeStruct(pack_shape, LOW),
        ),
        in_specs=[pl.BlockSpec(memory_space=pl.ANY)] * dp_count
        + [SMEM]
        + [VMEM] * 8
        + [SMEM]
        + [VMEM] * 2,
        out_specs=(VMEM,) * 5,
        scratch_shapes=[
            scratch((dp_count, experts_here, in_out_rows, hid), LOW),
            scratch((mp_count,) + x_shape, LOW),
            scratch((experts_here, samples, hid), LOW),
            scratch((experts_here, samples, hid)),
            scratch((experts_here, samples, width_out), LOW),
            scratch((mp_count, experts_here, own, width_out), LOW),
            scratch((mp_count, experts_here, own, width_out), LOW),
            scratch((own, all_gates)),
            scratch((TASKS, own, width_out), LOW),
            scratch((TASKS, own, width_out)),
            scratch((own, all_gates)),
            scratch((EXPERTS, own, width_out), LOW),
            scratch((pack_rows, TASKS * tower_hid + 128), LOW),
            scratch((pack_rows, 128)),
            scratch((own, hid)),
            scratch((own, features)),
            scratch((experts_here, samples, hid), LOW),
            scratch((mp_count,) + x_shape, LOW),
            scratch(x_shape, LOW),
            scratch(x_shape, LOW),
            scratch(x_shape, LOW),
            scratch(x_shape, LOW),
            scratch((2 * pack_shape[0], pack_shape[1]), LOW),
            scratch(pack_shape, LOW),
            scratch(pack_shape, LOW),
            sems(3, mp_count),
            sems(3, mp_count),
            sems(3),
            sems(3),
            sems(3),
            sems(3),
            sems(3, mp_count),
            sems(3, mp_count),
            sems(2),
            sems(2),
            sems(2, dp_count // 2),
        ],
        compiler_params=pltpu.CompilerParams(
            vmem_limit_bytes=60 * MIB, collective_id=0, has_side_effects=True
        ),
        name="dense",
    )(
        *w_mine,
        *w_theirs,
        lax.dynamic_slice_in_dim(counts, lax.axis_index("dp"), 1, 0),
        embedded,
        inner_here,
        outer_here,
        gating_low,
        biases[second:third].reshape(1, all_gates),
        towers.astype(LOW),
        biases[third:fourth].reshape(TASKS, tower_hid),
        heads,
        biases[fourth:].reshape(1, TASKS),
        labels,
        label_mask,
    )

    back_rows = pl.pallas_call(
        send_kernel,
        out_shape=jax.ShapeDtypeStruct((slots, lanes), LOW),
        in_specs=[SMEM, SMEM, VMEM],
        out_specs=VMEM,
        scratch_shapes=[
            pltpu.VMEM((tables_here // 2, 2 * samples, lanes), F32),
            pltpu.VMEM((2 * slots, lanes), F32),
        ],
        compiler_params=params(32),
        name="send",
    )(slot.reshape(-1), source.reshape(-1), embed_grad)
    share = share.reshape(devices // 4, pack_rows // devices, -1)
    arrived, shares = pl.pallas_call(
        swap_kernel,
        out_shape=(
            jax.ShapeDtypeStruct((devices, height, lanes), LOW),
            jax.ShapeDtypeStruct(share.shape, LOW),
        ),
        in_specs=[VMEM, VMEM],
        out_specs=(VMEM, VMEM),
        scratch_shapes=[sems(devices), sems(devices), sems(devices // 4), sems(devices // 4)],
        compiler_params=pltpu.CompilerParams(
            vmem_limit_bytes=16 * MIB, collective_id=3, has_side_effects=True
        ),
        name="swap",
    )(back_rows.reshape(devices, height, lanes), share)
    share = jnp.sum(shares.astype(F32), axis=0)
    partner = lax.ppermute(grad_parts[1], "dp", partners)
    partner, arrived = lax.optimization_barrier((partner, arrived))
    grad_parts = (grad_parts[0].astype(F32) + partner.astype(F32)).astype(LOW)
    grad_parts = exchange_side(
        grad_parts.reshape(devices // 2, experts_here * in_out_rows, hid_here)
    )
    grad_sum = jnp.sum(
        grad_parts.reshape(dp_count // 2, mp_count, experts_here, in_out_rows, -1).astype(F32), 0
    )
    owned = grad_sum.reshape(EXPERTS, in_out_rows, -1).transpose(1, 0, 2)
    in_sum, out_sum = owned[:in_rows], owned[in_rows:]

    table_grad, table_sq = pl.pallas_call(
        functools.partial(add_kernel, mp_count),
        out_shape=(
            jax.ShapeDtypeStruct((pairs * rows_dev, lanes), F32),
            jax.ShapeDtypeStruct((8, lanes), F32),
        ),
        in_specs=[SMEM, SMEM, SMEM, VMEM],
        out_specs=(VMEM, VMEM),
        scratch_shapes=[
            pltpu.VMEM((4 * slots + 8, lanes), F32),
            pltpu.SemaphoreType.DMA((mp_count,)),
        ]
        + [pltpu.VMEM((group_rows, lanes), F32)] * mp_count,
        compiler_params=params(60),
        name="add",
    )(sum_at.reshape(-1), part_at.reshape(-1), asked, arrived.reshape(slots, lanes))

    stat_end = EXPERTS + TASKS
    inner_rows = experts_here * hid // 128
    pay_rows = inner_rows + 8
    inner_sum, result = pl.pallas_call(
        functools.partial(total_kernel, features, width_out),
        out_shape=(
            jax.ShapeDtypeStruct((mp_count, inner_rows, 128), F32),
            jax.ShapeDtypeStruct((8, 128), F32),
        ),
        in_specs=[SMEM] + [VMEM] * 5,
        out_specs=(VMEM,) * 2,
        scratch_shapes=[
            scratch((pay_rows, 128)),
            scratch((devices, pay_rows, 128)),
            sems(devices),
            sems(devices),
        ],
        compiler_params=pltpu.CompilerParams(
            vmem_limit_bytes=16 * MIB, collective_id=4, has_side_effects=True
        ),
        name="total",
    )(
        jnp.sum(counts).reshape(1),
        inner_parts,
        stat_parts,
        table_sq,
        share,
        grad_sum.reshape(-1, 128),
    )
    factor = result[0, 0]
    share_low, result = lax.optimization_barrier((share.astype(LOW), result))
    whole = exchange_all(jnp.broadcast_to(share_low[None], (devices,) + share_low.shape))

    table_spec = pl.BlockSpec((2, d_emb, rows_dev), lambda p: (p, 0, 0))
    embed_out = pl.pallas_call(
        table_kernel,
        grid=(pairs,),
        out_shape=(jax.ShapeDtypeStruct(table_view.shape, F32),) * 3,
        in_specs=[
            pl.BlockSpec((8, 128), lambda p: (0, 0)),
            table_spec,
            table_spec,
            table_spec,
            pl.BlockSpec((1, rows_dev, lanes), lambda p: (p, 0, 0)),
        ],
        out_specs=(table_spec,) * 3,
        compiler_params=params(40),
        name="tables",
    )(
        result,
        table_view,
        jnp.transpose(embed_first, (0, 2, 1)),
        jnp.transpose(embed_second, (0, 2, 1)),
        table_grad.reshape(pairs, rows_dev, lanes),
    )
    embed_out = [jnp.transpose(value, (0, 2, 1)) for value in embed_out]
    in_out = adamw(expert_in, in_first, in_second, in_sum * factor, rate_dense)
    out_out = adamw(expert_out, out_first, out_second, out_sum * factor, rate_dense)
    whole, embed_out = lax.optimization_barrier((whole, embed_out))
    blocks_x = features // 128
    heads_at = blocks_x * all_gates
    tower_at = heads_at + TASKS * tower_hid // 128
    outer_at = tower_at + TASKS * tower_hid // 128
    rest_at = outer_at + EXPERTS * width_out // 128
    tower_spec = pl.BlockSpec((pack_rows // 4, TASKS * tower_hid), lambda c: (c, 0))
    gate_spec = pl.BlockSpec((all_gates, features), lambda c: (0, 0))
    head_spec = pl.BlockSpec((TASKS, tower_hid), lambda c: (0, 0))
    *small_out, packed = pl.pallas_call(
        functools.partial(small_kernel, TASKS, EXPERTS),
        grid=(4,),
        out_shape=(jax.ShapeDtypeStruct(towers.shape, F32),) * 3
        + (jax.ShapeDtypeStruct((all_gates, features), F32),) * 3
        + (jax.ShapeDtypeStruct(heads.shape, F32),) * 3
        + (jax.ShapeDtypeStruct((pack_rows, 128), F32),),
        in_specs=[
            pl.BlockSpec((8, 128), lambda c: (0, 0)),
            pl.BlockSpec(whole.shape, lambda c: (0, 0, 0)),
        ]
        + [tower_spec] * 3
        + [gate_spec] * 3
        + [head_spec] * 3,
        out_specs=(tower_spec,) * 3
        + (gate_spec,) * 3
        + (head_spec,) * 3
        + (pl.BlockSpec((pack_rows, 128), lambda c: (0, 0)),),
        compiler_params=params(48),
        name="small",
    )(
        result,
        whole,
        towers,
        towers_first,
        towers_second,
        gating.T,
        gating_first.T,
        gating_second.T,
        heads,
        heads_first,
        heads_second,
    )
    towers_out, heads_out = small_out[:3], small_out[6:]
    gating_out = [value.T for value in small_out[3:6]]
    bias_sum = jnp.concatenate(
        [
            inner_sum.reshape(-1),
            packed[outer_at:rest_at].reshape(-1),
            packed[rest_at, :all_gates],
            packed[tower_at:outer_at].reshape(-1),
            packed[rest_at + 1, :TASKS],
        ]
    )
    biases_out = adamw(biases, biases_first, biases_second, bias_sum * factor, rate_dense)
    stats = jnp.concatenate([result[3, stat_end + 2][None], result[3, 2 : stat_end + 2]])
    loss = result[2, :2]
    return (
        *embed_out,
        *in_out,
        in_out[0].astype(LOW),
        *out_out,
        out_out[0].astype(LOW),
        *gating_out,
        *towers_out,
        *heads_out,
        *biases_out,
        result[1, :1],
        loss,
        stats,
    )


def solution(mesh):
    rows = P(None, AXES, None)
    expert = P("dp", None, "mp")
    sample = P(AXES, None)
    placed = (P("dp", "mp"), P(), sample, sample) + (rows,) * 3 + (expert,) * 6 + (P(),) * 12
    results = (rows,) * 3 + (expert,) * 8 + (P(),) * 15
    return jax.shard_map(body, mesh=mesh, in_specs=placed, out_specs=results, check_vma=False)
```

```python
import functools
import math

import jax
import jax.numpy as jnp
from jax import lax
from jax.experimental import pallas as pl
from jax.experimental.pallas import tpu as pltpu
from jax.sharding import PartitionSpec as P

EXPERTS = 8
TASKS = 5
STEP = 3

HIGH = lax.Precision.HIGHEST
beta_one = 0.5
beta_two = 0.5
adam_eps = 1e-08
decay = 0.01
clip_max = 0.002
rate_table = 0.5
rate_dense = 0.02
stat_eps = 1e-06

LOW = jnp.bfloat16
F32 = jnp.float32
I32 = jnp.int32
MIB = 1024 * 1024
AXES = ("dp", "mp")


def params(mib):
    return pltpu.CompilerParams(vmem_limit_bytes=mib * MIB)


VMEM = pl.BlockSpec(memory_space=pltpu.VMEM)
SMEM = pl.BlockSpec(memory_space=pltpu.SMEM)


def adamw(weight, first, second, gradient, rate):
    first_next = beta_one * first + (1.0 - beta_one) * gradient
    second_next = beta_two * second + (1.0 - beta_two) * gradient * gradient
    corrected = first_next / (1.0 - beta_one**STEP)
    scaled = jnp.sqrt(second_next / (1.0 - beta_two**STEP))
    return (
        weight - rate * (corrected / (scaled + adam_eps) + decay * weight),
        first_next,
        second_next,
    )


def route(row_bits, ids_ref, out_ref, place_ref, slot_ref, from_ref):
    devices, _, capacity = out_ref.shape
    tables, samples = ids_ref.shape
    rows_dev = 1 << row_bits
    halves = devices * capacity // 2
    width = 256
    upper = (
        lax.broadcasted_iota(I32, (width, width), 0) <= lax.broadcasted_iota(I32, (width, width), 1)
    ).astype(LOW)
    owners = lax.broadcasted_iota(I32, (devices, width), 0)
    slots = lax.broadcasted_iota(I32, (capacity, width), 0)
    carry = jnp.zeros((devices, 1), F32)
    total = jnp.zeros((2 * devices, capacity), F32)
    for table in range(tables):
        parity = table % 2
        for part in range(samples // width):
            cols = pl.ds(part * width, width)
            ids = ids_ref[pl.ds(table, 1), cols]
            owner = ids >> row_bits
            code = table * rows_dev + (ids & (rows_dev - 1)) + 1
            onehot = (owner == owners).astype(F32)
            counted = jnp.dot(onehot.astype(LOW), upper, preferred_element_type=F32) + carry
            rank = jnp.sum(onehot * counted, axis=0, keepdims=True).astype(I32) - 1
            carry = counted[:, width - 1 :]
            at_slot = (rank == slots).astype(LOW)
            high = (code >> 7).astype(F32)
            low = (code & 127).astype(F32)
            pieces = jnp.concatenate([onehot * high, onehot * low], axis=0).astype(LOW)
            total += lax.dot_general(
                pieces, at_slot, (((1,), (1,)), ((), ())), preferred_element_type=F32
            )
            row = owner * (capacity // 2) + (rank >> 1)
            half = rank & 1
            place_ref[pl.ds(table, 1), cols] = (half ^ parity) * halves + row
            slot_ref[pl.ds(table, 1), cols] = half * halves + row
            sample = lax.broadcasted_iota(I32, (1, width), 1) + part * width
            from_ref[pl.ds(table, 1), cols] = (half ^ parity) * samples + sample
    codes = (total[:devices] * 128.0 + total[devices:]).astype(I32)
    first = lax.broadcasted_iota(I32, (devices, capacity), 1) == 0
    counted = jnp.where(first, carry * 65536.0, 0.0).astype(I32)
    out_ref[...] = (codes + counted).reshape(devices, 1, capacity)


def left_lanes(shape):
    return lax.broadcasted_iota(I32, shape, len(shape) - 1) < 64


def find_kernel(groups, at_ref, counts_ref, table_ref, out_ref, turned_ref, rows_ref):
    blocks, _, height, lanes = out_ref.shape
    tables, width, rows_dev = table_ref.shape
    group = pl.program_id(0)
    left = left_lanes((1, lanes))
    part = 512

    total = tables // 2 * rows_dev

    def turn_step(step, _):
        pair = lax.div(step, rows_dev // part)
        first = pl.multiple_of(lax.rem(step, rows_dev // part) * part, part)
        columns = table_ref[pl.ds(2 * pair, 2), :, pl.ds(first, part)]
        rows = columns.reshape(2 * width, part).T
        at = pl.multiple_of(step * part, part)
        turned_ref[pl.ds(at, part), :] = rows
        turned_ref[pl.ds(total + at, part), :] = pltpu.roll(rows, width, 1)
        return 0

    lax.fori_loop(0, total // part, turn_step, 0)

    def block_step(block, _):
        source = block * groups + group
        base = source * 2 * height

        def step(outer, _):
            got = []
            for inner in range(16):
                at = outer * 16 + inner
                even = turned_ref[pl.ds(at_ref[base + 2 * at], 1), :]
                odd = turned_ref[pl.ds(at_ref[base + 2 * at + 1], 1), :]
                got.append((at, jnp.where(left, even, odd)))
            for at, row in got:
                rows_ref[pl.ds(at, 1), :] = row
            return 0

        lax.fori_loop(0, (counts_ref[source] + 31) // 32, step, 0)
        out_ref[block, 0] = rows_ref[...].astype(LOW)
        return 0

    lax.fori_loop(0, blocks, block_step, 0)


def place_kernel(place_ref, rows_ref, out_ref, both_ref, flat_ref):
    count, lanes = rows_ref.shape
    samples = out_ref.shape[0]
    tables = place_ref.shape[0] // samples
    rows = rows_ref[...].astype(F32)
    both_ref[pl.ds(0, count), :] = rows
    both_ref[pl.ds(count, count), :] = pltpu.roll(rows, 64, 1)
    left = left_lanes((1, lanes))

    def step(outer, _):
        got = []
        for inner in range(8):
            sample = outer * 8 + inner
            for pair in range(tables // 2):
                even = both_ref[pl.ds(place_ref[2 * pair * samples + sample], 1), :]
                odd = both_ref[pl.ds(place_ref[(2 * pair + 1) * samples + sample], 1), :]
                got.append((pair, sample, jnp.where(left, even, odd)))
        for pair, sample, row in got:
            flat_ref[pair, pl.ds(sample, 1), :] = row
        return 0

    lax.fori_loop(0, samples // 8, step, 0)
    for pair in range(tables // 2):
        out_ref[:, pair * lanes : (pair + 1) * lanes] = flat_ref[pair].astype(LOW)


def send_kernel(slot_ref, from_ref, grad_ref, out_ref, both_ref, rows_ref):
    count, lanes = out_ref.shape
    samples = grad_ref.shape[0]
    tables = slot_ref.shape[0] // samples
    for pair in range(tables // 2):
        rows = grad_ref[:, pair * lanes : (pair + 1) * lanes]
        both_ref[pair, pl.ds(0, samples), :] = rows
        both_ref[pair, pl.ds(samples, samples), :] = pltpu.roll(rows, 64, 1)

    def step(outer, _):
        got = []
        for inner in range(8):
            sample = outer * 8 + inner
            for table in range(tables):
                row = both_ref[table // 2, pl.ds(from_ref[table * samples + sample], 1), :]
                got.append((slot_ref[table * samples + sample], row))
        for slot, row in got:
            rows_ref[pl.ds(slot, 1), :] = row
        return 0

    lax.fori_loop(0, samples // 8, step, 0)
    left = left_lanes((count, lanes))
    out_ref[...] = jnp.where(
        left, rows_ref[pl.ds(0, count), :], rows_ref[pl.ds(count, count), :]
    ).astype(LOW)


def swap_kernel(rows_ref, share_ref, out_ref, shares_ref, r_out, r_in, s_out, s_in):
    devices = rows_ref.shape[0]
    groups = share_ref.shape[0]
    peers = lax.axis_size("mp")
    dp, mp = lax.axis_index("dp"), lax.axis_index("mp")
    mine = lax.div(dp, 2) * (peers // 2) + lax.div(mp, 2)
    me = dp * peers + mp
    greet_all(devices, peers, me)

    def r_copy(step):
        target = lax.rem(me + step, devices)
        return pltpu.make_async_remote_copy(
            rows_ref.at[target],
            out_ref.at[me],
            r_out.at[step],
            r_in.at[step],
            device_id=place_of(target, peers),
            device_id_type=MESH,
        )

    def s_copy(step):
        target = lax.rem(mine + step, groups)
        to_dp = lax.div(target, peers // 2) * 2 + lax.rem(dp, 2)
        to_mp = lax.rem(target, peers // 2) * 2 + lax.rem(mp, 2)
        return pltpu.make_async_remote_copy(
            share_ref.at[target],
            shares_ref.at[mine],
            s_out.at[step],
            s_in.at[step],
            device_id={"dp": to_dp, "mp": to_mp},
            device_id_type=MESH,
        )

    def loop(first, copies, act):
        def step(at, _):
            act(copies(at))
            return 0

        lax.fori_loop(1, first, step, 0)

    loop(devices, r_copy, lambda copy: copy.start())
    loop(groups, s_copy, lambda copy: copy.start())
    out_ref[me] = rows_ref[me]
    shares_ref[mine] = share_ref[mine]
    loop(groups, s_copy, lambda copy: copy.wait())
    loop(devices, r_copy, lambda copy: copy.wait())


def add_kernel(
    groups, at_ref, part_at_ref, counts_ref, rows_ref, out_ref, square_ref, parts_ref, low_ref, sems, *sums
):
    count, lanes = rows_ref.shape
    sources = counts_ref.shape[0]
    height = count // sources
    table_rows = sums[0].shape[0]
    left = left_lanes((count, lanes))
    rows = rows_ref[...].astype(F32)
    turned = pltpu.roll(rows, 64, 1)
    parts_ref[pl.ds(0, count), :] = jnp.where(left, rows, 0.0)
    parts_ref[pl.ds(count, count), :] = jnp.where(left, 0.0, turned)
    parts_ref[pl.ds(2 * count, count), :] = jnp.where(left, turned, 0.0)
    parts_ref[pl.ds(3 * count, count), :] = jnp.where(left, 0.0, rows)
    parts_ref[pl.ds(4 * count, 8), :] = jnp.zeros((8, lanes), F32)

    def clear(at, _):
        for table in sums:
            table[pl.ds(pl.multiple_of(at * 64, 64), 64), :] = jnp.zeros((64, lanes), F32)
        return 0

    lax.fori_loop(0, table_rows // 64, clear, 0)

    def block_step(block, _):
        most = counts_ref[block * groups]
        for group in range(1, groups):
            most = jnp.maximum(most, counts_ref[block * groups + group])

        def step(outer, _):
            for inner in range(4):
                got = []
                for group in range(groups):
                    at = (block * groups + group) * 2 * height + outer * 4 + inner
                    here = pl.ds(at_ref[at], 1)
                    part = pl.ds(part_at_ref[at], 1)
                    got.append((here, sums[group][here, :] + parts_ref[part, :]))
                for group, (here, row) in enumerate(got):
                    sums[group][here, :] = row
            return 0

        lax.fori_loop(0, (most + 3) // 4, step, 0)
        return 0

    lax.fori_loop(0, sources // groups, block_step, 0)
    copies = []
    squares = jnp.zeros((8, lanes), F32)
    for group in range(groups):

        def square(at, total):
            here = pl.ds(pl.multiple_of(at * 64, 64), 64)
            rows = sums[group][here, :]
            low_ref[group, here, :] = rows.astype(LOW)
            return total + jnp.sum((rows * rows).reshape(8, 8, lanes), axis=0)

        squares = lax.fori_loop(0, table_rows // 64, square, squares)
        copies.append(
            pltpu.make_async_copy(
                low_ref.at[group],
                out_ref.at[pl.ds(group * table_rows, table_rows)],
                sems.at[group],
            )
        )
        copies[-1].start()
    square_ref[...] = squares
    for copy in copies:
        copy.wait()


def gelu_parts(value):
    scale = math.sqrt(2.0 / math.pi)
    square = value * value
    bend = jnp.tanh(scale * value * (1.0 + 0.044715 * square))
    half = 0.5 * (1.0 + bend)
    slope = half + 0.5 * value * (1.0 - bend * bend) * (scale * (1.0 + 3 * 0.044715 * square))
    return value * half, slope


def dot(a, b, axes=((1,), (0,)), precision=None):
    return lax.dot_general(
        a, b, (axes, ((), ())), preferred_element_type=F32, precision=precision
    )


NT = ((1,), (1,))
TN = ((0,), (0,))
MESH = pl.DeviceIdType.MESH


def meet(peers, partner=None):
    me = lax.axis_index("mp")
    barrier = pltpu.get_barrier_semaphore()
    if partner is not None:
        pl.semaphore_signal(
            barrier, inc=1, device_id={"dp": partner, "mp": me}, device_id_type=MESH
        )
    for step in range(1, peers):
        pl.semaphore_signal(
            barrier, inc=1, device_id={"mp": lax.rem(me + step, peers)}, device_id_type=MESH
        )
    pl.semaphore_wait(barrier, peers - 1 + (partner is not None))
    return me


def greet_all(devices, peers, me, between=None):
    barrier = pltpu.get_barrier_semaphore()

    def greet(step, _):
        target = lax.rem(me + step, devices)
        pl.semaphore_signal(
            barrier, inc=1, device_id=place_of(target, peers), device_id_type=MESH
        )
        return 0

    lax.fori_loop(1, devices, greet, 0)
    if between is not None:
        between()
    pl.semaphore_wait(barrier, devices - 1)


def place_of(device, peers):
    return {"dp": lax.div(device, peers), "mp": lax.rem(device, peers)}


def ask_kernel(
    row_bits,
    ids_ref,
    first_ref,
    second_ref,
    out_ref,
    full_ref,
    place_ref,
    slot_ref,
    from_ref,
    codes_ref,
    shard_ref,
    c_out,
    c_in,
    w_out,
    w_in,
):
    devices = codes_ref.shape[0]
    here, _, full = full_ref.shape
    width = shard_ref.shape[2]
    peers = full // width
    mp = lax.axis_index("mp")
    me = lax.axis_index("dp") * peers + mp
    columns = pl.ds(pl.multiple_of(mp * width, width), width)
    in_rows = first_ref.shape[0]

    def prepare():
        route(row_bits, ids_ref, codes_ref, place_ref, slot_ref, from_ref)
        for e in range(peers * here):
            shard_ref[e, :in_rows, :] = first_ref[:, e, :].astype(LOW)
            shard_ref[e, in_rows:, :] = second_ref[:, e, :].astype(LOW)
        full_ref[:, :, columns] = shard_ref[pl.ds(mp * here, here)]
        out_ref[me] = codes_ref[me]

    greet_all(devices, peers, me, prepare)

    def c_copy(step):
        target = lax.rem(me + step, devices)
        return pltpu.make_async_remote_copy(
            codes_ref.at[target],
            out_ref.at[me],
            c_out.at[step],
            c_in.at[step],
            device_id=place_of(target, peers),
            device_id_type=MESH,
        )

    def w_copy(step):
        target = lax.rem(mp + step, peers)
        return pltpu.make_async_remote_copy(
            shard_ref.at[pl.ds(target * here, here)],
            full_ref.at[:, :, columns],
            w_out.at[step],
            w_in.at[step],
            device_id={"mp": target},
            device_id_type=MESH,
        )

    def start(step, _):
        c_copy(step).start()
        return 0

    def finish(step, _):
        c_copy(step).wait()
        return 0

    lax.fori_loop(1, devices, start, 0)
    for step in range(1, peers):
        w_copy(step).start()
    lax.fori_loop(1, devices, finish, 0)
    for step in range(1, peers):
        w_copy(step).wait()


def dense_kernel(
    lines,
    *refs,
):
    mine, theirs = refs[:lines], refs[lines : 2 * lines]
    dense_part(mine, theirs, *refs[2 * lines :])


def dense_part(
    mine_refs,
    theirs_refs,
    count_ref,
    x_ref,
    b1_ref,
    b2_ref,
    wg_ref,
    bg_ref,
    w3_ref,
    tb1_ref,
    heads_ref,
    tb2_ref,
    labels_ref,
    mask_ref,
    stats_ref,
    dx_ref,
    parts_ref,
    g_b1_ref,
    share_ref,
    w_ref,
    blocks_ref,
    hid_ref,
    slope_ref,
    dy_ref,
    y_send,
    y_ref,
    gates_ref,
    mixb_ref,
    dz_ref,
    dmix_ref,
    dg_ref,
    dy_send,
    small_ref,
    pack_ref,
    act_ref,
    gate_ref,
    dpre_ref,
    dx_send,
    dx_near,
    dx_help,
    dx_sum,
    dx_far,
    core_recv,
    pair_send,
    pair_recv,
    x_out,
    x_in,
    y_out,
    y_in,
    d_out,
    d_in,
    g_out,
    g_in,
    s_out,
    s_in,
    w_in_sem,
):
    peers, samples, width = blocks_ref.shape
    here = hid_ref.shape[0]
    own, out_width = y_ref.shape[2], y_ref.shape[3]
    experts = peers * here
    tasks, tower_hid = heads_ref.shape
    shards, hid = w_ref.shape[0], w_ref.shape[3]
    in_rows = peers * width // shards
    rows_both = w_ref.shape[2]
    out_rows = rows_both - in_rows
    features = peers * width
    dp = lax.axis_index("dp")
    dp_side = lax.rem(dp, 2)
    pair = dp + 1 - 2 * dp_side
    lines = len(mine_refs)
    w_copies = []
    for at in range(lines):
        first = lax.rem(lax.div(dp, 2) + lines - at, lines) * 2
        w_copies += [
            pltpu.make_async_copy(
                mine_refs[at], w_ref.at[first + dp_side], w_in_sem.at[0, at]
            ),
            pltpu.make_async_copy(
                theirs_refs[at], w_ref.at[first + 1 - dp_side], w_in_sem.at[1, at]
            ),
        ]
    for copy in w_copies:
        copy.start()
    me = meet(peers, pair)
    side = lax.rem(me, 2)
    chip = lax.div(me, 2)
    near = me + 1 - 2 * side
    far = lax.rem(me + 2, peers)
    across = lax.rem(near + 2, peers)

    def rows_of(chunk):
        return pl.ds(pl.multiple_of(chunk * own, own), own)

    half = own // 2

    def part_rows(device, part):
        at = device * own + part * half
        return pl.ds(pl.multiple_of(at, half), half)

    def half_rows(part):
        return pl.ds(pl.multiple_of(part * half, half), half)

    def ahead_rows(pair_of, turn):
        first = lax.rem(2 * pair_of + 2 + 2 * lax.div(turn, 2), peers)
        part = lax.rem(turn, 2)
        return first, part, [part_rows(first + at, part) for at in range(2)]

    def back_chunk(turn):
        return lax.rem(2 * chip + turn, peers)

    def remote(source, target, out_sem, in_sem, device):
        return pltpu.make_async_remote_copy(
            source, target, out_sem, in_sem, device_id={"dp": dp, "mp": device}, device_id_type=MESH
        )

    def x_far(turn):
        rows = ahead_rows(1 - chip, turn)[2]
        return [
            remote(
                x_ref.at[rows[at]],
                blocks_ref.at[me, rows[at]],
                x_out.at[0, turn, at],
                x_in.at[0, turn, at],
                far,
            )
            for at in range(2)
        ]

    def x_near(turn):
        rows = ahead_rows(chip, turn)[2]
        return [
            remote(
                x_ref.at[rows[at]],
                blocks_ref.at[me, rows[at]],
                x_out.at[1, turn, at],
                x_in.at[1, turn, at],
                near,
            )
            for at in range(2)
        ]

    def x_hand(turn):
        rows = ahead_rows(chip, turn)[2]
        blocks = [blocks_ref.at[far, rows[at]] for at in range(2)]
        return [
            remote(blocks[at], blocks[at], x_out.at[2, turn, at], x_in.at[2, turn, at], near)
            for at in range(2)
        ]

    def y_copy(turn, at, part, relation, device):
        return remote(
            y_send.at[turn, at],
            y_ref.at[me, :, half_rows(part), :],
            y_out.at[relation, part],
            y_in.at[relation, part],
            device,
        )

    def d_copy(part, relation, device):
        return remote(
            dy_send.at[pl.ds(device * here, here), half_rows(part), :],
            dy_ref.at[:, part_rows(me, part), :],
            d_out.at[relation, part],
            d_in.at[relation, part],
            device,
        )

    def g_near(turn):
        rows = rows_of(back_chunk(turn))
        return remote(
            dx_send.at[near, rows], dx_near.at[rows], g_out.at[0, turn], g_in.at[0, turn], near
        )

    def g_help(turn):
        rows = rows_of(back_chunk(turn))
        return remote(
            dx_send.at[across, rows], dx_help.at[rows], g_out.at[1, turn], g_in.at[1, turn], near
        )

    def g_far(turn):
        rows = rows_of(back_chunk(turn))
        return remote(
            dx_sum.at[rows], dx_far.at[rows], g_out.at[2, turn], g_in.at[2, turn], far
        )

    for turn in range(peers):
        for copy in x_far(turn) + x_near(turn):
            copy.start()
    blocks_ref[me] = x_ref[...]
    limit = count_ref[0]
    for copy in w_copies:
        copy.wait()

    def pass_on(turn):
        for copy in x_far(turn):
            copy.wait_recv()
        for copy in x_hand(turn):
            copy.start()

    pass_on(0)

    def expert_step(turn, _):
        for copy in x_near(turn) + x_hand(turn):
            copy.wait_recv()

        @pl.when(turn < peers - 1)
        def _():
            pass_on(turn + 1)

        first, part, rows = ahead_rows(chip, turn)
        x = jnp.concatenate(
            [
                jnp.concatenate([blocks_ref[block, rows[at]] for block in range(peers)], axis=1)
                for at in range(2)
            ],
            axis=0,
        )
        for e in range(here):
            w_in = w_ref[:, e, :in_rows, :].reshape(peers * width, hid)
            act_ref[...] = dot(x, w_in) + b1_ref[e]

            def gelu_step(tile, _):
                at = pl.multiple_of(tile * 32, 32)
                value, slope = gelu_parts(act_ref[pl.ds(at, 32), :])
                place = lax.div(at, half)
                there = (first + place) * own + part * half + at - place * half
                there = pl.ds(pl.multiple_of(there, 32), 32)
                hid_ref[e, there, :] = value.astype(LOW)
                slope_ref[e, there, :] = slope
                return 0

            lax.fori_loop(0, own // 32, gelu_step, 0)
            w_out = w_ref[:, e, in_rows:, :].reshape(out_width, hid)
            hidden = jnp.concatenate([hid_ref[e, rows[at], :] for at in range(2)], axis=0)
            y = (dot(hidden, w_out, NT) + b2_ref[e]).astype(LOW)
            for at in range(2):
                y_send[turn, at, e] = y[at * half : (at + 1) * half]
        for at in range(2):
            device = first + at

            @pl.when(turn < 2)
            def _():
                y_copy(turn, at, part, 1 + lax.rem(side + at, 2), device).start()

            @pl.when(jnp.logical_and(turn >= 2, device != me))
            def _():
                y_copy(turn, at, part, 0, device).start()

            @pl.when(device == me)
            def _():
                y_ref[me, :, half_rows(part), :] = y_send[turn, at]

        return 0

    lax.fori_loop(0, peers, expert_step, 0)

    own_rows = rows_of(me)
    x_own = jnp.concatenate([blocks_ref[block, own_rows] for block in range(peers)], axis=1)
    logits = dot(x_own, wg_ref[...], NT) + bg_ref[...]
    for k in range(tasks):
        part = logits[:, k * experts : (k + 1) * experts]
        part = jnp.exp(part - jnp.max(part, axis=1, keepdims=True))
        gates_ref[:, k * experts : (k + 1) * experts] = part / jnp.sum(part, axis=1, keepdims=True)

    stats_ref[...] = jnp.zeros_like(stats_ref)

    def square_step(tile, total):
        at = pl.multiple_of(tile * 64, 64)
        valid = (lax.broadcasted_iota(I32, (64, 1), 0) + at) < limit
        part = jnp.where(valid, x_ref[pl.ds(at, 64), :].astype(F32), 0.0)
        return total + jnp.sum((part * part).reshape(8, 8, width), axis=0)

    x_square = lax.fori_loop(0, samples // 64, square_step, jnp.zeros((8, width), F32))
    stats_ref[experts + tasks, :, :width] = x_square
    tile_rows = 16

    def tile_of(tile):
        at = pl.multiple_of(tile * tile_rows, tile_rows)
        return at, pl.ds(at, tile_rows)

    def mix_step(tile, _):
        at, rows = tile_of(tile)
        valid = (lax.broadcasted_iota(I32, (tile_rows, 1), 0) + (at + me * own)) < limit
        gates = gates_ref[rows, :]
        mixed = [None] * tasks
        for e in range(experts):
            y = y_ref[e // here, e % here, rows, :].astype(F32)
            square = jnp.where(valid, y * y, 0.0)
            stats_ref[e] += square[:8] + square[8:]
            for k in range(tasks):
                term = gates[:, k * experts + e : k * experts + e + 1] * y
                mixed[k] = term if e == 0 else mixed[k] + term
        for k in range(tasks):
            square = jnp.where(valid, mixed[k] * mixed[k], 0.0)
            stats_ref[experts + k] += square[:8] + square[8:]
            mixb_ref[k, rows, :] = mixed[k].astype(LOW)
        return 0

    pack_ref[...] = jnp.zeros_like(pack_ref)
    blocks_x = peers * width // 128
    heads_at = blocks_x * tasks * experts
    tower_at = heads_at + tasks * tower_hid // 128
    outer_at = tower_at + tasks * tower_hid // 128
    rest_at = outer_at + experts * out_width // 128
    def tower_step(k, part):
        rows = half_rows(part)
        cols = slice(k * tower_hid, (k + 1) * tower_hid)
        z, slope = gelu_parts(dot(mixb_ref[k, rows, :], w3_ref[:, cols]) + tb1_ref[k : k + 1, :])
        head = heads_ref[k : k + 1, :]
        logit = jnp.sum(z * head, axis=1, keepdims=True) + tb2_ref[0, k]
        small = jnp.exp(-jnp.abs(logit))
        label = labels_ref[rows, k : k + 1].astype(F32)
        row_id = lax.broadcasted_iota(I32, (half, 1), 0) + (me * own + part * half)
        weight = jnp.where(row_id < limit, mask_ref[rows, k : k + 1].astype(F32), 0.0)
        soft = jnp.maximum(logit, 0.0) + jnp.log1p(small)
        loss = jnp.sum(weight * (soft - label * logit), axis=0, keepdims=True)
        stats_ref[experts + tasks + 1, :1, :1] += loss
        stats_ref[experts + tasks + 1, :1, 1:2] += jnp.sum(weight, axis=0, keepdims=True)
        chance = jnp.where(logit >= 0.0, 1.0, small) / (1.0 + small)
        dl = weight * (chance - label)
        g_head = jnp.sum(dl * z, axis=0, keepdims=True)
        dz = (dl * head * slope).astype(LOW)
        g_bias = jnp.sum(dz.astype(F32), axis=0, keepdims=True)
        for piece in range(tower_hid // 128):
            lane = slice(piece * 128, (piece + 1) * 128)
            at = k * (tower_hid // 128) + piece
            pack_ref[heads_at + at : heads_at + at + 1, :] += g_head[:, lane]
            pack_ref[tower_at + at : tower_at + at + 1, :] += g_bias[:, lane]
        pack_ref[rest_at + 1 : rest_at + 2, k : k + 1] += jnp.sum(dl, axis=0, keepdims=True)
        dz_ref[k, rows, :] = dz
        dmix_ref[k, rows, :] = dot(dz, w3_ref[:, cols], NT)

    def dy_step(tile, _):
        at, rows = tile_of(tile)
        gates = gates_ref[rows, :]
        dmix = [dmix_ref[k, rows, :] for k in range(tasks)]
        for e in range(experts):
            total = None
            for k in range(tasks):
                term = gates[:, k * experts + e : k * experts + e + 1] * dmix[k]
                total = term if k == 0 else total + term
            dy_send[e, rows, :] = total.astype(LOW)
        return 0

    def half_step(part, _):
        for relation, device in enumerate((near, far, across)):
            y_copy(0, 0, part, relation, device).wait_recv()
        tiles = half // tile_rows
        lax.fori_loop(part * tiles, (part + 1) * tiles, mix_step, 0)
        for k in range(tasks):
            tower_step(k, part)
        lax.fori_loop(part * tiles, (part + 1) * tiles, dy_step, 0)
        d_copy(part, 1, far).start()
        d_copy(part, 2, across).start()
        d_copy(part, 0, near).start()
        return 0

    lax.fori_loop(0, 2, half_step, 0)
    dy_ref[:, own_rows, :] = dy_send[pl.ds(me * here, here)]
    for k in range(tasks):
        cols = slice(k * tower_hid, (k + 1) * tower_hid)
        small_ref[:, cols] = dot(mixb_ref[k], dz_ref[k], TN).astype(LOW)
    ones = jnp.ones((8, own), LOW)
    for e in range(experts):
        g_outer = dot(ones, dy_send[e])
        for part in range(out_width // 128):
            at = outer_at + e * (out_width // 128) + part
            pack_ref[at : at + 1, :] = g_outer[:1, part * 128 : (part + 1) * 128]

    lane = lax.broadcasted_iota(I32, (tile_rows, tasks * experts), 1)

    def dg_step(tile, _):
        at, rows = tile_of(tile)
        dmix = [dmix_ref[k, rows, :] for k in range(tasks)]
        found = jnp.zeros((tile_rows, tasks * experts), F32)
        for e in range(experts):
            y = y_ref[e // here, e % here, rows, :].astype(F32)
            for k in range(tasks):
                value = jnp.sum(dmix[k] * y, axis=1, keepdims=True)
                found = jnp.where(lane == k * experts + e, value, found)
        dg_ref[rows, :] = found
        return 0

    lax.fori_loop(0, own // tile_rows, dg_step, 0)
    gates = gates_ref[...]
    dg = dg_ref[...]
    flat = (tasks * experts, tasks * experts)
    same = lax.broadcasted_iota(I32, flat, 0) // experts == lax.broadcasted_iota(I32, flat, 1) // experts
    mean = dot(gates * dg, same.astype(F32), precision=HIGH)
    dgl = (gates * (dg - mean)).astype(LOW)
    pack_ref[rest_at : rest_at + 1, : tasks * experts] = jnp.sum(
        dgl.astype(F32), axis=0, keepdims=True
    )
    g_gating = dot(dgl, x_own, TN)
    for part in range(blocks_x):
        at = part * tasks * experts
        pack_ref[at : at + tasks * experts, :] = g_gating[:, part * 128 : (part + 1) * 128]
    small_ref[:, tasks * tower_hid :] = pack_ref[...].astype(LOW)


    share = share_ref.shape[0]

    def share_rows(part):
        return pl.ds(pl.multiple_of(part * share, share), share)

    def core_copy():
        return pltpu.make_async_remote_copy(
            small_ref.at[pl.ds(pl.multiple_of((1 - side) * 2 * share, share), 2 * share)],
            core_recv,
            s_out.at[0],
            s_in.at[0],
            device_id={"dp": dp, "mp": near},
            device_id_type=MESH,
        )

    def pair_copy():
        return pltpu.make_async_remote_copy(
            pair_send,
            pair_recv,
            s_out.at[1],
            s_in.at[1],
            device_id={"dp": pair, "mp": me},
            device_id_type=MESH,
        )

    def core_sum(part):
        mine = small_ref[share_rows(side * 2 + part), :].astype(F32)
        return mine + core_recv[share_rows(part), :].astype(F32)

    core_copy().start()
    g_b1_ref[...] = jnp.zeros_like(g_b1_ref)

    gate_ref[...] = dot(dgl, wg_ref[...])

    def hand_on(turn):
        rows = rows_of(back_chunk(turn))
        g_help(turn).wait_recv()
        total = dx_send[far, rows].astype(F32) + dx_help[rows].astype(F32)
        dx_sum[rows] = total.astype(LOW)
        g_far(turn).start()

    act = jnp.ones((8, own), LOW)

    def chunk_step(turn, _):
        chunk = back_chunk(turn)
        rows = rows_of(chunk)

        @pl.when(jnp.logical_and(turn < 2, chunk != me))
        def _():
            for part in range(2):
                d_copy(part, 0, chunk).wait_recv()

        @pl.when(turn >= 2)
        def _():
            for part in range(2):
                d_copy(part, 1 + lax.rem(side + turn, 2), chunk).wait_recv()

        total = gate_ref[...] * jnp.where(chunk == me, 1.0, 0.0)
        for e in range(here):
            w_out = w_ref[:, e, in_rows:, :].reshape(out_width, hid)
            dpre = (dot(dy_ref[e, rows, :], w_out) * slope_ref[e, rows, :]).astype(LOW)
            dpre_ref[e, rows, :] = dpre
            g_b1_ref[e] += dot(act, dpre)
            w_in = w_ref[:, e, :in_rows, :].reshape(features, hid)
            total += dot(dpre, w_in, NT)
        for target in range(peers):
            dx_send[target, rows] = total[:, target * width : (target + 1) * width].astype(LOW)
        g_near(turn).start()
        g_help(turn).start()

        @pl.when(turn > 0)
        def _():
            hand_on(turn - 1)

        return 0

    lax.fori_loop(0, peers, chunk_step, 0)
    hand_on(peers - 1)
    core_copy().wait()
    pair_send[...] = core_sum(1 - dp_side).astype(LOW)
    pair_copy().start()

    lanes = parts_ref.shape[4]
    blocks_in = width // 128
    per_in = 128 // in_rows
    per_out = 128 // out_rows
    for e in range(here):

        def in_step(block, _):
            cols = pl.ds(pl.multiple_of(lax.rem(block, blocks_in) * 128, 128), 128)
            x = blocks_ref[lax.div(block, blocks_in), :, cols]
            value = dot(x, dpre_ref[e], TN).astype(LOW)
            for shard in range(per_in):
                for target in range(peers):
                    to = block * per_in + shard
                    away = lax.rem(to + dp, 2)
                    parts_ref[
                        away, lax.div(to, 2), target, e * rows_both : e * rows_both + in_rows, :
                    ] = value[
                        shard * in_rows : (shard + 1) * in_rows, target * lanes : (target + 1) * lanes
                    ]
            return 0

        lax.fori_loop(0, features // 128, in_step, 0)

        def out_step(block, _):
            cols = pl.ds(pl.multiple_of(block * 128, 128), 128)
            value = dot(dy_ref[e, :, cols], hid_ref[e], TN).astype(LOW)
            for shard in range(per_out):
                for target in range(peers):
                    to = block * per_out + shard
                    away = lax.rem(to + dp, 2)
                    parts_ref[
                        away,
                        lax.div(to, 2),
                        target,
                        e * rows_both + in_rows : (e + 1) * rows_both,
                        :,
                    ] = value[
                        shard * out_rows : (shard + 1) * out_rows,
                        target * lanes : (target + 1) * lanes,
                    ]
            return 0

        lax.fori_loop(0, out_width // 128, out_step, 0)

    pair_copy().wait()
    share_ref[...] = (core_sum(dp_side) + pair_recv[...].astype(F32)).astype(LOW)
    for turn in range(peers):
        g_near(turn).wait()
        g_far(turn).wait()
    dx_ref[...] = dx_send[me].astype(F32) + dx_near[...].astype(F32) + dx_far[...].astype(F32)
    for turn in range(peers):
        g_help(turn).wait_send()
        for copy in x_far(turn) + x_near(turn) + x_hand(turn):
            copy.wait_send()
    for relation, device in enumerate((near, far, across)):
        for part in range(2):
            y_copy(0, 0, part, relation, device).wait_send()
            d_copy(part, relation, device).wait_send()


def total_kernel(
    features,
    width_out,
    valid_ref,
    inner_ref,
    stats_ref,
    tables_ref,
    shares_ref,
    grads_ref,
    inner_out,
    result_ref,
    pay_ref,
    got_ref,
    t_out,
    t_in,
):
    devices = got_ref.shape[0]
    peers = inner_out.shape[0]
    here, _, hid = inner_ref.shape
    inner_rows = inner_out.shape[1]
    number = stats_ref.shape[0] - 2
    me = lax.axis_index("dp") * peers + lax.axis_index("mp")
    barrier = pltpu.get_barrier_semaphore()

    def greet(step, _):
        target = lax.rem(me + step, devices)
        pl.semaphore_signal(barrier, inc=1, device_id=place_of(target, peers), device_id_type=MESH)
        return 0

    lax.fori_loop(1, devices, greet, 0)
    lane = lax.broadcasted_iota(I32, (1, 128), 1)

    def whole_sum(value):
        return jnp.sum(jnp.sum(value, axis=0, keepdims=True), axis=1, keepdims=True)

    def grad_step(at, total):
        rows = grads_ref[pl.ds(pl.multiple_of(at * 64, 64), 64), :]
        return total + jnp.sum((rows * rows).reshape(8, 8, 128), axis=0)

    squares = lax.fori_loop(0, grads_ref.shape[0] // 64, grad_step, tables_ref[...])
    share = shares_ref[...]
    vector = jnp.where(lane == 0, stats_ref[number + 1, :1, :1], 0.0)
    vector = jnp.where(lane == 1, stats_ref[number + 1, :1, 1:2], vector)
    for at in range(number + 1):
        vector = jnp.where(lane == at + 2, whole_sum(stats_ref[at]), vector)
    vector = jnp.where(lane == number + 3, whole_sum(squares) + whole_sum(share * share), vector)
    pay_ref[...] = jnp.zeros_like(pay_ref)
    for e in range(here):
        for part in range(hid // 128):
            at = e * (hid // 128) + part
            pay_ref[at : at + 1, :] = inner_ref[e, :1, part * 128 : (part + 1) * 128]
    pay_ref[inner_rows : inner_rows + 1, :] = vector
    got_ref[me] = pay_ref[...]
    pl.semaphore_wait(barrier, devices - 1)

    def t_copy(step):
        target = lax.rem(me + step, devices)
        return pltpu.make_async_remote_copy(
            pay_ref,
            got_ref.at[me],
            t_out.at[step],
            t_in.at[step],
            device_id=place_of(target, peers),
            device_id_type=MESH,
        )

    def start(step, _):
        t_copy(step).start()
        return 0

    def finish(step, _):
        t_copy(step).wait()
        return 0

    lax.fori_loop(1, devices, start, 0)
    lax.fori_loop(1, devices, finish, 0)
    total = jnp.zeros((1, 128), F32)
    inner_sq = jnp.zeros((inner_rows, 128), F32)
    for group in range(peers):
        part = jnp.zeros((inner_rows, 128), F32)
        for block in range(devices // peers):
            source = block * peers + group
            part = part + got_ref[source, :inner_rows, :]
            total = total + got_ref[source, inner_rows : inner_rows + 1, :]
        inner_out[group] = part
        inner_sq = inner_sq + part * part

    def pick(at):
        return jnp.sum(jnp.where(lane == at, total, 0.0), axis=1, keepdims=True)

    weight = pick(1)
    grad_norm = jnp.sqrt(pick(number + 3) + whole_sum(inner_sq)) / weight
    factor = jnp.minimum(1.0, clip_max / grad_norm) / weight
    count = valid_ref[0].astype(F32)
    width = jnp.where(lane == number + 2, float(features), float(width_out))
    result_ref[...] = jnp.zeros_like(result_ref)
    result_ref[0:1, :] = jnp.broadcast_to(factor, (1, 128))
    result_ref[1:2, :] = jnp.broadcast_to(grad_norm, (1, 128))
    result_ref[2:3, :] = total
    result_ref[3:4, :] = jnp.sqrt(total / (count * width) + stat_eps)


def table_kernel(factor_ref, weight_ref, first_ref, second_ref, grad_ref, *outs):
    pair, width, rows = weight_ref.shape
    gradient = grad_ref[0].astype(F32).T.reshape(pair, width, rows) * factor_ref[:1, :1].reshape(1, 1, 1)
    results = adamw(weight_ref[...], first_ref[...], second_ref[...], gradient, rate_table)
    for out, result in zip(outs, results):
        out[...] = result


def small_kernel(
    tasks,
    experts,
    result_ref,
    whole_ref,
    t0_ref,
    t1_ref,
    t2_ref,
    g0_ref,
    g1_ref,
    g2_ref,
    h0_ref,
    h1_ref,
    h2_ref,
    t0_out,
    t1_out,
    t2_out,
    g0_out,
    g1_out,
    g2_out,
    h0_out,
    h1_out,
    h2_out,
    pack_ref,
):
    step = pl.program_id(0)
    peers = lax.axis_size("mp")
    groups = lax.axis_size("dp")
    rows, width = t0_ref.shape
    unit = whole_ref.shape[1]
    factor = result_ref[:1, :1]
    core, side = lax.div(step, 2), lax.rem(step, 2)
    for first in range(groups // 2):
        for second in range(peers // 2):
            source = (2 * first + side) * peers + 2 * second + core
            at = (first * (peers // 2) + second) * unit
            value = whole_ref[source]
            here = slice(at, at + unit)
            results = adamw(
                t0_ref[here, :],
                t1_ref[here, :],
                t2_ref[here, :],
                value[:, :width].astype(F32) * factor,
                rate_dense,
            )
            for out, result in zip((t0_out, t1_out, t2_out), results):
                out[here, :] = result
            pack_ref[pl.ds(step * rows + at, unit), :] = value[:, width:].astype(F32)

    @pl.when(step == pl.num_programs(0) - 1)
    def _():
        gates = tasks * experts
        features = g0_ref.shape[1]
        for part in range(features // 128):
            lane = slice(part * 128, (part + 1) * 128)
            results = adamw(
                g0_ref[:, lane],
                g1_ref[:, lane],
                g2_ref[:, lane],
                pack_ref[part * gates : (part + 1) * gates, :] * factor,
                rate_dense,
            )
            for out, result in zip((g0_out, g1_out, g2_out), results):
                out[:, lane] = result
        heads_at = features // 128 * gates
        parts = h0_ref.shape[1] // 128
        for task in range(tasks):
            for part in range(parts):
                lane = slice(part * 128, (part + 1) * 128)
                at = heads_at + task * parts + part
                row = slice(task, task + 1)
                results = adamw(
                    h0_ref[row, lane],
                    h1_ref[row, lane],
                    h2_ref[row, lane],
                    pack_ref[at : at + 1, :] * factor,
                    rate_dense,
                )
                for out, result in zip((h0_out, h1_out, h2_out), results):
                    out[row, lane] = result


def body(
    row_ids,
    counts,
    labels,
    label_mask,
    embeddings,
    embed_first,
    embed_second,
    expert_in,
    in_first,
    in_second,
    expert_out,
    out_first,
    out_second,
    gating,
    gating_first,
    gating_second,
    towers,
    towers_first,
    towers_second,
    heads,
    heads_first,
    heads_second,
    biases,
    biases_first,
    biases_second,
):
    devices = lax.axis_size(AXES)
    mp_count = lax.axis_size("mp")
    dp_count = lax.axis_size("dp")
    mp_index = lax.axis_index("mp")
    samples, tables_here = row_ids.shape
    tables, rows_dev, d_emb = embeddings.shape
    own = samples // mp_count
    requests = samples * tables_here
    capacity = 2 * requests // devices
    height = capacity // 2
    slots = devices * height
    row_bits = rows_dev.bit_length() - 1
    pairs = tables // 2
    lanes = 2 * d_emb
    group_rows = tables_here // 2 * rows_dev
    in_rows, out_rows = expert_in.shape[0], expert_out.shape[0]
    experts_here = EXPERTS // mp_count
    hid = expert_in.shape[2] * mp_count
    features = tables * d_emb
    width_out = out_rows * dp_count
    tower_hid = towers.shape[1] // TASKS

    in_out_rows = in_rows + out_rows
    hid_here = hid // mp_count
    sides = [
        [d * mp_count + m for d in range(x, dp_count, 2) for m in range(mp_count)] for x in range(2)
    ]
    partners = [(d, d ^ 1) for d in range(dp_count)]

    def exchange_side(parts):
        return lax.all_to_all(
            parts, AXES, split_axis=0, concat_axis=0, axis_index_groups=sides, tiled=True
        )

    def exchange_all(parts):
        return lax.all_to_all(parts, AXES, split_axis=0, concat_axis=0, tiled=True)

    def sems(*shape):
        return pltpu.SemaphoreType.DMA(shape)

    codes, shard, place, slot, source = pl.pallas_call(
        functools.partial(ask_kernel, row_bits),
        out_shape=(
            jax.ShapeDtypeStruct((devices, 1, capacity), I32),
            jax.ShapeDtypeStruct((experts_here, in_out_rows, hid), LOW),
            jax.ShapeDtypeStruct((tables_here, samples), I32),
            jax.ShapeDtypeStruct((tables_here, samples), I32),
            jax.ShapeDtypeStruct((tables_here, samples), I32),
        ),
        in_specs=[VMEM] * 3,
        out_specs=(VMEM,) * 5,
        scratch_shapes=[
            pltpu.VMEM((devices, 1, capacity), I32),
            pltpu.VMEM((EXPERTS, in_out_rows, hid_here), LOW),
            sems(devices),
            sems(devices),
            sems(mp_count),
            sems(mp_count),
        ],
        compiler_params=pltpu.CompilerParams(
            vmem_limit_bytes=32 * MIB, collective_id=2, has_side_effects=True
        ),
        name="ask",
    )(row_ids.T, expert_in, expert_out)
    w_far = []
    for ahead in range(1, dp_count // 2):
        steps = [(d, (d + 2 * ahead) % dp_count) for d in range(dp_count)]
        w_far.append(lax.ppermute(shard, "dp", steps))
    w_near = lax.ppermute(shard, "dp", partners)
    codes = codes.reshape(devices, capacity)
    asked = codes[:, 0] >> 16
    plain = codes & 65535
    found_at = jnp.maximum(plain - 1, 0)
    table_at = found_at >> row_bits
    sum_at = (table_at >> 1) * rows_dev + (found_at & (rows_dev - 1))
    number = jnp.arange(capacity, dtype=I32)[None, :]
    turned_at = ((table_at ^ number) & 1) * group_rows + sum_at
    part_at = ((number & 1) * 2 + (table_at & 1)) * slots + (number >> 1)
    part_at = part_at + jnp.arange(devices, dtype=I32)[:, None] * height
    part_at = jnp.where(plain > 0, part_at, 4 * slots)

    table_view = jnp.transpose(embeddings, (0, 2, 1))
    found = pl.pallas_call(
        functools.partial(find_kernel, mp_count),
        grid=(mp_count,),
        out_shape=jax.ShapeDtypeStruct((dp_count, mp_count, height, lanes), LOW),
        in_specs=[
            SMEM,
            SMEM,
            pl.BlockSpec((tables_here, d_emb, rows_dev), lambda m: (m, 0, 0)),
        ],
        out_specs=pl.BlockSpec((dp_count, 1, height, lanes), lambda m: (0, m, 0, 0)),
        scratch_shapes=[
            pltpu.VMEM((tables_here * rows_dev, lanes), F32),
            pltpu.VMEM((height, lanes), F32),
        ],
        compiler_params=params(60),
        name="find",
    )(turned_at.reshape(-1), asked, table_view)
    w_far, w_near, found = lax.optimization_barrier((w_far, w_near, found))
    w_mine = [shard] + w_far
    w_theirs = [w_near] + [lax.ppermute(line, "dp", partners) for line in w_far]
    returned = exchange_all(found.reshape(devices, height, lanes))
    embedded = pl.pallas_call(
        place_kernel,
        out_shape=jax.ShapeDtypeStruct((samples, tables_here * d_emb), LOW),
        in_specs=[SMEM, VMEM],
        out_specs=VMEM,
        scratch_shapes=[
            pltpu.VMEM((2 * slots, lanes), F32),
            pltpu.VMEM((tables_here // 2, samples, lanes), F32),
        ],
        compiler_params=params(32),
        name="place",
    )(place.reshape(-1), returned.reshape(slots, lanes))

    first = EXPERTS * hid
    second = first + EXPERTS * width_out
    third = second + TASKS * EXPERTS
    fourth = third + TASKS * tower_hid
    inner_here = lax.dynamic_index_in_dim(
        biases[:first].reshape(mp_count, experts_here, 1, hid), mp_index, 0, keepdims=False
    )
    outer_here = lax.dynamic_index_in_dim(
        biases[first:second].reshape(mp_count, experts_here, 1, width_out),
        mp_index,
        0,
        keepdims=False,
    )
    gating_low = gating.T.astype(LOW)
    all_gates = TASKS * EXPERTS
    pack_rows = width_out

    def scratch(shape, kind=F32):
        return pltpu.VMEM(shape, kind)

    pack_shape = (pack_rows // 4, TASKS * tower_hid + 128)
    x_shape = (samples, tables_here * d_emb)
    stat_parts, embed_grad, grad_parts, inner_parts, share = pl.pallas_call(
        functools.partial(dense_kernel, dp_count // 2),
        out_shape=(
            jax.ShapeDtypeStruct((EXPERTS + TASKS + 2, 8, width_out), F32),
            jax.ShapeDtypeStruct(x_shape, F32),
            jax.ShapeDtypeStruct(
                (2, dp_count // 2, mp_count, experts_here * in_out_rows, hid_here), LOW
            ),
            jax.ShapeDtypeStruct((experts_here, 8, hid), F32),
            jax.ShapeDtypeStruct(pack_shape, LOW),
        ),
        in_specs=[pl.BlockSpec(memory_space=pl.ANY)] * dp_count
        + [SMEM]
        + [VMEM] * 8
        + [SMEM]
        + [VMEM] * 2,
        out_specs=(VMEM,) * 5,
        scratch_shapes=[
            scratch((dp_count, experts_here, in_out_rows, hid), LOW),
            scratch((mp_count,) + x_shape, LOW),
            scratch((experts_here, samples, hid), LOW),
            scratch((experts_here, samples, hid)),
            scratch((experts_here, samples, width_out), LOW),
            scratch((mp_count, 2, experts_here, own // 2, width_out), LOW),
            scratch((mp_count, experts_here, own, width_out), LOW),
            scratch((own, all_gates)),
            scratch((TASKS, own, width_out), LOW),
            scratch((TASKS, own, tower_hid), LOW),
            scratch((TASKS, own, width_out)),
            scratch((own, all_gates)),
            scratch((EXPERTS, own, width_out), LOW),
            scratch((pack_rows, TASKS * tower_hid + 128), LOW),
            scratch((pack_rows, 128)),
            scratch((own, hid)),
            scratch((own, features)),
            scratch((experts_here, samples, hid), LOW),
            scratch((mp_count,) + x_shape, LOW),
            scratch(x_shape, LOW),
            scratch(x_shape, LOW),
            scratch(x_shape, LOW),
            scratch(x_shape, LOW),
            scratch((2 * pack_shape[0], pack_shape[1]), LOW),
            scratch(pack_shape, LOW),
            scratch(pack_shape, LOW),
            sems(3, mp_count, 2),
            sems(3, mp_count, 2),
            sems(3, 2),
            sems(3, 2),
            sems(3, 2),
            sems(3, 2),
            sems(3, mp_count),
            sems(3, mp_count),
            sems(2),
            sems(2),
            sems(2, dp_count // 2),
        ],
        compiler_params=pltpu.CompilerParams(
            vmem_limit_bytes=60 * MIB, collective_id=0, has_side_effects=True
        ),
        name="dense",
    )(
        *w_mine,
        *w_theirs,
        lax.dynamic_slice_in_dim(counts, lax.axis_index("dp"), 1, 0),
        embedded,
        inner_here,
        outer_here,
        gating_low,
        biases[second:third].reshape(1, all_gates),
        towers.astype(LOW),
        biases[third:fourth].reshape(TASKS, tower_hid),
        heads,
        biases[fourth:].reshape(1, TASKS),
        labels,
        label_mask,
    )

    back_rows = pl.pallas_call(
        send_kernel,
        out_shape=jax.ShapeDtypeStruct((slots, lanes), LOW),
        in_specs=[SMEM, SMEM, VMEM],
        out_specs=VMEM,
        scratch_shapes=[
            pltpu.VMEM((tables_here // 2, 2 * samples, lanes), F32),
            pltpu.VMEM((2 * slots, lanes), F32),
        ],
        compiler_params=params(32),
        name="send",
    )(slot.reshape(-1), source.reshape(-1), embed_grad)
    share = share.reshape(devices // 4, pack_rows // devices, -1)
    arrived, shares = pl.pallas_call(
        swap_kernel,
        out_shape=(
            jax.ShapeDtypeStruct((devices, height, lanes), LOW),
            jax.ShapeDtypeStruct(share.shape, LOW),
        ),
        in_specs=[VMEM, VMEM],
        out_specs=(VMEM, VMEM),
        scratch_shapes=[sems(devices), sems(devices), sems(devices // 4), sems(devices // 4)],
        compiler_params=pltpu.CompilerParams(
            vmem_limit_bytes=16 * MIB, collective_id=3, has_side_effects=True
        ),
        name="swap",
    )(back_rows.reshape(devices, height, lanes), share)
    share = jnp.sum(shares.astype(F32), axis=0)
    partner = lax.ppermute(grad_parts[1], "dp", partners)
    partner, arrived = lax.optimization_barrier((partner, arrived))
    grad_parts = (grad_parts[0].astype(F32) + partner.astype(F32)).astype(LOW)
    grad_parts = exchange_side(
        grad_parts.reshape(devices // 2, experts_here * in_out_rows, hid_here)
    )
    grad_sum = jnp.sum(
        grad_parts.reshape(dp_count // 2, mp_count, experts_here, in_out_rows, -1).astype(F32), 0
    )
    owned = grad_sum.reshape(EXPERTS, in_out_rows, -1).transpose(1, 0, 2)
    in_sum, out_sum = owned[:in_rows], owned[in_rows:]

    table_grad, table_sq = pl.pallas_call(
        functools.partial(add_kernel, mp_count),
        out_shape=(
            jax.ShapeDtypeStruct((pairs * rows_dev, lanes), LOW),
            jax.ShapeDtypeStruct((8, lanes), F32),
        ),
        in_specs=[SMEM, SMEM, SMEM, VMEM],
        out_specs=(pl.BlockSpec(memory_space=pl.ANY), VMEM),
        scratch_shapes=[
            pltpu.VMEM((4 * slots + 8, lanes), F32),
            pltpu.VMEM((mp_count, group_rows, lanes), LOW),
            pltpu.SemaphoreType.DMA((mp_count,)),
        ]
        + [pltpu.VMEM((group_rows, lanes), F32)] * mp_count,
        compiler_params=params(60),
        name="add",
    )(sum_at.reshape(-1), part_at.reshape(-1), asked, arrived.reshape(slots, lanes))

    stat_end = EXPERTS + TASKS
    inner_rows = experts_here * hid // 128
    pay_rows = inner_rows + 8
    inner_sum, result = pl.pallas_call(
        functools.partial(total_kernel, features, width_out),
        out_shape=(
            jax.ShapeDtypeStruct((mp_count, inner_rows, 128), F32),
            jax.ShapeDtypeStruct((8, 128), F32),
        ),
        in_specs=[SMEM] + [VMEM] * 5,
        out_specs=(VMEM,) * 2,
        scratch_shapes=[
            scratch((pay_rows, 128)),
            scratch((devices, pay_rows, 128)),
            sems(devices),
            sems(devices),
        ],
        compiler_params=pltpu.CompilerParams(
            vmem_limit_bytes=16 * MIB, collective_id=4, has_side_effects=True
        ),
        name="total",
    )(
        jnp.sum(counts).reshape(1),
        inner_parts,
        stat_parts,
        table_sq,
        share,
        grad_sum.reshape(-1, 128),
    )
    factor = result[0, 0]
    share_low, result = lax.optimization_barrier((share.astype(LOW), result))
    whole = exchange_all(jnp.broadcast_to(share_low[None], (devices,) + share_low.shape))

    table_spec = pl.BlockSpec((2, d_emb, rows_dev), lambda p: (p, 0, 0))
    embed_out = pl.pallas_call(
        table_kernel,
        grid=(pairs,),
        out_shape=(jax.ShapeDtypeStruct(table_view.shape, F32),) * 3,
        in_specs=[
            pl.BlockSpec((8, 128), lambda p: (0, 0)),
            table_spec,
            table_spec,
            table_spec,
            pl.BlockSpec((1, rows_dev, lanes), lambda p: (p, 0, 0)),
        ],
        out_specs=(table_spec,) * 3,
        compiler_params=params(58),
        name="tables",
    )(
        result,
        table_view,
        jnp.transpose(embed_first, (0, 2, 1)),
        jnp.transpose(embed_second, (0, 2, 1)),
        table_grad.reshape(pairs, rows_dev, lanes),
    )
    embed_out = [jnp.transpose(value, (0, 2, 1)) for value in embed_out]
    in_out = adamw(expert_in, in_first, in_second, in_sum * factor, rate_dense)
    out_out = adamw(expert_out, out_first, out_second, out_sum * factor, rate_dense)
    whole, embed_out = lax.optimization_barrier((whole, embed_out))
    blocks_x = features // 128
    heads_at = blocks_x * all_gates
    tower_at = heads_at + TASKS * tower_hid // 128
    outer_at = tower_at + TASKS * tower_hid // 128
    rest_at = outer_at + EXPERTS * width_out // 128
    tower_spec = pl.BlockSpec((pack_rows // 4, TASKS * tower_hid), lambda c: (c, 0))
    gate_spec = pl.BlockSpec((all_gates, features), lambda c: (0, 0))
    head_spec = pl.BlockSpec((TASKS, tower_hid), lambda c: (0, 0))
    *small_out, packed = pl.pallas_call(
        functools.partial(small_kernel, TASKS, EXPERTS),
        grid=(4,),
        out_shape=(jax.ShapeDtypeStruct(towers.shape, F32),) * 3
        + (jax.ShapeDtypeStruct((all_gates, features), F32),) * 3
        + (jax.ShapeDtypeStruct(heads.shape, F32),) * 3
        + (jax.ShapeDtypeStruct((pack_rows, 128), F32),),
        in_specs=[
            pl.BlockSpec((8, 128), lambda c: (0, 0)),
            pl.BlockSpec(whole.shape, lambda c: (0, 0, 0)),
        ]
        + [tower_spec] * 3
        + [gate_spec] * 3
        + [head_spec] * 3,
        out_specs=(tower_spec,) * 3
        + (gate_spec,) * 3
        + (head_spec,) * 3
        + (pl.BlockSpec((pack_rows, 128), lambda c: (0, 0)),),
        compiler_params=params(48),
        name="small",
    )(
        result,
        whole,
        towers,
        towers_first,
        towers_second,
        gating.T,
        gating_first.T,
        gating_second.T,
        heads,
        heads_first,
        heads_second,
    )
    towers_out, heads_out = small_out[:3], small_out[6:]
    gating_out = [value.T for value in small_out[3:6]]
    bias_sum = jnp.concatenate(
        [
            inner_sum.reshape(-1),
            packed[outer_at:rest_at].reshape(-1),
            packed[rest_at, :all_gates],
            packed[tower_at:outer_at].reshape(-1),
            packed[rest_at + 1, :TASKS],
        ]
    )
    biases_out = adamw(biases, biases_first, biases_second, bias_sum * factor, rate_dense)
    stats = jnp.concatenate([result[3, stat_end + 2][None], result[3, 2 : stat_end + 2]])
    loss = result[2, :2]
    return (
        *embed_out,
        *in_out,
        in_out[0].astype(LOW),
        *out_out,
        out_out[0].astype(LOW),
        *gating_out,
        *towers_out,
        *heads_out,
        *biases_out,
        result[1, :1],
        loss,
        stats,
    )


def solution(mesh):
    rows = P(None, AXES, None)
    expert = P("dp", None, "mp")
    sample = P(AXES, None)
    placed = (P("dp", "mp"), P(), sample, sample) + (rows,) * 3 + (expert,) * 6 + (P(),) * 12
    results = (rows,) * 3 + (expert,) * 8 + (P(),) * 15
    return jax.shard_map(body, mesh=mesh, in_specs=placed, out_specs=results, check_vma=False)
```

```python
import functools
import math

import jax
import jax.numpy as jnp
from jax import lax
from jax.experimental import pallas as pl
from jax.experimental.pallas import tpu as pltpu
from jax.sharding import PartitionSpec as P

EXPERTS = 8
TASKS = 5
STEP = 3

HIGH = lax.Precision.HIGHEST
beta_one = 0.5
beta_two = 0.5
adam_eps = 1e-08
decay = 0.01
clip_max = 0.002
rate_table = 0.5
rate_dense = 0.02
stat_eps = 1e-06

LOW = jnp.bfloat16
F32 = jnp.float32
I32 = jnp.int32
MIB = 1024 * 1024
AXES = ("dp", "mp")


def params(mib):
    return pltpu.CompilerParams(vmem_limit_bytes=mib * MIB)


VMEM = pl.BlockSpec(memory_space=pltpu.VMEM)
SMEM = pl.BlockSpec(memory_space=pltpu.SMEM)


def adamw(weight, first, second, gradient, rate):
    first_next = beta_one * first + (1.0 - beta_one) * gradient
    second_next = beta_two * second + (1.0 - beta_two) * gradient * gradient
    corrected = first_next / (1.0 - beta_one**STEP)
    scaled = jnp.sqrt(second_next / (1.0 - beta_two**STEP))
    return (
        weight - rate * (corrected / (scaled + adam_eps) + decay * weight),
        first_next,
        second_next,
    )


def route(row_bits, ids_ref, out_ref, place_ref, slot_ref, from_ref):
    devices, _, capacity = out_ref.shape
    tables, samples = ids_ref.shape
    rows_dev = 1 << row_bits
    halves = devices * capacity // 2
    width = 256
    upper = (
        lax.broadcasted_iota(I32, (width, width), 0) <= lax.broadcasted_iota(I32, (width, width), 1)
    ).astype(LOW)
    owners = lax.broadcasted_iota(I32, (devices, width), 0)
    slots = lax.broadcasted_iota(I32, (capacity, width), 0)
    carry = jnp.zeros((devices, 1), F32)
    total = jnp.zeros((2 * devices, capacity), F32)
    for table in range(tables):
        parity = table % 2
        for part in range(samples // width):
            cols = pl.ds(part * width, width)
            ids = ids_ref[pl.ds(table, 1), cols]
            owner = ids >> row_bits
            code = table * rows_dev + (ids & (rows_dev - 1)) + 1
            onehot = (owner == owners).astype(F32)
            counted = jnp.dot(onehot.astype(LOW), upper, preferred_element_type=F32) + carry
            rank = jnp.sum(onehot * counted, axis=0, keepdims=True).astype(I32) - 1
            carry = counted[:, width - 1 :]
            at_slot = (rank == slots).astype(LOW)
            high = (code >> 7).astype(F32)
            low = (code & 127).astype(F32)
            pieces = jnp.concatenate([onehot * high, onehot * low], axis=0).astype(LOW)
            total += lax.dot_general(
                pieces, at_slot, (((1,), (1,)), ((), ())), preferred_element_type=F32
            )
            row = owner * (capacity // 2) + (rank >> 1)
            half = rank & 1
            place_ref[pl.ds(table, 1), cols] = (half ^ parity) * halves + row
            slot_ref[pl.ds(table, 1), cols] = half * halves + row
            sample = lax.broadcasted_iota(I32, (1, width), 1) + part * width
            from_ref[pl.ds(table, 1), cols] = (half ^ parity) * samples + sample
    codes = (total[:devices] * 128.0 + total[devices:]).astype(I32)
    first = lax.broadcasted_iota(I32, (devices, capacity), 1) == 0
    counted = jnp.where(first, carry * 65536.0, 0.0).astype(I32)
    out_ref[...] = (codes + counted).reshape(devices, 1, capacity)


def left_lanes(shape):
    return lax.broadcasted_iota(I32, shape, len(shape) - 1) < 64


def find_kernel(groups, first_group, at_ref, counts_ref, table_ref, *refs):
    out_ref, turned_ref, rows_ref = refs[-3:]
    blocks, _, height, lanes = out_ref.shape
    tables, width, rows_dev = table_ref.shape
    group = pl.program_id(0) + first_group
    left = left_lanes((1, lanes))
    part = 512

    total = tables // 2 * rows_dev

    def turn_step(step, _):
        pair = lax.div(step, rows_dev // part)
        first = pl.multiple_of(lax.rem(step, rows_dev // part) * part, part)
        columns = table_ref[pl.ds(2 * pair, 2), :, pl.ds(first, part)]
        rows = columns.reshape(2 * width, part).T
        at = pl.multiple_of(step * part, part)
        turned_ref[pl.ds(at, part), :] = rows
        turned_ref[pl.ds(total + at, part), :] = pltpu.roll(rows, width, 1)
        return 0

    lax.fori_loop(0, total // part, turn_step, 0)

    def block_step(block, _):
        source = block * groups + group
        base = source * 2 * height

        def step(outer, _):
            got = []
            for inner in range(16):
                at = outer * 16 + inner
                even = turned_ref[pl.ds(at_ref[base + 2 * at], 1), :]
                odd = turned_ref[pl.ds(at_ref[base + 2 * at + 1], 1), :]
                got.append((at, jnp.where(left, even, odd)))
            for at, row in got:
                rows_ref[pl.ds(at, 1), :] = row
            return 0

        lax.fori_loop(0, (counts_ref[source] + 31) // 32, step, 0)
        out_ref[block, 0] = rows_ref[...].astype(LOW)
        return 0

    lax.fori_loop(0, blocks, block_step, 0)


def place_kernel(place_ref, rows_ref, out_ref, both_ref, flat_ref):
    count, lanes = rows_ref.shape
    samples = out_ref.shape[0]
    tables = place_ref.shape[0] // samples
    rows = rows_ref[...].astype(F32)
    both_ref[pl.ds(0, count), :] = rows
    both_ref[pl.ds(count, count), :] = pltpu.roll(rows, 64, 1)
    left = left_lanes((1, lanes))

    def step(outer, _):
        got = []
        for inner in range(8):
            sample = outer * 8 + inner
            for pair in range(tables // 2):
                even = both_ref[pl.ds(place_ref[2 * pair * samples + sample], 1), :]
                odd = both_ref[pl.ds(place_ref[(2 * pair + 1) * samples + sample], 1), :]
                got.append((pair, sample, jnp.where(left, even, odd)))
        for pair, sample, row in got:
            flat_ref[pair, pl.ds(sample, 1), :] = row
        return 0

    lax.fori_loop(0, samples // 8, step, 0)
    for pair in range(tables // 2):
        out_ref[:, pair * lanes : (pair + 1) * lanes] = flat_ref[pair].astype(LOW)


def send_kernel(slot_ref, from_ref, grad_ref, out_ref, both_ref, rows_ref):
    count, lanes = out_ref.shape
    samples = grad_ref.shape[0]
    tables = slot_ref.shape[0] // samples
    for pair in range(tables // 2):
        rows = grad_ref[:, pair * lanes : (pair + 1) * lanes]
        both_ref[pair, pl.ds(0, samples), :] = rows
        both_ref[pair, pl.ds(samples, samples), :] = pltpu.roll(rows, 64, 1)

    def step(outer, _):
        got = []
        for inner in range(8):
            sample = outer * 8 + inner
            for table in range(tables):
                row = both_ref[table // 2, pl.ds(from_ref[table * samples + sample], 1), :]
                got.append((slot_ref[table * samples + sample], row))
        for slot, row in got:
            rows_ref[pl.ds(slot, 1), :] = row
        return 0

    lax.fori_loop(0, samples // 8, step, 0)
    left = left_lanes((count, lanes))
    out_ref[...] = jnp.where(
        left, rows_ref[pl.ds(0, count), :], rows_ref[pl.ds(count, count), :]
    ).astype(LOW)


def swap_kernel(rows_ref, share_ref, out_ref, shares_ref, r_out, r_in, s_out, s_in):
    devices = rows_ref.shape[0]
    groups = share_ref.shape[0]
    peers = lax.axis_size("mp")
    dp, mp = lax.axis_index("dp"), lax.axis_index("mp")
    mine = lax.div(dp, 2) * (peers // 2) + lax.div(mp, 2)
    me = dp * peers + mp
    greet_all(devices, peers, me)

    def r_copy(step):
        target = lax.rem(me + step, devices)
        return pltpu.make_async_remote_copy(
            rows_ref.at[target],
            out_ref.at[me],
            r_out.at[step],
            r_in.at[step],
            device_id=place_of(target, peers),
            device_id_type=MESH,
        )

    def s_copy(step):
        target = lax.rem(mine + step, groups)
        to_dp = lax.div(target, peers // 2) * 2 + lax.rem(dp, 2)
        to_mp = lax.rem(target, peers // 2) * 2 + lax.rem(mp, 2)
        return pltpu.make_async_remote_copy(
            share_ref.at[target],
            shares_ref.at[mine],
            s_out.at[step],
            s_in.at[step],
            device_id={"dp": to_dp, "mp": to_mp},
            device_id_type=MESH,
        )

    def loop(first, copies, act):
        def step(at, _):
            act(copies(at))
            return 0

        lax.fori_loop(1, first, step, 0)

    loop(devices, r_copy, lambda copy: copy.start())
    loop(groups, s_copy, lambda copy: copy.start())
    out_ref[me] = rows_ref[me]
    shares_ref[mine] = share_ref[mine]
    loop(groups, s_copy, lambda copy: copy.wait())
    loop(devices, r_copy, lambda copy: copy.wait())


def add_kernel(
    groups, at_ref, part_at_ref, counts_ref, rows_ref, out_ref, square_ref, parts_ref, low_ref, sems, *sums
):
    count, lanes = rows_ref.shape
    sources = counts_ref.shape[0]
    height = count // sources
    table_rows = sums[0].shape[0]
    left = left_lanes((count, lanes))
    rows = rows_ref[...].astype(F32)
    turned = pltpu.roll(rows, 64, 1)
    parts_ref[pl.ds(0, count), :] = jnp.where(left, rows, 0.0)
    parts_ref[pl.ds(count, count), :] = jnp.where(left, 0.0, turned)
    parts_ref[pl.ds(2 * count, count), :] = jnp.where(left, turned, 0.0)
    parts_ref[pl.ds(3 * count, count), :] = jnp.where(left, 0.0, rows)
    parts_ref[pl.ds(4 * count, 8), :] = jnp.zeros((8, lanes), F32)

    def clear(at, _):
        for table in sums:
            table[pl.ds(pl.multiple_of(at * 64, 64), 64), :] = jnp.zeros((64, lanes), F32)
        return 0

    lax.fori_loop(0, table_rows // 64, clear, 0)

    def block_step(block, _):
        most = counts_ref[block * groups]
        for group in range(1, groups):
            most = jnp.maximum(most, counts_ref[block * groups + group])

        def step(outer, _):
            for inner in range(4):
                got = []
                for group in range(groups):
                    at = (block * groups + group) * 2 * height + outer * 4 + inner
                    here = pl.ds(at_ref[at], 1)
                    part = pl.ds(part_at_ref[at], 1)
                    got.append((here, sums[group][here, :] + parts_ref[part, :]))
                for group, (here, row) in enumerate(got):
                    sums[group][here, :] = row
            return 0

        lax.fori_loop(0, (most + 3) // 4, step, 0)
        return 0

    lax.fori_loop(0, sources // groups, block_step, 0)
    copies = []
    squares = jnp.zeros((8, lanes), F32)
    for group in range(groups):

        def square(at, total):
            here = pl.ds(pl.multiple_of(at * 64, 64), 64)
            rows = sums[group][here, :]
            low_ref[group, here, :] = rows.astype(LOW)
            return total + jnp.sum((rows * rows).reshape(8, 8, lanes), axis=0)

        squares = lax.fori_loop(0, table_rows // 64, square, squares)
        copies.append(
            pltpu.make_async_copy(
                low_ref.at[group],
                out_ref.at[pl.ds(group * table_rows, table_rows)],
                sems.at[group],
            )
        )
        copies[-1].start()
    square_ref[...] = squares
    for copy in copies:
        copy.wait()


def gelu_parts(value):
    scale = math.sqrt(2.0 / math.pi)
    square = value * value
    bend = jnp.tanh(scale * value * (1.0 + 0.044715 * square))
    half = 0.5 * (1.0 + bend)
    slope = half + 0.5 * value * (1.0 - bend * bend) * (scale * (1.0 + 3 * 0.044715 * square))
    return value * half, slope


def dot(a, b, axes=((1,), (0,)), precision=None):
    return lax.dot_general(
        a, b, (axes, ((), ())), preferred_element_type=F32, precision=precision
    )


NT = ((1,), (1,))
TN = ((0,), (0,))
MESH = pl.DeviceIdType.MESH


def meet(peers, partner=None):
    me = lax.axis_index("mp")
    barrier = pltpu.get_barrier_semaphore()
    if partner is not None:
        pl.semaphore_signal(
            barrier, inc=1, device_id={"dp": partner, "mp": me}, device_id_type=MESH
        )
    for step in range(1, peers):
        pl.semaphore_signal(
            barrier, inc=1, device_id={"mp": lax.rem(me + step, peers)}, device_id_type=MESH
        )
    pl.semaphore_wait(barrier, peers - 1 + (partner is not None))
    return me


def greet_all(devices, peers, me, between=None):
    barrier = pltpu.get_barrier_semaphore()

    def greet(step, _):
        target = lax.rem(me + step, devices)
        pl.semaphore_signal(
            barrier, inc=1, device_id=place_of(target, peers), device_id_type=MESH
        )
        return 0

    lax.fori_loop(1, devices, greet, 0)
    if between is not None:
        between()
    pl.semaphore_wait(barrier, devices - 1)


def place_of(device, peers):
    return {"dp": lax.div(device, peers), "mp": lax.rem(device, peers)}


def ask_kernel(
    row_bits,
    ids_ref,
    first_ref,
    second_ref,
    out_ref,
    full_ref,
    place_ref,
    slot_ref,
    from_ref,
    codes_ref,
    shard_ref,
    c_out,
    c_in,
    w_out,
    w_in,
):
    devices = codes_ref.shape[0]
    here, _, full = full_ref.shape
    width = shard_ref.shape[2]
    peers = full // width
    mp = lax.axis_index("mp")
    me = lax.axis_index("dp") * peers + mp
    columns = pl.ds(pl.multiple_of(mp * width, width), width)
    in_rows = first_ref.shape[0]

    def prepare():
        route(row_bits, ids_ref, codes_ref, place_ref, slot_ref, from_ref)
        for e in range(peers * here):
            shard_ref[e, :in_rows, :] = first_ref[:, e, :].astype(LOW)
            shard_ref[e, in_rows:, :] = second_ref[:, e, :].astype(LOW)
        full_ref[:, :, columns] = shard_ref[pl.ds(mp * here, here)]
        out_ref[me] = codes_ref[me]

    greet_all(devices, peers, me, prepare)

    def c_copy(step):
        target = lax.rem(me + step, devices)
        return pltpu.make_async_remote_copy(
            codes_ref.at[target],
            out_ref.at[me],
            c_out.at[step],
            c_in.at[step],
            device_id=place_of(target, peers),
            device_id_type=MESH,
        )

    def w_copy(step):
        target = lax.rem(mp + step, peers)
        return pltpu.make_async_remote_copy(
            shard_ref.at[pl.ds(target * here, here)],
            full_ref.at[:, :, columns],
            w_out.at[step],
            w_in.at[step],
            device_id={"mp": target},
            device_id_type=MESH,
        )

    def start(step, _):
        c_copy(step).start()
        return 0

    def finish(step, _):
        c_copy(step).wait()
        return 0

    lax.fori_loop(1, devices, start, 0)
    for step in range(1, peers):
        w_copy(step).start()
    lax.fori_loop(1, devices, finish, 0)
    for step in range(1, peers):
        w_copy(step).wait()


def dense_kernel(
    lines,
    *refs,
):
    mine, theirs = refs[:lines], refs[lines : 2 * lines]
    dense_part(mine, theirs, *refs[2 * lines :])


def dense_part(
    mine_refs,
    theirs_refs,
    count_ref,
    x_ref,
    b1_ref,
    b2_ref,
    wg_ref,
    bg_ref,
    w3_ref,
    tb1_ref,
    heads_ref,
    tb2_ref,
    labels_ref,
    mask_ref,
    stats_ref,
    dx_ref,
    parts_ref,
    g_b1_ref,
    share_ref,
    w_ref,
    blocks_ref,
    hid_ref,
    slope_ref,
    dy_ref,
    y_send,
    y_ref,
    gates_ref,
    mixb_ref,
    dz_ref,
    dmix_ref,
    dg_ref,
    dy_send,
    small_ref,
    pack_ref,
    act_ref,
    gate_ref,
    dpre_ref,
    dx_send,
    dx_near,
    dx_help,
    dx_sum,
    dx_far,
    core_recv,
    pair_send,
    pair_recv,
    x_out,
    x_in,
    y_out,
    y_in,
    d_out,
    d_in,
    g_out,
    g_in,
    s_out,
    s_in,
    w_in_sem,
):
    peers, samples, width = blocks_ref.shape
    here = hid_ref.shape[0]
    own, out_width = y_ref.shape[2], y_ref.shape[3]
    experts = peers * here
    tasks, tower_hid = heads_ref.shape
    shards, hid = w_ref.shape[0], w_ref.shape[3]
    in_rows = peers * width // shards
    rows_both = w_ref.shape[2]
    out_rows = rows_both - in_rows
    features = peers * width
    dp = lax.axis_index("dp")
    dp_side = lax.rem(dp, 2)
    pair = dp + 1 - 2 * dp_side
    lines = len(mine_refs)
    w_copies = []
    for at in range(lines):
        first = lax.rem(lax.div(dp, 2) + lines - at, lines) * 2
        w_copies += [
            pltpu.make_async_copy(
                mine_refs[at], w_ref.at[first + dp_side], w_in_sem.at[0, at]
            ),
            pltpu.make_async_copy(
                theirs_refs[at], w_ref.at[first + 1 - dp_side], w_in_sem.at[1, at]
            ),
        ]
    for copy in w_copies:
        copy.start()
    me = meet(peers, pair)
    side = lax.rem(me, 2)
    chip = lax.div(me, 2)
    near = me + 1 - 2 * side
    far = lax.rem(me + 2, peers)
    across = lax.rem(near + 2, peers)

    def rows_of(chunk):
        return pl.ds(pl.multiple_of(chunk * own, own), own)

    half = own // 2

    def part_rows(device, part):
        at = device * own + part * half
        return pl.ds(pl.multiple_of(at, half), half)

    def half_rows(part):
        return pl.ds(pl.multiple_of(part * half, half), half)

    def ahead_rows(pair_of, turn):
        first = lax.rem(2 * pair_of + 2 + 2 * lax.div(turn, 2), peers)
        part = lax.rem(turn, 2)
        return first, part, [part_rows(first + at, part) for at in range(2)]

    def back_chunk(turn):
        return lax.rem(2 * chip + turn, peers)

    def remote(source, target, out_sem, in_sem, device):
        return pltpu.make_async_remote_copy(
            source, target, out_sem, in_sem, device_id={"dp": dp, "mp": device}, device_id_type=MESH
        )

    def x_far(turn):
        rows = ahead_rows(1 - chip, turn)[2]
        return [
            remote(
                x_ref.at[rows[at]],
                blocks_ref.at[me, rows[at]],
                x_out.at[0, turn, at],
                x_in.at[0, turn, at],
                far,
            )
            for at in range(2)
        ]

    def x_near(turn):
        rows = ahead_rows(chip, turn)[2]
        return [
            remote(
                x_ref.at[rows[at]],
                blocks_ref.at[me, rows[at]],
                x_out.at[1, turn, at],
                x_in.at[1, turn, at],
                near,
            )
            for at in range(2)
        ]

    def x_hand(turn):
        rows = ahead_rows(chip, turn)[2]
        blocks = [blocks_ref.at[far, rows[at]] for at in range(2)]
        return [
            remote(blocks[at], blocks[at], x_out.at[2, turn, at], x_in.at[2, turn, at], near)
            for at in range(2)
        ]

    def y_copy(turn, at, part, relation, device):
        return remote(
            y_send.at[turn, at],
            y_ref.at[me, :, half_rows(part), :],
            y_out.at[relation, part],
            y_in.at[relation, part],
            device,
        )

    def d_copy(part, relation, device):
        return remote(
            dy_send.at[pl.ds(device * here, here), half_rows(part), :],
            dy_ref.at[:, part_rows(me, part), :],
            d_out.at[relation, part],
            d_in.at[relation, part],
            device,
        )

    def g_near(turn):
        rows = rows_of(back_chunk(turn))
        return remote(
            dx_send.at[near, rows], dx_near.at[rows], g_out.at[0, turn], g_in.at[0, turn], near
        )

    def g_help(turn):
        rows = rows_of(back_chunk(turn))
        return remote(
            dx_send.at[across, rows], dx_help.at[rows], g_out.at[1, turn], g_in.at[1, turn], near
        )

    def g_far(turn):
        rows = rows_of(back_chunk(turn))
        return remote(
            dx_sum.at[rows], dx_far.at[rows], g_out.at[2, turn], g_in.at[2, turn], far
        )

    for turn in range(peers):
        for copy in x_far(turn) + x_near(turn):
            copy.start()
    blocks_ref[me] = x_ref[...]
    limit = count_ref[0]
    for copy in w_copies:
        copy.wait()

    def pass_on(turn):
        for copy in x_far(turn):
            copy.wait_recv()
        for copy in x_hand(turn):
            copy.start()

    pass_on(0)

    def expert_step(turn, _):
        for copy in x_near(turn) + x_hand(turn):
            copy.wait_recv()

        @pl.when(turn < peers - 1)
        def _():
            pass_on(turn + 1)

        first, part, rows = ahead_rows(chip, turn)
        x = jnp.concatenate(
            [
                jnp.concatenate([blocks_ref[block, rows[at]] for block in range(peers)], axis=1)
                for at in range(2)
            ],
            axis=0,
        )
        for e in range(here):
            w_in = w_ref[:, e, :in_rows, :].reshape(peers * width, hid)
            act_ref[...] = dot(x, w_in) + b1_ref[e]

            def gelu_step(tile, _):
                at = pl.multiple_of(tile * 32, 32)
                value, slope = gelu_parts(act_ref[pl.ds(at, 32), :])
                place = lax.div(at, half)
                there = (first + place) * own + part * half + at - place * half
                there = pl.ds(pl.multiple_of(there, 32), 32)
                hid_ref[e, there, :] = value.astype(LOW)
                slope_ref[e, there, :] = slope
                return 0

            lax.fori_loop(0, own // 32, gelu_step, 0)
            w_out = w_ref[:, e, in_rows:, :].reshape(out_width, hid)
            hidden = jnp.concatenate([hid_ref[e, rows[at], :] for at in range(2)], axis=0)
            y = (dot(hidden, w_out, NT) + b2_ref[e]).astype(LOW)
            for at in range(2):
                y_send[turn, at, e] = y[at * half : (at + 1) * half]
        for at in range(2):
            device = first + at

            @pl.when(turn < 2)
            def _():
                y_copy(turn, at, part, 1 + lax.rem(side + at, 2), device).start()

            @pl.when(jnp.logical_and(turn >= 2, device != me))
            def _():
                y_copy(turn, at, part, 0, device).start()

            @pl.when(device == me)
            def _():
                y_ref[me, :, half_rows(part), :] = y_send[turn, at]

        return 0

    lax.fori_loop(0, peers, expert_step, 0)

    own_rows = rows_of(me)
    x_own = jnp.concatenate([blocks_ref[block, own_rows] for block in range(peers)], axis=1)
    logits = dot(x_own, wg_ref[...], NT) + bg_ref[...]
    for k in range(tasks):
        part = logits[:, k * experts : (k + 1) * experts]
        part = jnp.exp(part - jnp.max(part, axis=1, keepdims=True))
        gates_ref[:, k * experts : (k + 1) * experts] = part / jnp.sum(part, axis=1, keepdims=True)

    stats_ref[...] = jnp.zeros_like(stats_ref)

    def square_step(tile, total):
        at = pl.multiple_of(tile * 64, 64)
        valid = (lax.broadcasted_iota(I32, (64, 1), 0) + at) < limit
        part = jnp.where(valid, x_ref[pl.ds(at, 64), :].astype(F32), 0.0)
        return total + jnp.sum((part * part).reshape(8, 8, width), axis=0)

    x_square = lax.fori_loop(0, samples // 64, square_step, jnp.zeros((8, width), F32))
    stats_ref[experts + tasks, :, :width] = x_square
    tile_rows = 16

    def tile_of(tile):
        at = pl.multiple_of(tile * tile_rows, tile_rows)
        return at, pl.ds(at, tile_rows)

    def mix_step(tile, _):
        at, rows = tile_of(tile)
        valid = (lax.broadcasted_iota(I32, (tile_rows, 1), 0) + (at + me * own)) < limit
        gates = gates_ref[rows, :]
        mixed = [None] * tasks
        for e in range(experts):
            y = y_ref[e // here, e % here, rows, :].astype(F32)
            square = jnp.where(valid, y * y, 0.0)
            stats_ref[e] += square[:8] + square[8:]
            for k in range(tasks):
                term = gates[:, k * experts + e : k * experts + e + 1] * y
                mixed[k] = term if e == 0 else mixed[k] + term
        for k in range(tasks):
            square = jnp.where(valid, mixed[k] * mixed[k], 0.0)
            stats_ref[experts + k] += square[:8] + square[8:]
            mixb_ref[k, rows, :] = mixed[k].astype(LOW)
        return 0

    pack_ref[...] = jnp.zeros_like(pack_ref)
    blocks_x = peers * width // 128
    heads_at = blocks_x * tasks * experts
    tower_at = heads_at + tasks * tower_hid // 128
    outer_at = tower_at + tasks * tower_hid // 128
    rest_at = outer_at + experts * out_width // 128
    def tower_step(k, part):
        rows = half_rows(part)
        cols = slice(k * tower_hid, (k + 1) * tower_hid)
        z, slope = gelu_parts(dot(mixb_ref[k, rows, :], w3_ref[:, cols]) + tb1_ref[k : k + 1, :])
        head = heads_ref[k : k + 1, :]
        logit = jnp.sum(z * head, axis=1, keepdims=True) + tb2_ref[0, k]
        small = jnp.exp(-jnp.abs(logit))
        label = labels_ref[rows, k : k + 1].astype(F32)
        row_id = lax.broadcasted_iota(I32, (half, 1), 0) + (me * own + part * half)
        weight = jnp.where(row_id < limit, mask_ref[rows, k : k + 1].astype(F32), 0.0)
        soft = jnp.maximum(logit, 0.0) + jnp.log1p(small)
        loss = jnp.sum(weight * (soft - label * logit), axis=0, keepdims=True)
        stats_ref[experts + tasks + 1, :1, :1] += loss
        stats_ref[experts + tasks + 1, :1, 1:2] += jnp.sum(weight, axis=0, keepdims=True)
        chance = jnp.where(logit >= 0.0, 1.0, small) / (1.0 + small)
        dl = weight * (chance - label)
        g_head = jnp.sum(dl * z, axis=0, keepdims=True)
        dz = (dl * head * slope).astype(LOW)
        g_bias = jnp.sum(dz.astype(F32), axis=0, keepdims=True)
        for piece in range(tower_hid // 128):
            lane = slice(piece * 128, (piece + 1) * 128)
            at = k * (tower_hid // 128) + piece
            pack_ref[heads_at + at : heads_at + at + 1, :] += g_head[:, lane]
            pack_ref[tower_at + at : tower_at + at + 1, :] += g_bias[:, lane]
        pack_ref[rest_at + 1 : rest_at + 2, k : k + 1] += jnp.sum(dl, axis=0, keepdims=True)
        dz_ref[k, rows, :] = dz
        dmix_ref[k, rows, :] = dot(dz, w3_ref[:, cols], NT)

    def dy_step(tile, _):
        at, rows = tile_of(tile)
        gates = gates_ref[rows, :]
        dmix = [dmix_ref[k, rows, :] for k in range(tasks)]
        for e in range(experts):
            total = None
            for k in range(tasks):
                term = gates[:, k * experts + e : k * experts + e + 1] * dmix[k]
                total = term if k == 0 else total + term
            dy_send[e, rows, :] = total.astype(LOW)
        return 0

    def half_step(part, _):
        for relation, device in enumerate((near, far, across)):
            y_copy(0, 0, part, relation, device).wait_recv()
        tiles = half // tile_rows
        lax.fori_loop(part * tiles, (part + 1) * tiles, mix_step, 0)
        for k in range(tasks):
            tower_step(k, part)
        lax.fori_loop(part * tiles, (part + 1) * tiles, dy_step, 0)
        d_copy(part, 1, far).start()
        d_copy(part, 2, across).start()
        d_copy(part, 0, near).start()
        return 0

    lax.fori_loop(0, 2, half_step, 0)
    dy_ref[:, own_rows, :] = dy_send[pl.ds(me * here, here)]
    for k in range(tasks):
        cols = slice(k * tower_hid, (k + 1) * tower_hid)
        small_ref[:, cols] = dot(mixb_ref[k], dz_ref[k], TN).astype(LOW)
    ones = jnp.ones((8, own), LOW)
    for e in range(experts):
        g_outer = dot(ones, dy_send[e])
        for part in range(out_width // 128):
            at = outer_at + e * (out_width // 128) + part
            pack_ref[at : at + 1, :] = g_outer[:1, part * 128 : (part + 1) * 128]

    lane = lax.broadcasted_iota(I32, (tile_rows, tasks * experts), 1)

    def dg_step(tile, _):
        at, rows = tile_of(tile)
        dmix = [dmix_ref[k, rows, :] for k in range(tasks)]
        found = jnp.zeros((tile_rows, tasks * experts), F32)
        for e in range(experts):
            y = y_ref[e // here, e % here, rows, :].astype(F32)
            for k in range(tasks):
                value = jnp.sum(dmix[k] * y, axis=1, keepdims=True)
                found = jnp.where(lane == k * experts + e, value, found)
        dg_ref[rows, :] = found
        return 0

    lax.fori_loop(0, own // tile_rows, dg_step, 0)
    gates = gates_ref[...]
    dg = dg_ref[...]
    flat = (tasks * experts, tasks * experts)
    same = lax.broadcasted_iota(I32, flat, 0) // experts == lax.broadcasted_iota(I32, flat, 1) // experts
    mean = dot(gates * dg, same.astype(F32), precision=HIGH)
    dgl = (gates * (dg - mean)).astype(LOW)
    pack_ref[rest_at : rest_at + 1, : tasks * experts] = jnp.sum(
        dgl.astype(F32), axis=0, keepdims=True
    )
    g_gating = dot(dgl, x_own, TN)
    for part in range(blocks_x):
        at = part * tasks * experts
        pack_ref[at : at + tasks * experts, :] = g_gating[:, part * 128 : (part + 1) * 128]
    small_ref[:, tasks * tower_hid :] = pack_ref[...].astype(LOW)


    share = share_ref.shape[0]

    def share_rows(part):
        return pl.ds(pl.multiple_of(part * share, share), share)

    def core_copy():
        return pltpu.make_async_remote_copy(
            small_ref.at[pl.ds(pl.multiple_of((1 - side) * 2 * share, share), 2 * share)],
            core_recv,
            s_out.at[0],
            s_in.at[0],
            device_id={"dp": dp, "mp": near},
            device_id_type=MESH,
        )

    def pair_copy():
        return pltpu.make_async_remote_copy(
            pair_send,
            pair_recv,
            s_out.at[1],
            s_in.at[1],
            device_id={"dp": pair, "mp": me},
            device_id_type=MESH,
        )

    def core_sum(part):
        mine = small_ref[share_rows(side * 2 + part), :].astype(F32)
        return mine + core_recv[share_rows(part), :].astype(F32)

    core_copy().start()
    g_b1_ref[...] = jnp.zeros_like(g_b1_ref)

    gate_ref[...] = dot(dgl, wg_ref[...])

    def hand_on(turn):
        rows = rows_of(back_chunk(turn))
        g_help(turn).wait_recv()
        total = dx_send[far, rows].astype(F32) + dx_help[rows].astype(F32)
        dx_sum[rows] = total.astype(LOW)
        g_far(turn).start()

    act = jnp.ones((8, own), LOW)

    def chunk_step(turn, _):
        chunk = back_chunk(turn)
        rows = rows_of(chunk)

        @pl.when(jnp.logical_and(turn < 2, chunk != me))
        def _():
            for part in range(2):
                d_copy(part, 0, chunk).wait_recv()

        @pl.when(turn >= 2)
        def _():
            for part in range(2):
                d_copy(part, 1 + lax.rem(side + turn, 2), chunk).wait_recv()

        total = gate_ref[...] * jnp.where(chunk == me, 1.0, 0.0)
        for e in range(here):
            w_out = w_ref[:, e, in_rows:, :].reshape(out_width, hid)
            dpre = (dot(dy_ref[e, rows, :], w_out) * slope_ref[e, rows, :]).astype(LOW)
            dpre_ref[e, rows, :] = dpre
            g_b1_ref[e] += dot(act, dpre)
            w_in = w_ref[:, e, :in_rows, :].reshape(features, hid)
            total += dot(dpre, w_in, NT)
        for target in range(peers):
            dx_send[target, rows] = total[:, target * width : (target + 1) * width].astype(LOW)
        g_near(turn).start()
        g_help(turn).start()

        @pl.when(turn > 0)
        def _():
            hand_on(turn - 1)

        return 0

    lax.fori_loop(0, peers, chunk_step, 0)
    hand_on(peers - 1)
    core_copy().wait()
    pair_send[...] = core_sum(1 - dp_side).astype(LOW)
    pair_copy().start()

    lanes = parts_ref.shape[4]
    blocks_in = width // 128
    per_in = 128 // in_rows
    per_out = 128 // out_rows
    for e in range(here):

        def in_step(block, _):
            cols = pl.ds(pl.multiple_of(lax.rem(block, blocks_in) * 128, 128), 128)
            x = blocks_ref[lax.div(block, blocks_in), :, cols]
            value = dot(x, dpre_ref[e], TN).astype(LOW)
            for shard in range(per_in):
                for target in range(peers):
                    to = block * per_in + shard
                    away = lax.rem(to + dp, 2)
                    parts_ref[
                        away, lax.div(to, 2), target, e * rows_both : e * rows_both + in_rows, :
                    ] = value[
                        shard * in_rows : (shard + 1) * in_rows, target * lanes : (target + 1) * lanes
                    ]
            return 0

        lax.fori_loop(0, features // 128, in_step, 0)

        def out_step(block, _):
            cols = pl.ds(pl.multiple_of(block * 128, 128), 128)
            value = dot(dy_ref[e, :, cols], hid_ref[e], TN).astype(LOW)
            for shard in range(per_out):
                for target in range(peers):
                    to = block * per_out + shard
                    away = lax.rem(to + dp, 2)
                    parts_ref[
                        away,
                        lax.div(to, 2),
                        target,
                        e * rows_both + in_rows : (e + 1) * rows_both,
                        :,
                    ] = value[
                        shard * out_rows : (shard + 1) * out_rows,
                        target * lanes : (target + 1) * lanes,
                    ]
            return 0

        lax.fori_loop(0, out_width // 128, out_step, 0)

    pair_copy().wait()
    share_ref[...] = (core_sum(dp_side) + pair_recv[...].astype(F32)).astype(LOW)
    for turn in range(peers):
        g_near(turn).wait()
        g_far(turn).wait()
    dx_ref[...] = dx_send[me].astype(F32) + dx_near[...].astype(F32) + dx_far[...].astype(F32)
    for turn in range(peers):
        g_help(turn).wait_send()
        for copy in x_far(turn) + x_near(turn) + x_hand(turn):
            copy.wait_send()
    for relation, device in enumerate((near, far, across)):
        for part in range(2):
            y_copy(0, 0, part, relation, device).wait_send()
            d_copy(part, relation, device).wait_send()


def total_kernel(
    features,
    width_out,
    valid_ref,
    inner_ref,
    stats_ref,
    tables_ref,
    shares_ref,
    grads_ref,
    inner_out,
    result_ref,
    pay_ref,
    got_ref,
    t_out,
    t_in,
):
    devices = got_ref.shape[0]
    peers = inner_out.shape[0]
    here, _, hid = inner_ref.shape
    inner_rows = inner_out.shape[1]
    number = stats_ref.shape[0] - 2
    me = lax.axis_index("dp") * peers + lax.axis_index("mp")
    barrier = pltpu.get_barrier_semaphore()

    def greet(step, _):
        target = lax.rem(me + step, devices)
        pl.semaphore_signal(barrier, inc=1, device_id=place_of(target, peers), device_id_type=MESH)
        return 0

    lax.fori_loop(1, devices, greet, 0)
    lane = lax.broadcasted_iota(I32, (1, 128), 1)

    def whole_sum(value):
        return jnp.sum(jnp.sum(value, axis=0, keepdims=True), axis=1, keepdims=True)

    def grad_step(at, total):
        rows = grads_ref[pl.ds(pl.multiple_of(at * 64, 64), 64), :]
        return total + jnp.sum((rows * rows).reshape(8, 8, 128), axis=0)

    squares = lax.fori_loop(0, grads_ref.shape[0] // 64, grad_step, tables_ref[...])
    share = shares_ref[...]
    vector = jnp.where(lane == 0, stats_ref[number + 1, :1, :1], 0.0)
    vector = jnp.where(lane == 1, stats_ref[number + 1, :1, 1:2], vector)
    for at in range(number + 1):
        vector = jnp.where(lane == at + 2, whole_sum(stats_ref[at]), vector)
    vector = jnp.where(lane == number + 3, whole_sum(squares) + whole_sum(share * share), vector)
    pay_ref[...] = jnp.zeros_like(pay_ref)
    for e in range(here):
        for part in range(hid // 128):
            at = e * (hid // 128) + part
            pay_ref[at : at + 1, :] = inner_ref[e, :1, part * 128 : (part + 1) * 128]
    pay_ref[inner_rows : inner_rows + 1, :] = vector
    got_ref[me] = pay_ref[...]
    pl.semaphore_wait(barrier, devices - 1)

    def t_copy(step):
        target = lax.rem(me + step, devices)
        return pltpu.make_async_remote_copy(
            pay_ref,
            got_ref.at[me],
            t_out.at[step],
            t_in.at[step],
            device_id=place_of(target, peers),
            device_id_type=MESH,
        )

    def start(step, _):
        t_copy(step).start()
        return 0

    def finish(step, _):
        t_copy(step).wait()
        return 0

    lax.fori_loop(1, devices, start, 0)
    lax.fori_loop(1, devices, finish, 0)
    total = jnp.zeros((1, 128), F32)
    inner_sq = jnp.zeros((inner_rows, 128), F32)
    for group in range(peers):
        part = jnp.zeros((inner_rows, 128), F32)
        for block in range(devices // peers):
            source = block * peers + group
            part = part + got_ref[source, :inner_rows, :]
            total = total + got_ref[source, inner_rows : inner_rows + 1, :]
        inner_out[group] = part
        inner_sq = inner_sq + part * part

    def pick(at):
        return jnp.sum(jnp.where(lane == at, total, 0.0), axis=1, keepdims=True)

    weight = pick(1)
    grad_norm = jnp.sqrt(pick(number + 3) + whole_sum(inner_sq)) / weight
    factor = jnp.minimum(1.0, clip_max / grad_norm) / weight
    count = valid_ref[0].astype(F32)
    width = jnp.where(lane == number + 2, float(features), float(width_out))
    result_ref[...] = jnp.zeros_like(result_ref)
    result_ref[0:1, :] = jnp.broadcast_to(factor, (1, 128))
    result_ref[1:2, :] = jnp.broadcast_to(grad_norm, (1, 128))
    result_ref[2:3, :] = total
    result_ref[3:4, :] = jnp.sqrt(total / (count * width) + stat_eps)


def table_kernel(factor_ref, weight_ref, first_ref, second_ref, grad_ref, *outs):
    pair, width, rows = weight_ref.shape
    gradient = grad_ref[0].astype(F32).T.reshape(pair, width, rows) * factor_ref[:1, :1].reshape(1, 1, 1)
    results = adamw(weight_ref[...], first_ref[...], second_ref[...], gradient, rate_table)
    for out, result in zip(outs, results):
        out[...] = result


def small_kernel(
    tasks,
    experts,
    result_ref,
    whole_ref,
    t0_ref,
    t1_ref,
    t2_ref,
    g0_ref,
    g1_ref,
    g2_ref,
    h0_ref,
    h1_ref,
    h2_ref,
    t0_out,
    t1_out,
    t2_out,
    g0_out,
    g1_out,
    g2_out,
    h0_out,
    h1_out,
    h2_out,
    pack_ref,
):
    step = pl.program_id(0)
    peers = lax.axis_size("mp")
    groups = lax.axis_size("dp")
    rows, width = t0_ref.shape
    unit = whole_ref.shape[1]
    factor = result_ref[:1, :1]
    core, side = lax.div(step, 2), lax.rem(step, 2)
    for first in range(groups // 2):
        for second in range(peers // 2):
            source = (2 * first + side) * peers + 2 * second + core
            at = (first * (peers // 2) + second) * unit
            value = whole_ref[source]
            here = slice(at, at + unit)
            results = adamw(
                t0_ref[here, :],
                t1_ref[here, :],
                t2_ref[here, :],
                value[:, :width].astype(F32) * factor,
                rate_dense,
            )
            for out, result in zip((t0_out, t1_out, t2_out), results):
                out[here, :] = result
            pack_ref[pl.ds(step * rows + at, unit), :] = value[:, width:].astype(F32)

    @pl.when(step == pl.num_programs(0) - 1)
    def _():
        gates = tasks * experts
        features = g0_ref.shape[1]
        for part in range(features // 128):
            lane = slice(part * 128, (part + 1) * 128)
            results = adamw(
                g0_ref[:, lane],
                g1_ref[:, lane],
                g2_ref[:, lane],
                pack_ref[part * gates : (part + 1) * gates, :] * factor,
                rate_dense,
            )
            for out, result in zip((g0_out, g1_out, g2_out), results):
                out[:, lane] = result
        heads_at = features // 128 * gates
        parts = h0_ref.shape[1] // 128
        for task in range(tasks):
            for part in range(parts):
                lane = slice(part * 128, (part + 1) * 128)
                at = heads_at + task * parts + part
                row = slice(task, task + 1)
                results = adamw(
                    h0_ref[row, lane],
                    h1_ref[row, lane],
                    h2_ref[row, lane],
                    pack_ref[at : at + 1, :] * factor,
                    rate_dense,
                )
                for out, result in zip((h0_out, h1_out, h2_out), results):
                    out[row, lane] = result


def body(
    row_ids,
    counts,
    labels,
    label_mask,
    embeddings,
    embed_first,
    embed_second,
    expert_in,
    in_first,
    in_second,
    expert_out,
    out_first,
    out_second,
    gating,
    gating_first,
    gating_second,
    towers,
    towers_first,
    towers_second,
    heads,
    heads_first,
    heads_second,
    biases,
    biases_first,
    biases_second,
):
    devices = lax.axis_size(AXES)
    mp_count = lax.axis_size("mp")
    dp_count = lax.axis_size("dp")
    mp_index = lax.axis_index("mp")
    samples, tables_here = row_ids.shape
    tables, rows_dev, d_emb = embeddings.shape
    own = samples // mp_count
    requests = samples * tables_here
    capacity = 2 * requests // devices
    height = capacity // 2
    slots = devices * height
    row_bits = rows_dev.bit_length() - 1
    pairs = tables // 2
    lanes = 2 * d_emb
    group_rows = tables_here // 2 * rows_dev
    in_rows, out_rows = expert_in.shape[0], expert_out.shape[0]
    experts_here = EXPERTS // mp_count
    hid = expert_in.shape[2] * mp_count
    features = tables * d_emb
    width_out = out_rows * dp_count
    tower_hid = towers.shape[1] // TASKS

    in_out_rows = in_rows + out_rows
    hid_here = hid // mp_count
    sides = [
        [d * mp_count + m for d in range(x, dp_count, 2) for m in range(mp_count)] for x in range(2)
    ]
    partners = [(d, d ^ 1) for d in range(dp_count)]

    def exchange_side(parts):
        return lax.all_to_all(
            parts, AXES, split_axis=0, concat_axis=0, axis_index_groups=sides, tiled=True
        )

    def exchange_all(parts):
        return lax.all_to_all(parts, AXES, split_axis=0, concat_axis=0, tiled=True)

    def sems(*shape):
        return pltpu.SemaphoreType.DMA(shape)

    codes, shard, place, slot, source = pl.pallas_call(
        functools.partial(ask_kernel, row_bits),
        out_shape=(
            jax.ShapeDtypeStruct((devices, 1, capacity), I32),
            jax.ShapeDtypeStruct((experts_here, in_out_rows, hid), LOW),
            jax.ShapeDtypeStruct((tables_here, samples), I32),
            jax.ShapeDtypeStruct((tables_here, samples), I32),
            jax.ShapeDtypeStruct((tables_here, samples), I32),
        ),
        in_specs=[VMEM] * 3,
        out_specs=(VMEM,) * 5,
        scratch_shapes=[
            pltpu.VMEM((devices, 1, capacity), I32),
            pltpu.VMEM((EXPERTS, in_out_rows, hid_here), LOW),
            sems(devices),
            sems(devices),
            sems(mp_count),
            sems(mp_count),
        ],
        compiler_params=pltpu.CompilerParams(
            vmem_limit_bytes=32 * MIB, collective_id=2, has_side_effects=True
        ),
        name="ask",
    )(row_ids.T, expert_in, expert_out)
    w_far = []
    for ahead in range(1, dp_count // 2):
        steps = [(d, (d + 2 * ahead) % dp_count) for d in range(dp_count)]
        w_far.append(lax.ppermute(shard, "dp", steps))
    w_near = lax.ppermute(shard, "dp", partners)
    codes = codes.reshape(devices, capacity)
    asked = codes[:, 0] >> 16
    plain = codes & 65535
    found_at = jnp.maximum(plain - 1, 0)
    table_at = found_at >> row_bits
    sum_at = (table_at >> 1) * rows_dev + (found_at & (rows_dev - 1))
    number = jnp.arange(capacity, dtype=I32)[None, :]
    turned_at = ((table_at ^ number) & 1) * group_rows + sum_at
    part_at = ((number & 1) * 2 + (table_at & 1)) * slots + (number >> 1)
    part_at = part_at + jnp.arange(devices, dtype=I32)[:, None] * height
    part_at = jnp.where(plain > 0, part_at, 4 * slots)

    table_view = jnp.transpose(embeddings, (0, 2, 1))
    def find(first, many, before):
        return pl.pallas_call(
            functools.partial(find_kernel, mp_count, first),
            grid=(many,),
            out_shape=jax.ShapeDtypeStruct((dp_count, mp_count, height, lanes), LOW),
            in_specs=[
                SMEM,
                SMEM,
                pl.BlockSpec((tables_here, d_emb, rows_dev), lambda m: (m + first, 0, 0)),
            ]
            + [pl.BlockSpec(memory_space=pl.ANY)] * len(before),
            out_specs=pl.BlockSpec((dp_count, 1, height, lanes), lambda m: (0, m + first, 0, 0)),
            scratch_shapes=[
                pltpu.VMEM((tables_here * rows_dev, lanes), F32),
                pltpu.VMEM((height, lanes), F32),
            ],
            input_output_aliases={3: 0} if before else {},
            compiler_params=params(60),
            name="find",
        )(turned_at.reshape(-1), asked, table_view, *before)

    found = find(0, mp_count // 2, [])
    line, found = lax.optimization_barrier((w_far[0], found))
    w_theirs = [w_near, lax.ppermute(line, "dp", partners)]
    found = find(mp_count // 2, mp_count - mp_count // 2, [found])
    rest, w_theirs, found = lax.optimization_barrier((w_far[1:], w_theirs, found))
    w_mine = [shard, line] + rest
    w_theirs = w_theirs + [lax.ppermute(line, "dp", partners) for line in rest]
    returned = exchange_all(found.reshape(devices, height, lanes))
    embedded = pl.pallas_call(
        place_kernel,
        out_shape=jax.ShapeDtypeStruct((samples, tables_here * d_emb), LOW),
        in_specs=[SMEM, VMEM],
        out_specs=VMEM,
        scratch_shapes=[
            pltpu.VMEM((2 * slots, lanes), F32),
            pltpu.VMEM((tables_here // 2, samples, lanes), F32),
        ],
        compiler_params=params(32),
        name="place",
    )(place.reshape(-1), returned.reshape(slots, lanes))

    first = EXPERTS * hid
    second = first + EXPERTS * width_out
    third = second + TASKS * EXPERTS
    fourth = third + TASKS * tower_hid
    inner_here = lax.dynamic_index_in_dim(
        biases[:first].reshape(mp_count, experts_here, 1, hid), mp_index, 0, keepdims=False
    )
    outer_here = lax.dynamic_index_in_dim(
        biases[first:second].reshape(mp_count, experts_here, 1, width_out),
        mp_index,
        0,
        keepdims=False,
    )
    gating_low = gating.T.astype(LOW)
    all_gates = TASKS * EXPERTS
    pack_rows = width_out

    def scratch(shape, kind=F32):
        return pltpu.VMEM(shape, kind)

    pack_shape = (pack_rows // 4, TASKS * tower_hid + 128)
    x_shape = (samples, tables_here * d_emb)
    stat_parts, embed_grad, grad_parts, inner_parts, share = pl.pallas_call(
        functools.partial(dense_kernel, dp_count // 2),
        out_shape=(
            jax.ShapeDtypeStruct((EXPERTS + TASKS + 2, 8, width_out), F32),
            jax.ShapeDtypeStruct(x_shape, F32),
            jax.ShapeDtypeStruct(
                (2, dp_count // 2, mp_count, experts_here * in_out_rows, hid_here), LOW
            ),
            jax.ShapeDtypeStruct((experts_here, 8, hid), F32),
            jax.ShapeDtypeStruct(pack_shape, LOW),
        ),
        in_specs=[pl.BlockSpec(memory_space=pl.ANY)] * dp_count
        + [SMEM]
        + [VMEM] * 8
        + [SMEM]
        + [VMEM] * 2,
        out_specs=(VMEM,) * 5,
        scratch_shapes=[
            scratch((dp_count, experts_here, in_out_rows, hid), LOW),
            scratch((mp_count,) + x_shape, LOW),
            scratch((experts_here, samples, hid), LOW),
            scratch((experts_here, samples, hid)),
            scratch((experts_here, samples, width_out), LOW),
            scratch((mp_count, 2, experts_here, own // 2, width_out), LOW),
            scratch((mp_count, experts_here, own, width_out), LOW),
            scratch((own, all_gates)),
            scratch((TASKS, own, width_out), LOW),
            scratch((TASKS, own, tower_hid), LOW),
            scratch((TASKS, own, width_out)),
            scratch((own, all_gates)),
            scratch((EXPERTS, own, width_out), LOW),
            scratch((pack_rows, TASKS * tower_hid + 128), LOW),
            scratch((pack_rows, 128)),
            scratch((own, hid)),
            scratch((own, features)),
            scratch((experts_here, samples, hid), LOW),
            scratch((mp_count,) + x_shape, LOW),
            scratch(x_shape, LOW),
            scratch(x_shape, LOW),
            scratch(x_shape, LOW),
            scratch(x_shape, LOW),
            scratch((2 * pack_shape[0], pack_shape[1]), LOW),
            scratch(pack_shape, LOW),
            scratch(pack_shape, LOW),
            sems(3, mp_count, 2),
            sems(3, mp_count, 2),
            sems(3, 2),
            sems(3, 2),
            sems(3, 2),
            sems(3, 2),
            sems(3, mp_count),
            sems(3, mp_count),
            sems(2),
            sems(2),
            sems(2, dp_count // 2),
        ],
        compiler_params=pltpu.CompilerParams(
            vmem_limit_bytes=60 * MIB, collective_id=0, has_side_effects=True
        ),
        name="dense",
    )(
        *w_mine,
        *w_theirs,
        lax.dynamic_slice_in_dim(counts, lax.axis_index("dp"), 1, 0),
        embedded,
        inner_here,
        outer_here,
        gating_low,
        biases[second:third].reshape(1, all_gates),
        towers.astype(LOW),
        biases[third:fourth].reshape(TASKS, tower_hid),
        heads,
        biases[fourth:].reshape(1, TASKS),
        labels,
        label_mask,
    )

    back_rows = pl.pallas_call(
        send_kernel,
        out_shape=jax.ShapeDtypeStruct((slots, lanes), LOW),
        in_specs=[SMEM, SMEM, VMEM],
        out_specs=VMEM,
        scratch_shapes=[
            pltpu.VMEM((tables_here // 2, 2 * samples, lanes), F32),
            pltpu.VMEM((2 * slots, lanes), F32),
        ],
        compiler_params=params(32),
        name="send",
    )(slot.reshape(-1), source.reshape(-1), embed_grad)
    share = share.reshape(devices // 4, pack_rows // devices, -1)
    arrived, shares = pl.pallas_call(
        swap_kernel,
        out_shape=(
            jax.ShapeDtypeStruct((devices, height, lanes), LOW),
            jax.ShapeDtypeStruct(share.shape, LOW),
        ),
        in_specs=[VMEM, VMEM],
        out_specs=(VMEM, VMEM),
        scratch_shapes=[sems(devices), sems(devices), sems(devices // 4), sems(devices // 4)],
        compiler_params=pltpu.CompilerParams(
            vmem_limit_bytes=16 * MIB, collective_id=3, has_side_effects=True
        ),
        name="swap",
    )(back_rows.reshape(devices, height, lanes), share)
    share = jnp.sum(shares.astype(F32), axis=0)
    partner = lax.ppermute(grad_parts[1], "dp", partners)
    partner, arrived = lax.optimization_barrier((partner, arrived))
    grad_parts = (grad_parts[0].astype(F32) + partner.astype(F32)).astype(LOW)
    grad_parts = exchange_side(
        grad_parts.reshape(devices // 2, experts_here * in_out_rows, hid_here)
    )
    grad_sum = jnp.sum(
        grad_parts.reshape(dp_count // 2, mp_count, experts_here, in_out_rows, -1).astype(F32), 0
    )
    owned = grad_sum.reshape(EXPERTS, in_out_rows, -1).transpose(1, 0, 2)
    in_sum, out_sum = owned[:in_rows], owned[in_rows:]

    table_grad, table_sq = pl.pallas_call(
        functools.partial(add_kernel, mp_count),
        out_shape=(
            jax.ShapeDtypeStruct((pairs * rows_dev, lanes), LOW),
            jax.ShapeDtypeStruct((8, lanes), F32),
        ),
        in_specs=[SMEM, SMEM, SMEM, VMEM],
        out_specs=(pl.BlockSpec(memory_space=pl.ANY), VMEM),
        scratch_shapes=[
            pltpu.VMEM((4 * slots + 8, lanes), F32),
            pltpu.VMEM((mp_count, group_rows, lanes), LOW),
            pltpu.SemaphoreType.DMA((mp_count,)),
        ]
        + [pltpu.VMEM((group_rows, lanes), F32)] * mp_count,
        compiler_params=params(60),
        name="add",
    )(sum_at.reshape(-1), part_at.reshape(-1), asked, arrived.reshape(slots, lanes))

    stat_end = EXPERTS + TASKS
    inner_rows = experts_here * hid // 128
    pay_rows = inner_rows + 8
    inner_sum, result = pl.pallas_call(
        functools.partial(total_kernel, features, width_out),
        out_shape=(
            jax.ShapeDtypeStruct((mp_count, inner_rows, 128), F32),
            jax.ShapeDtypeStruct((8, 128), F32),
        ),
        in_specs=[SMEM] + [VMEM] * 5,
        out_specs=(VMEM,) * 2,
        scratch_shapes=[
            scratch((pay_rows, 128)),
            scratch((devices, pay_rows, 128)),
            sems(devices),
            sems(devices),
        ],
        compiler_params=pltpu.CompilerParams(
            vmem_limit_bytes=16 * MIB, collective_id=4, has_side_effects=True
        ),
        name="total",
    )(
        jnp.sum(counts).reshape(1),
        inner_parts,
        stat_parts,
        table_sq,
        share,
        grad_sum.reshape(-1, 128),
    )
    factor = result[0, 0]
    share_low, result = lax.optimization_barrier((share.astype(LOW), result))
    whole = exchange_all(jnp.broadcast_to(share_low[None], (devices,) + share_low.shape))

    table_spec = pl.BlockSpec((2, d_emb, rows_dev), lambda p: (p, 0, 0))
    embed_out = pl.pallas_call(
        table_kernel,
        grid=(pairs,),
        out_shape=(jax.ShapeDtypeStruct(table_view.shape, F32),) * 3,
        in_specs=[
            pl.BlockSpec((8, 128), lambda p: (0, 0)),
            table_spec,
            table_spec,
            table_spec,
            pl.BlockSpec((1, rows_dev, lanes), lambda p: (p, 0, 0)),
        ],
        out_specs=(table_spec,) * 3,
        compiler_params=params(58),
        name="tables",
    )(
        result,
        table_view,
        jnp.transpose(embed_first, (0, 2, 1)),
        jnp.transpose(embed_second, (0, 2, 1)),
        table_grad.reshape(pairs, rows_dev, lanes),
    )
    embed_out = [jnp.transpose(value, (0, 2, 1)) for value in embed_out]
    in_out = adamw(expert_in, in_first, in_second, in_sum * factor, rate_dense)
    out_out = adamw(expert_out, out_first, out_second, out_sum * factor, rate_dense)
    whole, embed_out = lax.optimization_barrier((whole, embed_out))
    blocks_x = features // 128
    heads_at = blocks_x * all_gates
    tower_at = heads_at + TASKS * tower_hid // 128
    outer_at = tower_at + TASKS * tower_hid // 128
    rest_at = outer_at + EXPERTS * width_out // 128
    tower_spec = pl.BlockSpec((pack_rows // 4, TASKS * tower_hid), lambda c: (c, 0))
    gate_spec = pl.BlockSpec((all_gates, features), lambda c: (0, 0))
    head_spec = pl.BlockSpec((TASKS, tower_hid), lambda c: (0, 0))
    *small_out, packed = pl.pallas_call(
        functools.partial(small_kernel, TASKS, EXPERTS),
        grid=(4,),
        out_shape=(jax.ShapeDtypeStruct(towers.shape, F32),) * 3
        + (jax.ShapeDtypeStruct((all_gates, features), F32),) * 3
        + (jax.ShapeDtypeStruct(heads.shape, F32),) * 3
        + (jax.ShapeDtypeStruct((pack_rows, 128), F32),),
        in_specs=[
            pl.BlockSpec((8, 128), lambda c: (0, 0)),
            pl.BlockSpec(whole.shape, lambda c: (0, 0, 0)),
        ]
        + [tower_spec] * 3
        + [gate_spec] * 3
        + [head_spec] * 3,
        out_specs=(tower_spec,) * 3
        + (gate_spec,) * 3
        + (head_spec,) * 3
        + (pl.BlockSpec((pack_rows, 128), lambda c: (0, 0)),),
        compiler_params=params(48),
        name="small",
    )(
        result,
        whole,
        towers,
        towers_first,
        towers_second,
        gating.T,
        gating_first.T,
        gating_second.T,
        heads,
        heads_first,
        heads_second,
    )
    towers_out, heads_out = small_out[:3], small_out[6:]
    gating_out = [value.T for value in small_out[3:6]]
    bias_sum = jnp.concatenate(
        [
            inner_sum.reshape(-1),
            packed[outer_at:rest_at].reshape(-1),
            packed[rest_at, :all_gates],
            packed[tower_at:outer_at].reshape(-1),
            packed[rest_at + 1, :TASKS],
        ]
    )
    biases_out = adamw(biases, biases_first, biases_second, bias_sum * factor, rate_dense)
    stats = jnp.concatenate([result[3, stat_end + 2][None], result[3, 2 : stat_end + 2]])
    loss = result[2, :2]
    return (
        *embed_out,
        *in_out,
        in_out[0].astype(LOW),
        *out_out,
        out_out[0].astype(LOW),
        *gating_out,
        *towers_out,
        *heads_out,
        *biases_out,
        result[1, :1],
        loss,
        stats,
    )


def solution(mesh):
    rows = P(None, AXES, None)
    expert = P("dp", None, "mp")
    sample = P(AXES, None)
    placed = (P("dp", "mp"), P(), sample, sample) + (rows,) * 3 + (expert,) * 6 + (P(),) * 12
    results = (rows,) * 3 + (expert,) * 8 + (P(),) * 15
    return jax.shard_map(body, mesh=mesh, in_specs=placed, out_specs=results, check_vma=False)
```
